32 devices in a mesh: grp: 2 (over y), lat: 4 (over z), tm: 2 (over x), chan: 2 (over core).
Axes of the slice: x: 2, y: 2, z: 4, core: 2. Of those that a mesh axis runs over, the one named last changes fastest.
Arguments:
- innovations: bfloat16 [4, 4, 73, 32, 128], P(None, ('grp', 'tm'), None, ('lat', 'chan')), parts along dimension 1, may hold values from -6 to 6
- obs_mask: int32 [4, 8, 4], P(('grp', 'tm'), ('lat', 'chan')), parts along dimension 0, may hold values 0 or 1
- slopes: bfloat16 [4, 128, 32, 128], P(('grp', 'tm'), 'chan', 'lat'), parts along dimension 0, may hold values from -0.14941406 to 1.09375
- layer_of: int32 [2], replicated, may hold values from 0 to 7
- weight_in: bfloat16 [8, 3, 3, 73, 128], P(None, None, None, None, 'chan'), may hold values from -0.1875 to 0.1875
- weight_out: bfloat16 [8, 3, 3, 128, 73], P(None, None, None, 'chan'), may hold values from -0.25 to 0.25
Outputs:
- gradients: float32 [4, 4, 73, 32, 128], P(None, ('grp', 'tm'), None, ('lat', 'chan')), parts along dimension 1
The draws below stay inside these ranges and needn't reach their ends.
There are 2 independent parts, one for each index of `grp`. The reference program is written for one: setup_inputs(seed, part) draws one part's arguments, and reference() takes and returns one part's arrays. A program takes and returns all parts, laid end to end along the dimension named above; an argument that names none is the same for every part. Nothing has to cross between parts.
All inputs are finite; a program needn't handle non-finite values. No bound on the sum of `obs_mask` on one device may be relied on, other than what follows from the above.
Results may differ from the reference program's by a relative error of at most 0.011.
Values may be sent and summed in bfloat16 or wider, within the bound.
A program may use at most 64 MiB of HBM per device.

```python
import jax
import jax.numpy as jnp
from jax import lax

C = 73
HID = 128
LAYERS = 8
FRONTS = 4
WIN = 128
SECTIONS = 2
LATS = 32


def set_ends(drawn, stream_key, low, largest):
    longest = drawn.shape.index(max(drawn.shape))
    spots = []
    for shift in (0, 1):
        where = [jax.random.randint(jax.random.fold_in(stream_key, axis), (), 0, length) for axis, length in enumerate(drawn.shape)]
        where[longest] = (where[longest] + shift) % drawn.shape[longest]
        spots.append(tuple(where))
    return drawn.at[spots[0]].set(low).at[spots[1]].set(largest)


def shard_levels(stream_key, shape, shards, smallest, largest):
    factor_of = 1.0
    for dim, parts in shards:
        heights = jax.random.uniform(jax.random.fold_in(jax.random.fold_in(stream_key, 6), dim), (parts,), jnp.float32, smallest / len(shards), largest / len(shards))
        factor_of = factor_of * jnp.repeat(jnp.exp(heights), shape[dim] // parts).reshape((-1,) + (1,) * (len(shape) - 1 - dim))
    return factor_of


def bell_draw(stream_key, extent, spread, bound, shards=(), dtype=jnp.bfloat16):
    factor_of = shard_levels(stream_key, extent, shards, -0.22, 0.18) if shards else 1.0
    values = jax.random.normal(stream_key, extent, jnp.float32) * spread * factor_of
    return jnp.minimum(jnp.maximum(values, -bound), bound).astype(dtype)


def setup_inputs(seed: int = 0, part: int = 0) -> dict:
    key_list = jax.random.split(jax.random.key(seed), 7)
    part_keys = jax.random.split(jax.random.fold_in(key_list[6], part), 7)
    return {
        "innovations": bell_draw(part_keys[0], (FRONTS, SECTIONS, C, LATS, WIN), 1.0, 6.0, ((1, 2), (3, 8))),
        "obs_mask": set_ends((jax.random.randint(part_keys[1], (SECTIONS, LATS // 4, WIN // 32), 0, 2) < 1).astype(jnp.int32), jax.random.fold_in(part_keys[1], 1), 0, 1),
        "slopes": jnp.clip(-0.14941406 + 1.2431641 * jax.random.uniform(part_keys[2], (SECTIONS, HID, LATS, WIN), jnp.float32) ** shard_levels(part_keys[2], (SECTIONS, HID, LATS, WIN), ((0, 2), (1, 2), (2, 4)), -0.2, 0.2), -0.14941406, 1.09375).astype(jnp.bfloat16),
        "layer_of": jax.random.randint(key_list[3], (SECTIONS,), 0, LAYERS).astype(jnp.int32),
        "weight_in": bell_draw(key_list[4], (LAYERS, 3, 3, C, HID), (9 * HID) ** -0.5, 0.1875, ((4, 2),)),
        "weight_out": bell_draw(key_list[5], (LAYERS, 3, 3, HID, C), (9 * C) ** -0.5, 0.25, ((3, 2),)),
    }


def spread_tiles(obs_tiles):
    return jnp.repeat(jnp.repeat(obs_tiles, 4, axis=-2), 32, axis=-1).astype(jnp.float32)


def transposed_conv(field, kernel):
    height = field.shape[2]
    width = field.shape[3]
    padded = jnp.pad(field.astype(jnp.float32), ((0, 0), (0, 0), (1, 1), (1, 1)))
    summed = None
    for row_off in range(3):
        for col_off in range(3):
            shifted = padded[:, :, 2 - row_off:2 - row_off + height, 2 - col_off:2 - col_off + width]
            contrib = jnp.einsum('ij,fjhw->fihw', kernel[row_off, col_off].astype(jnp.float32), shifted, precision=lax.Precision.HIGHEST)
            summed = contrib if summed is None else summed + contrib
    return summed


def reference(innovations, obs_mask, slopes, layer_of, weight_in, weight_out):
    forcing = innovations.astype(jnp.float32) * spread_tiles(obs_mask)[None, :, None]
    adjoint = jnp.zeros((FRONTS, C, LATS, WIN), jnp.float32)
    fresh = [None] * SECTIONS
    for section in reversed(range(SECTIONS)):
        layer_no = layer_of[section]
        rounded = adjoint.astype(jnp.bfloat16)
        hidden_grad = transposed_conv(rounded, weight_out[layer_no])
        scaled = (slopes[section].astype(jnp.float32)[None] * hidden_grad).astype(jnp.bfloat16)
        adjoint = adjoint + transposed_conv(scaled, weight_in[layer_no]) + forcing[:, section]
        fresh[section] = adjoint
    return jnp.stack(fresh, axis=1)
```

```python
import functools

import jax
import jax.numpy as jnp
from jax import lax
from jax.experimental import pallas as pl
from jax.experimental.pallas import tpu as pltpu
from jax.sharding import PartitionSpec as P

MESH = pl.DeviceIdType.MESH
BF16 = jnp.bfloat16
F32 = jnp.float32


def round_up(n, m):
    return -(-n // m) * m


def pair_kernel(dims, layer_ref, mask_ref, inn_hbm, slopes_hbm, w_in_hbm, w_out_hbm, out_ref,
                inn_ref, slopes_ref, w_in_ref, w_out_ref, w_wide, w_tall,
                raw, frc, adj, res, slope_f32, slope_rows, slope_win, w1_ref, w2_ref, w1_other,
                w2_other, vs, hs, ss, load_inn, load_rest,
                x_send, x_recv, r_send, r_recv, h_send, h_recv, w_send, w_recv, s_send, s_recv,
                t_send, t_recv):
    fronts, chans, rows, win, half, band, lats, owners = dims
    pad = frc.shape[2]
    rims = rows + 4
    hid_rows = rows + 2
    far = fronts - 1
    grp = lax.axis_index("grp")
    lat = lax.axis_index("lat")
    tm = lax.axis_index("tm")
    core = lax.axis_index("chan")

    def dev(lat_no, tm_no, core_no):
        return (grp, lat_no, tm_no, core_no)

    partner = dev(lat, tm, 1 - core)
    opposite = dev(lat, 1 - tm, core)
    has_down = lat > 0
    has_up = lat < lats - 1
    first = (lat == 0) & (core == 0)
    final = (lat == lats - 1) & (core == 1)
    not_first = jnp.logical_not(first)
    not_final = jnp.logical_not(final)

    barrier = pltpu.get_barrier_semaphore()

    def greet(device):
        pl.semaphore_signal(barrier, inc=1, device_id=device, device_id_type=MESH)

    greet(opposite)

    @pl.when(has_down)
    def _():
        greet(dev(lat - 1, tm, 0))
        greet(dev(lat - 1, tm, 1))

    @pl.when(has_up)
    def _():
        greet(dev(lat + 1, tm, 0))
        greet(dev(lat + 1, tm, 1))

    greet(partner)
    greeted = 2 + 2 * has_down.astype(jnp.int32) + 2 * has_up.astype(jnp.int32)

    def inn_copy(f):
        return pltpu.make_async_copy(inn_hbm.at[f], inn_ref.at[f], load_inn.at[f])

    loads = [
        pltpu.make_async_copy(slopes_hbm, slopes_ref, load_rest.at[0]),
        pltpu.make_async_copy(w_out_hbm, w_out_ref, load_rest.at[1]),
        pltpu.make_async_copy(w_in_hbm, w_in_ref, load_rest.at[2]),
    ]

    lane = lax.broadcasted_iota(jnp.int32, (1, win), 1)
    tiles = mask_ref.shape[0]
    width = win // tiles
    spread = jnp.zeros((1, win), F32)
    for k in range(tiles):
        spread = jnp.where(lane // width == k, mask_ref[k].astype(F32), spread)

    def load_raw(f):
        raw[...] = inn_ref[f].astype(F32).reshape(chans * rows, win)

    def forcing_row(r):
        return raw[pl.ds(r, chans, stride=rows), :] * spread

    def put_out(f, r, value):
        out_ref[pl.ds(f * (chans * rows) + r, chans, stride=rows), :] = value

    starts = (core * 2, (1 - core) * 2)

    def x_copy(k, f):
        part = adj.at[f, pl.ds(2 + starts[k], 2)]
        return pltpu.make_async_remote_copy(
            src_ref=part, dst_ref=part, send_sem=x_send.at[k, f], recv_sem=x_recv.at[k, f],
            device_id=opposite, device_id_type=MESH)

    def r_copy(k):
        part = res.at[pl.ds(2 * k, 2)]
        return pltpu.make_async_remote_copy(
            src_ref=part, dst_ref=part, send_sem=r_send.at[k], recv_sem=r_recv.at[k],
            device_id=opposite, device_id_type=MESH)

    spans = ((0, 1), (band - 1, 1), (3 - 2 * core, 4), (1 + 4 * core, 2))

    def t_copy(k):
        part = slope_rows.at[pl.ds(*spans[k])]
        return pltpu.make_async_remote_copy(
            src_ref=part, dst_ref=part, send_sem=t_send.at[k], recv_sem=t_recv.at[k],
            device_id=opposite, device_id_type=MESH)

    def halo_down(f):
        return pltpu.make_async_remote_copy(
            src_ref=adj.at[f, pl.ds(2, 2)], dst_ref=adj.at[f, pl.ds(rims - 2, 2)],
            send_sem=h_send.at[0, f], recv_sem=h_recv.at[0, f],
            device_id=dev(lat - (1 - core), tm, 1 - core), device_id_type=MESH)

    def halo_up(f):
        return pltpu.make_async_remote_copy(
            src_ref=adj.at[f, pl.ds(rows, 2)], dst_ref=adj.at[f, pl.ds(0, 2)],
            send_sem=h_send.at[1, f], recv_sem=h_recv.at[1, f],
            device_id=dev(lat + core, tm, 1 - core), device_id_type=MESH)

    def pass_on(k, f):
        @pl.when(not_first & (core == k))
        def _():
            halo_down(f).start()

        @pl.when(not_final & (core == 1 - k))
        def _():
            halo_up(f).start()

    def halos_here(f):
        @pl.when(not_final)
        def _():
            halo_down(f).wait_recv()

        @pl.when(not_first)
        def _():
            halo_up(f).wait_recv()

    def halos_sent(f):
        @pl.when(not_first)
        def _():
            halo_down(f).wait_send()

        @pl.when(not_final)
        def _():
            halo_up(f).wait_send()

    w1_copy = pltpu.make_async_remote_copy(
        src_ref=w1_ref, dst_ref=w1_other, send_sem=w_send.at[0], recv_sem=w_recv.at[0],
        device_id=partner, device_id_type=MESH)
    w2_copy = pltpu.make_async_remote_copy(
        src_ref=w2_ref, dst_ref=w2_other, send_sem=w_send.at[1], recv_sem=w_recv.at[1],
        device_id=partner, device_id_type=MESH)
    own = hid_rows - 1
    mine_from = core * (rows - 1)
    partner_from = (1 - core) * (rows - 1)
    s_copy = pltpu.make_async_remote_copy(
        src_ref=slope_rows.at[pl.ds(partner_from, own)],
        dst_ref=slope_win.at[1, pl.ds(core, own)],
        send_sem=s_send.at[0], recv_sem=s_recv.at[0],
        device_id=partner, device_id_type=MESH)
    s_down = pltpu.make_async_remote_copy(
        src_ref=slope_rows.at[0], dst_ref=slope_win.at[1 - core, hid_rows - 1],
        send_sem=s_send.at[1], recv_sem=s_recv.at[1 + (1 - core)],
        device_id=dev(lat - 1, tm, 1), device_id_type=MESH)
    s_up = pltpu.make_async_remote_copy(
        src_ref=slope_rows.at[band - 1], dst_ref=slope_win.at[core, 0],
        send_sem=s_send.at[2], recv_sem=s_recv.at[1 + core],
        device_id=dev(lat + 1, tm, 0), device_id_type=MESH)

    def slope_edges_start():
        @pl.when(has_down)
        def _():
            s_down.start()

        @pl.when(has_up)
        def _():
            s_up.start()

    def slopes_here():
        s_copy.wait_recv()

        @pl.when(has_down & (core == 0))
        def _():
            s_up_recv(slope_win, slope_rows, s_send, s_recv, 0, partner)

        @pl.when(has_up & (core == 1))
        def _():
            s_up_recv(slope_win, slope_rows, s_send, s_recv, hid_rows - 1, partner)

    def own_slopes():
        slope_win[0, pl.ds(1 - core, own)] = slope_rows[pl.ds(mine_from, own)]

    def all_sent():
        w1_copy.wait_send()
        w2_copy.wait_send()
        s_copy.wait_send()

        @pl.when(has_down)
        def _():
            s_down.wait_send()

        @pl.when(has_up)
        def _():
            s_up.wait_send()

    def clear_rims():
        @pl.when(first)
        def _():
            slope_win[:, 0] = jnp.zeros((2, half, win), BF16)
            for f in range(fronts):
                adj[f, 0:2] = jnp.zeros((2, pad, win), BF16)

        @pl.when(final)
        def _():
            slope_win[:, hid_rows - 1] = jnp.zeros((2, half, win), BF16)
            for f in range(fronts):
                adj[f, rims - 2:rims] = jnp.zeros((2, pad, win), BF16)

    def prepare_weights():
        w_wide[...] = jnp.zeros_like(w_wide)
        w_tall[...] = jnp.zeros_like(w_tall)
        layer = layer_ref[0]
        loads[1].wait()
        for a in range(3):
            for b in range(3):
                w_wide[b, a * half:(a + 1) * half, 0:chans] = w_out_ref[layer, a, b].astype(F32)
        wide = w_wide[0] + pltpu.roll(w_wide[1], pad, 1) + pltpu.roll(w_wide[2], 2 * pad, 1)
        w1_ref[...] = wide.astype(BF16)
        loads[2].wait()
        for a in range(3):
            for b in range(3):
                w_tall[a, b * half:(b + 1) * half, 0:chans] = w_in_ref[layer, a, b].astype(F32)
        for a in range(3):
            w2_ref[a * pad:(a + 1) * pad, :] = w_tall[a].T[0:pad].astype(BF16)

    left_edge = lane == 0
    right_edge = lane == win - 1

    def shifts(x):
        ahead = jnp.where(right_edge, 0.0, pltpu.roll(x, win - 1, 1))
        behind = jnp.where(left_edge, 0.0, pltpu.roll(x, 1, 1))
        return ahead.astype(BF16), x.astype(BF16), behind.astype(BF16)

    def spread_rows(f, row_nos):
        for r in row_nos:
            for b, part in enumerate(shifts(adj[f, r].astype(F32))):
                vs[f % 2, b * pad:(b + 1) * pad, r * win:(r + 1) * win] = part

    def first_conv(f, low, high):
        columns = slice(low * win, high * win)
        for side, w_ref in enumerate((w1_ref, w1_other)):
            hs[f % 2, side, :, columns] = jnp.dot(
                w_ref[:, 0:3 * pad], vs[f % 2, :, columns], preferred_element_type=F32)

    def begin(f):
        spread_rows(f, range(2, rows + 2))
        first_conv(f, 2, rows + 2)

    def rim_conv(f):
        spread_rows(f, (0, 1, rims - 2, rims - 1))
        first_conv(f, 0, 2)
        first_conv(f, rims - 2, rims)

    def rest(f):
        for side in range(2):
            for p in range(hid_rows):
                grad = sum(hs[f % 2, side, a * half:(a + 1) * half, (p + 2 - a) * win:(p + 3 - a) * win]
                           for a in range(3))
                scaled = (slope_win[side, p].astype(F32) * grad).astype(BF16).astype(F32)
                for b, part in enumerate(shifts(scaled)):
                    ss[f % 2, side, b * half:(b + 1) * half, p * win:(p + 1) * win] = part
        g = (jnp.dot(w2_ref[...], ss[f % 2, 0], preferred_element_type=F32)
             + jnp.dot(w2_other[...], ss[f % 2, 1], preferred_element_type=F32))
        return [adj[f, r + 2].astype(F32)
                + sum(g[a * pad:(a + 1) * pad, (r + 2 - a) * win:(r + 3 - a) * win] for a in range(3))
                for r in range(rows)]

    @pl.when(tm == 1)
    def _():
        for f in range(fronts):
            inn_copy(f).start()
        for load in loads[1:]:
            load.start()
        clear_rims()
        if pad > chans:
            for f in range(fronts):
                for r in range(rows):
                    adj[f, r + 2, chans:pad, :] = jnp.zeros((pad - chans, win), BF16)

        for f in range(fronts):
            inn_copy(f).wait()
            load_raw(f)
            for r in range(rows):
                value = forcing_row(r)
                adj[f, r + 2, 0:chans, :] = value.astype(BF16)
                put_out(f, r, value)
        pl.semaphore_wait(barrier, greeted)
        for f in range(far):
            x_copy(0, f).start()
        for f in range(far):
            x_copy(1, f).start()
        pass_on(0, far)
        pass_on(1, far)
        prepare_weights()
        w1_copy.start()
        w2_copy.start()

        t_copy(0).wait_recv()
        t_copy(1).wait_recv()
        slope_edges_start()
        w1_copy.wait_recv()
        begin(far)
        halos_here(far)
        rim_conv(far)
        w2_copy.wait_recv()
        t_copy(2).wait_recv()
        s_copy.start()
        t_copy(3).wait_recv()
        own_slopes()
        slopes_here()
        for r, value in enumerate(rest(far)):
            res[r] = value.astype(BF16)
            if r % 2 == 1:
                r_copy(r // 2).start()

        all_sent()
        halos_sent(far)
        for k in range(2):
            for f in range(far):
                x_copy(k, f).wait_send()
        for k in range(2):
            r_copy(k).wait_send()

    @pl.when(tm == 0)
    def _():
        for load in loads:
            load.start()
        for f in range(fronts):
            inn_copy(f).start()
        clear_rims()

        loads[0].wait()
        slope_f32[...] = slopes_ref[...].astype(F32)
        for r in range(band):
            slope_rows[r] = slope_f32[pl.ds(r, half, stride=band), :].astype(BF16)
        own_slopes()
        prepare_weights()

        pl.semaphore_wait(barrier, greeted)
        for k in range(4):
            t_copy(k).start()
        slope_edges_start()
        w1_copy.start()
        s_copy.start()
        w2_copy.start()

        for f in range(fronts):
            inn_copy(f).wait()
            load_raw(f)
            for r in range(rows):
                frc[f, r, 0:chans, :] = forcing_row(r).astype(BF16)

        for f in range(far):
            x_copy(0, f).wait_recv()
            pass_on(0, f)

        w1_copy.wait_recv()
        w2_copy.wait_recv()
        slopes_here()

        def finish(f):
            halos_here(f)
            rim_conv(f)
            for r, value in enumerate(rest(f)):
                put_out(f, r, value[0:chans] + frc[f, r, 0:chans, :].astype(F32))

        for f in range(far):
            x_copy(1, f).wait_recv()
            pass_on(1, f)
            if f > 0:
                finish(f - 1)
            begin(f)
        finish(far - 1)

        for k in range(2):
            r_copy(k).wait_recv()
            for r in (2 * k, 2 * k + 1):
                put_out(far, r, res[r, 0:chans, :].astype(F32) + frc[far, r, 0:chans, :].astype(F32))

        all_sent()
        for f in range(far):
            halos_sent(f)
        for k in range(4):
            t_copy(k).wait_send()


def chain_kernel(dims, layer_ref, mask_ref, inn_hbm, slopes_hbm, w_in_hbm, w_out_hbm, out_ref,
           inn_ref, slopes_ref, w_in_ref, w_out_ref, w_wide, w_tall,
           raw, send_x, adj, slope_f32, slope_rows, slope_win, w1_ref, w2_ref, w1_other,
           w2_other, vs, hs, ss, load_inn, load_rest,
           x_send, x_recv, h_send, h_recv, w_send, w_recv, s_send, s_recv):
    fronts, chans, rows, win, half, band, lats, owners = dims
    pad = send_x.shape[2]
    rims = rows + 4
    hid_rows = rows + 2
    grp = lax.axis_index("grp")
    lat = lax.axis_index("lat")
    tm = lax.axis_index("tm")
    core = lax.axis_index("chan")
    last = owners - 1

    def dev(lat_no, tm_no, core_no):
        return (grp, lat_no, tm_no, core_no)

    barrier = pltpu.get_barrier_semaphore()

    def greet(device):
        pl.semaphore_signal(barrier, inc=1, device_id=device, device_id_type=MESH)

    def inn_copy(f):
        return pltpu.make_async_copy(inn_hbm.at[f], inn_ref.at[f], load_inn.at[f])

    for f in range(fronts):
        inn_copy(f).start()

    lane = lax.broadcasted_iota(jnp.int32, (1, win), 1)
    tiles = mask_ref.shape[0]
    width = win // tiles
    spread = jnp.zeros((1, win), F32)
    for k in range(tiles):
        spread = jnp.where(lane // width == k, mask_ref[k].astype(F32), spread)

    def load_raw(f):
        raw[...] = inn_ref[f].astype(F32).reshape(chans * rows, win)

    def forcing_row(r):
        return raw[pl.ds(r, chans, stride=rows), :] * spread

    def put_out(f, r, value):
        out_ref[pl.ds(f * (chans * rows) + r, chans, stride=rows), :] = value

    starts = (core * 2, (1 - core) * 2)

    def x_copy(k, f):
        return pltpu.make_async_remote_copy(
            src_ref=send_x.at[f, pl.ds(starts[k], 2)], dst_ref=adj.at[f, pl.ds(2 + starts[k], 2)],
            send_sem=x_send.at[k, f], recv_sem=x_recv.at[k, f],
            device_id=dev(lat, lax.rem(tm + owners - 1, owners), core), device_id_type=MESH)

    def put_send(f, r, value):
        send_x[f, r, 0:chans, :] = value.astype(BF16)

    def clear_send():
        if pad > chans:
            for f in range(fronts):
                for r in range(rows):
                    send_x[f, r, chans:pad, :] = jnp.zeros((pad - chans, win), BF16)

    @pl.when(tm == last)
    def _():
        greet(dev(lat, tm - 1, core))
        clear_send()

        for f in range(fronts):
            inn_copy(f).wait()
            load_raw(f)
            for r in range(rows):
                value = forcing_row(r)
                put_out(f, r, value)
                put_send(f, r, value)
            if f == 0:
                pl.semaphore_wait(barrier, 1)
            x_copy(0, f).start()

        for f in range(fronts):
            x_copy(1, f).start()
        for f in range(fronts):
            for k in range(2):
                x_copy(k, f).wait_send()

    @pl.when(tm < last)
    def _():
        has_down = lat > 0
        has_up = lat < lats - 1
        greet(dev(lat, tm + 1, core))
        greet(dev(lat, tm, 1 - core))

        @pl.when(has_down)
        def _():
            greet(dev(lat - 1, tm, 0))
            greet(dev(lat - 1, tm, 1))

        @pl.when(has_up)
        def _():
            greet(dev(lat + 1, tm, 0))
            greet(dev(lat + 1, tm, 1))

        greeted = 2 + 2 * has_down.astype(jnp.int32) + 2 * has_up.astype(jnp.int32)
        if owners > 2:
            @pl.when(tm > 0)
            def _():
                greet(dev(lat, tm - 1, core))
            greeted = greeted + (tm > 0).astype(jnp.int32)
        clear_send()

        loads = [
            pltpu.make_async_copy(slopes_hbm, slopes_ref, load_rest.at[0]),
            pltpu.make_async_copy(w_out_hbm, w_out_ref, load_rest.at[1]),
            pltpu.make_async_copy(w_in_hbm, w_in_ref, load_rest.at[2]),
        ]
        for load in loads:
            load.start()
        w_wide[...] = jnp.zeros_like(w_wide)
        w_tall[...] = jnp.zeros_like(w_tall)

        loads[0].wait()
        slope_f32[...] = slopes_ref[...].astype(F32)
        for r in range(band):
            slope_rows[r] = slope_f32[pl.ds(r, half, stride=band), :].astype(BF16)

        first = (lat == 0) & (core == 0)
        final = (lat == lats - 1) & (core == 1)

        @pl.when(first)
        def _():
            slope_win[:, 0] = jnp.zeros((2, half, win), BF16)
            for f in range(fronts):
                adj[f, 0:2] = jnp.zeros((2, pad, win), BF16)

        @pl.when(final)
        def _():
            slope_win[:, hid_rows - 1] = jnp.zeros((2, half, win), BF16)
            for f in range(fronts):
                adj[f, rims - 2:rims] = jnp.zeros((2, pad, win), BF16)

        layer = layer_ref[tm]
        loads[1].wait()
        for a in range(3):
            for b in range(3):
                w_wide[b, a * half:(a + 1) * half, 0:chans] = w_out_ref[layer, a, b].astype(F32)
        wide = w_wide[0] + pltpu.roll(w_wide[1], pad, 1) + pltpu.roll(w_wide[2], 2 * pad, 1)
        w1_ref[...] = wide.astype(BF16)
        loads[2].wait()
        for a in range(3):
            for b in range(3):
                w_tall[a, b * half:(b + 1) * half, 0:chans] = w_in_ref[layer, a, b].astype(F32)
        for a in range(3):
            w2_ref[a * pad:(a + 1) * pad, :] = w_tall[a].T[0:pad].astype(BF16)

        pl.semaphore_wait(barrier, greeted)

        partner = dev(lat, tm, 1 - core)
        w1_copy = pltpu.make_async_remote_copy(
            src_ref=w1_ref, dst_ref=w1_other, send_sem=w_send.at[0], recv_sem=w_recv.at[0],
            device_id=partner, device_id_type=MESH)
        w2_copy = pltpu.make_async_remote_copy(
            src_ref=w2_ref, dst_ref=w2_other, send_sem=w_send.at[1], recv_sem=w_recv.at[1],
            device_id=partner, device_id_type=MESH)
        own = hid_rows - 1
        mine_from = core * (rows - 1)
        partner_from = (1 - core) * (rows - 1)
        s_copy = pltpu.make_async_remote_copy(
            src_ref=slope_rows.at[pl.ds(partner_from, own)],
            dst_ref=slope_win.at[1, pl.ds(core, own)],
            send_sem=s_send.at[0], recv_sem=s_recv.at[0],
            device_id=partner, device_id_type=MESH)
        s_down = pltpu.make_async_remote_copy(
            src_ref=slope_rows.at[0], dst_ref=slope_win.at[1 - core, hid_rows - 1],
            send_sem=s_send.at[1], recv_sem=s_recv.at[1 + (1 - core)],
            device_id=dev(lat - 1, tm, 1), device_id_type=MESH)
        s_up = pltpu.make_async_remote_copy(
            src_ref=slope_rows.at[band - 1], dst_ref=slope_win.at[core, 0],
            send_sem=s_send.at[2], recv_sem=s_recv.at[1 + core],
            device_id=dev(lat + 1, tm, 0), device_id_type=MESH)

        w1_copy.start()
        s_copy.start()
        w2_copy.start()

        @pl.when(has_down)
        def _():
            s_down.start()

        @pl.when(has_up)
        def _():
            s_up.start()

        slope_win[0, pl.ds(1 - core, own)] = slope_rows[pl.ds(mine_from, own)]

        not_first = jnp.logical_not(first)
        not_final = jnp.logical_not(final)

        def halo_down(f):
            return pltpu.make_async_remote_copy(
                src_ref=adj.at[f, pl.ds(2, 2)], dst_ref=adj.at[f, pl.ds(rims - 2, 2)],
                send_sem=h_send.at[0, f], recv_sem=h_recv.at[0, f],
                device_id=dev(lat - (1 - core), tm, 1 - core), device_id_type=MESH)

        def halo_up(f):
            return pltpu.make_async_remote_copy(
                src_ref=adj.at[f, pl.ds(rows, 2)], dst_ref=adj.at[f, pl.ds(0, 2)],
                send_sem=h_send.at[1, f], recv_sem=h_recv.at[1, f],
                device_id=dev(lat + core, tm, 1 - core), device_id_type=MESH)

        def pass_on(k, f):
            x_copy(k, f).wait_recv()

            @pl.when(not_first & (core == k))
            def _():
                halo_down(f).start()

            @pl.when(not_final & (core == 1 - k))
            def _():
                halo_up(f).start()

        left_edge = lane == 0
        right_edge = lane == win - 1

        def shifts(x):
            ahead = jnp.where(right_edge, 0.0, pltpu.roll(x, win - 1, 1))
            behind = jnp.where(left_edge, 0.0, pltpu.roll(x, 1, 1))
            return ahead.astype(BF16), x.astype(BF16), behind.astype(BF16)

        def spread_rows(f, row_nos):
            for r in row_nos:
                for b, part in enumerate(shifts(adj[f, r].astype(F32))):
                    vs[f % 2, b * pad:(b + 1) * pad, r * win:(r + 1) * win] = part

        def first_conv(f, low, high):
            columns = slice(low * win, high * win)
            for side, w_ref in enumerate((w1_ref, w1_other)):
                hs[f % 2, side, :, columns] = jnp.dot(
                    w_ref[:, 0:3 * pad], vs[f % 2, :, columns], preferred_element_type=F32)

        def compute(f):
            spread_rows(f, (0, 1, rims - 2, rims - 1))
            first_conv(f, 0, 2)
            first_conv(f, rims - 2, rims)
            for side in range(2):
                for p in range(hid_rows):
                    grad = sum(hs[f % 2, side, a * half:(a + 1) * half, (p + 2 - a) * win:(p + 3 - a) * win]
                               for a in range(3))
                    scaled = (slope_win[side, p].astype(F32) * grad).astype(BF16).astype(F32)
                    for b, part in enumerate(shifts(scaled)):
                        ss[f % 2, side, b * half:(b + 1) * half, p * win:(p + 1) * win] = part
            g = (jnp.dot(w2_ref[...], ss[f % 2, 0], preferred_element_type=F32)
                 + jnp.dot(w2_other[...], ss[f % 2, 1], preferred_element_type=F32))
            for r in range(rows):
                total = sum(g[a * pad:(a + 1) * pad, (r + 2 - a) * win:(r + 3 - a) * win]
                            for a in range(3))
                value = adj[f, r + 2].astype(F32) + total + send_x[f, r].astype(F32)
                value = value[0:chans]
                put_out(f, r, value)
                if owners > 2:
                    put_send(f, r, value)

        def finish(pair):
            for f in pair:
                @pl.when(not_final)
                def _():
                    halo_down(f).wait_recv()

                @pl.when(not_first)
                def _():
                    halo_up(f).wait_recv()

            for f in pair:
                compute(f)
            if owners > 2:
                @pl.when(tm > 0)
                def _():
                    for f in pair:
                        for k in range(2):
                            x_copy(k, f).start()

        for f in range(fronts):
            inn_copy(f).wait()
            load_raw(f)
            for r in range(rows):
                put_send(f, r, forcing_row(r))

        def begin(f):
            spread_rows(f, range(2, rows + 2))
            first_conv(f, 2, rows + 2)

        w1_copy.wait_recv()
        w2_copy.wait_recv()
        s_copy.wait_recv()

        @pl.when(has_down & (core == 0))
        def _():
            s_up_recv(slope_win, slope_rows, s_send, s_recv, 0, dev(lat, tm, 1 - core))

        @pl.when(has_up & (core == 1))
        def _():
            s_up_recv(slope_win, slope_rows, s_send, s_recv, hid_rows - 1, dev(lat, tm, 1 - core))

        @pl.loop(0, fronts)
        def _(f):
            pass_on(0, f)

        waiting = []
        for f in range(fronts):
            pass_on(1, f)
            if len(waiting) == 1:
                finish(waiting)
                waiting = []
            begin(f)
            waiting.append(f)
        finish(waiting)

        w1_copy.wait_send()
        w2_copy.wait_send()
        s_copy.wait_send()

        @pl.when(has_down)
        def _():
            s_down.wait_send()

        @pl.when(has_up)
        def _():
            s_up.wait_send()

        @pl.loop(0, fronts)
        def _(f):
            @pl.when(not_first)
            def _():
                halo_down(f).wait_send()

            @pl.when(not_final)
            def _():
                halo_up(f).wait_send()

            if owners > 2:
                @pl.when(tm > 0)
                def _():
                    for k in range(2):
                        x_copy(k, f).wait_send()


def s_up_recv(slope_win, slope_rows, s_send, s_recv, row, device):
    for side in range(2):
        pltpu.make_async_remote_copy(
            src_ref=slope_rows.at[0], dst_ref=slope_win.at[side, row],
            send_sem=s_send.at[1], recv_sem=s_recv.at[1 + side],
            device_id=device, device_id_type=MESH).wait_recv()


def in_hbm(array):
    return pltpu.with_memory_space_constraint(array, pltpu.HBM)


def per_device(mesh, innovations, obs_mask, slopes, layer_of, weight_in, weight_out):
    fronts, secs, chans, rows, win = innovations.shape
    _, half, band, _ = slopes.shape
    owners = mesh.shape["tm"]
    lats = mesh.shape["lat"]
    assert secs == 1 and band == 2 * rows and rows == 4 and owners > 1
    pair = owners == 2 and fronts > 1
    pad = round_up(chans, 16)
    rims, hid_rows = rows + 4, rows + 2

    layers = weight_in.shape[0]
    wide = round_up(3 * pad, 128)

    smem = pl.BlockSpec(memory_space=pltpu.SMEM)
    hbm = pl.BlockSpec(memory_space=pltpu.HBM)
    vmem = pl.BlockSpec(memory_space=pltpu.VMEM)
    out = pl.pallas_call(
        functools.partial(pair_kernel if pair else chain_kernel, (fronts, chans, rows, win, half, band, lats, owners)),
        out_shape=pltpu.VMEM((fronts * chans * rows, win), F32),
        in_specs=[smem, smem, hbm, hbm, hbm, hbm],
        out_specs=vmem,
        scratch_shapes=[
            pltpu.VMEM((fronts, chans, rows, win), BF16),
            pltpu.VMEM((half * band, win), BF16),
            pltpu.VMEM((layers, 3, 3, half, chans), BF16),
            pltpu.VMEM((layers, 3, 3, half, chans), BF16),
            pltpu.VMEM((3, 3 * half, wide), F32),
            pltpu.VMEM((3, 3 * half, 128), F32),
            pltpu.VMEM((chans * rows, win), F32),
            pltpu.VMEM((fronts, rows, pad, win), BF16),
            pltpu.VMEM((fronts, rims, pad, win), BF16),
            *([pltpu.VMEM((rows, pad, win), BF16)] if pair else []),
            pltpu.VMEM((half * band, win), F32),
            pltpu.VMEM((band, half, win), BF16),
            pltpu.VMEM((2, hid_rows, half, win), BF16),
            pltpu.VMEM((3 * half, wide), BF16),
            pltpu.VMEM((3 * pad, 3 * half), BF16),
            pltpu.VMEM((3 * half, wide), BF16),
            pltpu.VMEM((3 * pad, 3 * half), BF16),
            pltpu.VMEM((2, 3 * pad, rims * win), BF16),
            pltpu.VMEM((2, 2, 3 * half, rims * win), F32),
            pltpu.VMEM((2, 2, 3 * half, hid_rows * win), BF16),
            pltpu.SemaphoreType.DMA((fronts,)),
            pltpu.SemaphoreType.DMA((3,)),
            pltpu.SemaphoreType.DMA((2, fronts)),
            pltpu.SemaphoreType.DMA((2, fronts)),
            *([pltpu.SemaphoreType.DMA((2,))] * 2 if pair else []),
            pltpu.SemaphoreType.DMA((2, fronts)),
            pltpu.SemaphoreType.DMA((2, fronts)),
            pltpu.SemaphoreType.DMA((2,)),
            pltpu.SemaphoreType.DMA((2,)),
            pltpu.SemaphoreType.DMA((3,)),
            pltpu.SemaphoreType.DMA((3,)),
            *([pltpu.SemaphoreType.DMA((4,))] * 2 if pair else []),
        ],
        compiler_params=pltpu.CompilerParams(
            collective_id=0, has_side_effects=True, vmem_limit_bytes=32 * 1024 * 1024
        ),
    )(
        in_hbm(layer_of),
        in_hbm(obs_mask.reshape(obs_mask.shape[-1])),
        in_hbm(innovations.reshape(fronts, chans, rows, win)),
        in_hbm(slopes.reshape(half * band, win)),
        in_hbm(weight_in.swapaxes(3, 4)),
        in_hbm(weight_out),
    )
    return out.reshape(innovations.shape)


def solution(mesh):
    return jax.shard_map(
        functools.partial(per_device, mesh),
        mesh=mesh,
        in_specs=(
            P(None, ("grp", "tm"), None, ("lat", "chan"), None),
            P(("grp", "tm"), ("lat", "chan"), None),
            P(("grp", "tm"), "chan", "lat", None),
            P(),
            P(None, None, None, None, "chan"),
            P(None, None, None, "chan", None),
        ),
        out_specs=P(None, ("grp", "tm"), None, ("lat", "chan"), None),
        check_vma=False,
    )
```

```python
import functools

import jax
import jax.numpy as jnp
from jax import lax
from jax.experimental import pallas as pl
from jax.experimental.pallas import tpu as pltpu
from jax.sharding import PartitionSpec as P

MESH = pl.DeviceIdType.MESH
BF16 = jnp.bfloat16
F32 = jnp.float32


def round_up(n, m):
    return -(-n // m) * m


def pair_kernel(dims, layer_ref, mask_ref, inn_hbm, slopes_hbm, w_in_hbm, w_out_hbm, out_ref,
                inn_ref, slopes_ref, w_in_ref, w_out_ref, w_wide, w_tall,
                raw, frc, adj, res, slope_f32, slope_rows, slope_win, w1_ref, w2_ref, w1_other,
                w2_other, vs, hs, ss, load_inn, load_rest,
                x_send, x_recv, r_send, r_recv, h_send, h_recv, w_send, w_recv, s_send, s_recv,
                t_send, t_recv, above):
    fronts, chans, rows, win, half, band, lats, owners = dims
    pad = frc.shape[2]
    rims = rows + 4
    hid_rows = rows + 2
    far = fronts - 1
    grp = lax.axis_index("grp")
    lat = lax.axis_index("lat")
    tm = lax.axis_index("tm")
    core = lax.axis_index("chan")

    def dev(lat_no, tm_no, core_no):
        return (grp, lat_no, tm_no, core_no)

    partner = dev(lat, tm, 1 - core)
    opposite = dev(lat, 1 - tm, core)
    has_down = lat > 0
    has_up = lat < lats - 1
    first = (lat == 0) & (core == 0)
    final = (lat == lats - 1) & (core == 1)
    not_first = jnp.logical_not(first)
    not_final = jnp.logical_not(final)

    barrier = pltpu.get_barrier_semaphore()

    def greet(device):
        pl.semaphore_signal(barrier, inc=1, device_id=device, device_id_type=MESH)

    greet(opposite)

    @pl.when(has_up)
    def _():
        greet(dev(lat + 1, tm, 0))

        @pl.when(core == 1)
        def _():
            greet(dev(lat + 1, tm, 1))

        @pl.when(tm == 0)
        def _():
            greet(dev(lat + 1, 1, 0))

        @pl.when((tm == 1) & (core == 1))
        def _():
            greet(dev(lat + 1, 0, 0))
            greet(dev(lat + 1, 0, 1))

    greet(partner)
    below = has_down.astype(jnp.int32)

    def enter():
        pl.semaphore_wait(barrier, 2 + below * (2 - core + (1 - tm) + 2 * tm * (1 - core)))

        @pl.when(has_down & (core == 0))
        def _():
            for c in range(2):
                pl.semaphore_signal(above, inc=1, device_id=dev(lat - 1, tm, c), device_id_type=MESH)

        @pl.when(has_down & (core == 0) & (tm == 1))
        def _():
            for c in range(2):
                pl.semaphore_signal(above, inc=1, device_id=dev(lat - 1, 0, c), device_id_type=MESH)

    def wait_above():
        @pl.when(has_up)
        def _():
            pl.semaphore_wait(above, 2 - tm)

    def inn_copy(f):
        return pltpu.make_async_copy(inn_hbm.at[f], inn_ref.at[f], load_inn.at[f])

    loads = [
        pltpu.make_async_copy(slopes_hbm, slopes_ref, load_rest.at[0]),
        pltpu.make_async_copy(w_out_hbm, w_out_ref, load_rest.at[1]),
        pltpu.make_async_copy(w_in_hbm, w_in_ref, load_rest.at[2]),
    ]

    lane = lax.broadcasted_iota(jnp.int32, (1, win), 1)
    tiles = mask_ref.shape[0]
    width = win // tiles
    spread = jnp.zeros((1, win), F32)
    for k in range(tiles):
        spread = jnp.where(lane // width == k, mask_ref[k].astype(F32), spread)

    def load_raw(f):
        raw[...] = inn_ref[f].astype(F32).reshape(chans * rows, win)

    def forcing_row(r):
        return raw[pl.ds(r, chans, stride=rows), :] * spread

    def put_out(f, r, value):
        out_ref[pl.ds(f * (chans * rows) + r, chans, stride=rows), :] = value

    starts = (core * 2, (1 - core) * 2)

    def x_copy(k, f):
        part = adj.at[f, pl.ds(2 + starts[k], 2)]
        return pltpu.make_async_remote_copy(
            src_ref=part, dst_ref=part, send_sem=x_send.at[k, f], recv_sem=x_recv.at[k, f],
            device_id=opposite, device_id_type=MESH)

    def r_copy(k):
        part = res.at[pl.ds(2 * k, 2)]
        return pltpu.make_async_remote_copy(
            src_ref=part, dst_ref=part, send_sem=r_send.at[k], recv_sem=r_recv.at[k],
            device_id=opposite, device_id_type=MESH)

    spans = ((3 - 3 * core, 5), (5 * core, 3))

    def t_copy(k):
        part = slope_rows.at[pl.ds(*spans[k])]
        return pltpu.make_async_remote_copy(
            src_ref=part, dst_ref=part, send_sem=t_send.at[k], recv_sem=t_recv.at[k],
            device_id=opposite, device_id_type=MESH)

    def halo_down(f):
        return pltpu.make_async_remote_copy(
            src_ref=adj.at[f, pl.ds(2, 2)], dst_ref=adj.at[f, pl.ds(rims - 2, 2)],
            send_sem=h_send.at[0, f], recv_sem=h_recv.at[0, f],
            device_id=dev(lat - (1 - core), tm, 1 - core), device_id_type=MESH)

    def halo_up(f):
        return pltpu.make_async_remote_copy(
            src_ref=adj.at[f, pl.ds(rows, 2)], dst_ref=adj.at[f, pl.ds(0, 2)],
            send_sem=h_send.at[1, f], recv_sem=h_recv.at[1, f],
            device_id=dev(lat + core, tm, 1 - core), device_id_type=MESH)

    def pass_on(k, f):
        @pl.when(not_first & (core == k))
        def _():
            halo_down(f).start()

        @pl.when(not_final & (core == 1 - k))
        def _():
            halo_up(f).start()

    def halos_here(f):
        @pl.when(not_final)
        def _():
            halo_down(f).wait_recv()

        @pl.when(not_first)
        def _():
            halo_up(f).wait_recv()

    def halos_sent(f):
        @pl.when(not_first)
        def _():
            halo_down(f).wait_send()

        @pl.when(not_final)
        def _():
            halo_up(f).wait_send()

    w1_copy = pltpu.make_async_remote_copy(
        src_ref=w1_ref, dst_ref=w1_other, send_sem=w_send.at[0], recv_sem=w_recv.at[0],
        device_id=partner, device_id_type=MESH)
    w2_copy = pltpu.make_async_remote_copy(
        src_ref=w2_ref, dst_ref=w2_other, send_sem=w_send.at[1], recv_sem=w_recv.at[1],
        device_id=partner, device_id_type=MESH)
    own = hid_rows - 1
    mine_from = core * (rows - 1)
    partner_from = (1 - core) * (rows - 1)
    s_copy = pltpu.make_async_remote_copy(
        src_ref=slope_rows.at[pl.ds(partner_from, own)],
        dst_ref=slope_win.at[1, pl.ds(core, own)],
        send_sem=s_send.at[0], recv_sem=s_recv.at[0],
        device_id=partner, device_id_type=MESH)

    def s_down(to, k):
        return pltpu.make_async_remote_copy(
            src_ref=slope_rows.at[0], dst_ref=slope_win.at[1 - core, hid_rows - 1],
            send_sem=s_send.at[1 + k], recv_sem=s_recv.at[1 + (1 - core)],
            device_id=dev(lat - 1, to, 1), device_id_type=MESH)

    def s_up(to, k):
        return pltpu.make_async_remote_copy(
            src_ref=slope_rows.at[band - 1], dst_ref=slope_win.at[core, 0],
            send_sem=s_send.at[3 + k], recv_sem=s_recv.at[1 + core],
            device_id=dev(lat + 1, to, 0), device_id_type=MESH)

    def slope_down(act, to):
        @pl.when(has_down)
        def _():
            act(s_down(to, to))

    def slope_up(act, to):
        @pl.when(has_up)
        def _():
            act(s_up(to, to))

    def start(copy):
        copy.start()

    def slopes_here():
        s_copy.wait_recv()

        @pl.when(has_down & (core == 0))
        def _():
            s_up_recv(slope_win, slope_rows, s_send, s_recv, 0, partner)

        @pl.when(has_up & (core == 1))
        def _():
            s_up_recv(slope_win, slope_rows, s_send, s_recv, hid_rows - 1, partner)

    def own_slopes():
        slope_win[0, pl.ds(1 - core, own)] = slope_rows[pl.ds(mine_from, own)]

    def all_sent():
        w1_copy.wait_send()
        w2_copy.wait_send()
        s_copy.wait_send()

    def clear_rims():
        @pl.when(first)
        def _():
            slope_win[:, 0] = jnp.zeros((2, half, win), BF16)
            for f in range(fronts):
                adj[f, 0:2] = jnp.zeros((2, pad, win), BF16)

        @pl.when(final)
        def _():
            slope_win[:, hid_rows - 1] = jnp.zeros((2, half, win), BF16)
            for f in range(fronts):
                adj[f, rims - 2:rims] = jnp.zeros((2, pad, win), BF16)

    def prepare_weights():
        w_wide[...] = jnp.zeros_like(w_wide)
        w_tall[...] = jnp.zeros_like(w_tall)
        layer = layer_ref[0]
        loads[1].wait()
        for a in range(3):
            for b in range(3):
                w_wide[b, a * half:(a + 1) * half, 0:chans] = w_out_ref[layer, a, b].astype(F32)
        wide = w_wide[0] + pltpu.roll(w_wide[1], pad, 1) + pltpu.roll(w_wide[2], 2 * pad, 1)
        w1_ref[...] = wide.astype(BF16)
        loads[2].wait()
        for a in range(3):
            for b in range(3):
                w_tall[a, b * half:(b + 1) * half, 0:chans] = w_in_ref[layer, a, b].astype(F32)
        for a in range(3):
            w2_ref[a * pad:(a + 1) * pad, :] = w_tall[a].T[0:pad].astype(BF16)

    left_edge = lane == 0
    right_edge = lane == win - 1

    def shifts(x):
        ahead = jnp.where(right_edge, 0.0, pltpu.roll(x, win - 1, 1))
        behind = jnp.where(left_edge, 0.0, pltpu.roll(x, 1, 1))
        return ahead.astype(BF16), x.astype(BF16), behind.astype(BF16)

    def spread_rows(f, row_nos):
        for r in row_nos:
            for b, part in enumerate(shifts(adj[f, r].astype(F32))):
                vs[f % 2, b * pad:(b + 1) * pad, r * win:(r + 1) * win] = part

    def first_conv(f, low, high):
        columns = slice(low * win, high * win)
        for side, w_ref in enumerate((w1_ref, w1_other)):
            hs[f % 2, side, :, columns] = jnp.dot(
                w_ref[:, 0:3 * pad], vs[f % 2, :, columns], preferred_element_type=F32)

    def begin(f):
        spread_rows(f, range(2, rows + 2))
        first_conv(f, 2, rows + 2)

    def rim_conv(f):
        spread_rows(f, (0, 1, rims - 2, rims - 1))
        first_conv(f, 0, 2)
        first_conv(f, rims - 2, rims)

    def rest(f):
        for side in range(2):
            for p in range(hid_rows):
                grad = sum(hs[f % 2, side, a * half:(a + 1) * half, (p + 2 - a) * win:(p + 3 - a) * win]
                           for a in range(3))
                scaled = (slope_win[side, p].astype(F32) * grad).astype(BF16).astype(F32)
                for b, part in enumerate(shifts(scaled)):
                    ss[f % 2, side, b * half:(b + 1) * half, p * win:(p + 1) * win] = part
        g = (jnp.dot(w2_ref[...], ss[f % 2, 0], preferred_element_type=F32)
             + jnp.dot(w2_other[...], ss[f % 2, 1], preferred_element_type=F32))
        return [adj[f, r + 2].astype(F32)
                + sum(g[a * pad:(a + 1) * pad, (r + 2 - a) * win:(r + 3 - a) * win] for a in range(3))
                for r in range(rows)]

    @pl.when(tm == 1)
    def _():
        for f in range(fronts):
            inn_copy(f).start()
        for load in loads[1:]:
            load.start()
        clear_rims()
        if pad > chans:
            for f in range(fronts):
                for r in range(rows):
                    adj[f, r + 2, chans:pad, :] = jnp.zeros((pad - chans, win), BF16)

        def take(f):
            inn_copy(f).wait()
            load_raw(f)
            for r in range(rows):
                adj[f, r + 2, 0:chans, :] = forcing_row(r).astype(BF16)

        take(0)
        enter()
        x_copy(0, 0).start()
        for f in range(1, far):
            take(f)
            x_copy(0, f).start()
        for f in range(far):
            x_copy(1, f).start()
        take(far)
        wait_above()
        pass_on(0, far)
        pass_on(1, far)
        prepare_weights()
        w1_copy.start()
        w2_copy.start()
        for f in range(fronts):
            for r in range(rows):
                put_out(f, r, adj[f, r + 2, 0:chans, :].astype(F32))

        w1_copy.wait_recv()
        begin(far)
        halos_here(far)
        rim_conv(far)
        w2_copy.wait_recv()
        t_copy(0).wait_recv()
        s_copy.start()
        t_copy(1).wait_recv()
        own_slopes()
        slopes_here()
        for r, value in enumerate(rest(far)):
            res[r] = value.astype(BF16)
            if r % 2 == 1:
                r_copy(r // 2).start()

        all_sent()
        halos_sent(far)
        for k in range(2):
            for f in range(far):
                x_copy(k, f).wait_send()
        for k in range(2):
            r_copy(k).wait_send()

    @pl.when(tm == 0)
    def _():
        for load in loads:
            load.start()
        for f in range(fronts):
            inn_copy(f).start()
        clear_rims()

        loads[0].wait()
        slope_f32[...] = slopes_ref[...].astype(F32)
        for r in range(band):
            slope_rows[r] = slope_f32[pl.ds(r, half, stride=band), :].astype(BF16)
        enter()
        slope_down(start, 1)
        for k in range(2):
            t_copy(k).start()
        slope_down(start, 0)
        s_copy.start()
        own_slopes()
        prepare_weights()
        wait_above()
        slope_up(start, 1)
        slope_up(start, 0)
        w1_copy.start()
        w2_copy.start()

        for f in range(fronts):
            inn_copy(f).wait()
            load_raw(f)
            for r in range(rows):
                frc[f, r, 0:chans, :] = forcing_row(r).astype(BF16)

        for f in range(far):
            x_copy(0, f).wait_recv()
            pass_on(0, f)

        w1_copy.wait_recv()
        w2_copy.wait_recv()
        slopes_here()

        def finish(f):
            halos_here(f)
            rim_conv(f)
            for r, value in enumerate(rest(f)):
                put_out(f, r, value[0:chans] + frc[f, r, 0:chans, :].astype(F32))

        for f in range(far):
            x_copy(1, f).wait_recv()
            pass_on(1, f)
            if f > 0:
                finish(f - 1)
            begin(f)
        finish(far - 1)

        for k in range(2):
            r_copy(k).wait_recv()
            for r in (2 * k, 2 * k + 1):
                put_out(far, r, res[r, 0:chans, :].astype(F32) + frc[far, r, 0:chans, :].astype(F32))

        all_sent()
        for f in range(far):
            halos_sent(f)
        for k in range(2):
            t_copy(k).wait_send()
            slope_down(lambda copy: copy.wait_send(), k)
            slope_up(lambda copy: copy.wait_send(), k)


def chain_kernel(dims, layer_ref, mask_ref, inn_hbm, slopes_hbm, w_in_hbm, w_out_hbm, out_ref,
           inn_ref, slopes_ref, w_in_ref, w_out_ref, w_wide, w_tall,
           raw, send_x, adj, slope_f32, slope_rows, slope_win, w1_ref, w2_ref, w1_other,
           w2_other, vs, hs, ss, load_inn, load_rest,
           x_send, x_recv, h_send, h_recv, w_send, w_recv, s_send, s_recv):
    fronts, chans, rows, win, half, band, lats, owners = dims
    pad = send_x.shape[2]
    rims = rows + 4
    hid_rows = rows + 2
    grp = lax.axis_index("grp")
    lat = lax.axis_index("lat")
    tm = lax.axis_index("tm")
    core = lax.axis_index("chan")
    last = owners - 1

    def dev(lat_no, tm_no, core_no):
        return (grp, lat_no, tm_no, core_no)

    barrier = pltpu.get_barrier_semaphore()

    def greet(device):
        pl.semaphore_signal(barrier, inc=1, device_id=device, device_id_type=MESH)

    def inn_copy(f):
        return pltpu.make_async_copy(inn_hbm.at[f], inn_ref.at[f], load_inn.at[f])

    for f in range(fronts):
        inn_copy(f).start()

    lane = lax.broadcasted_iota(jnp.int32, (1, win), 1)
    tiles = mask_ref.shape[0]
    width = win // tiles
    spread = jnp.zeros((1, win), F32)
    for k in range(tiles):
        spread = jnp.where(lane // width == k, mask_ref[k].astype(F32), spread)

    def load_raw(f):
        raw[...] = inn_ref[f].astype(F32).reshape(chans * rows, win)

    def forcing_row(r):
        return raw[pl.ds(r, chans, stride=rows), :] * spread

    def put_out(f, r, value):
        out_ref[pl.ds(f * (chans * rows) + r, chans, stride=rows), :] = value

    starts = (core * 2, (1 - core) * 2)

    def x_copy(k, f):
        return pltpu.make_async_remote_copy(
            src_ref=send_x.at[f, pl.ds(starts[k], 2)], dst_ref=adj.at[f, pl.ds(2 + starts[k], 2)],
            send_sem=x_send.at[k, f], recv_sem=x_recv.at[k, f],
            device_id=dev(lat, lax.rem(tm + owners - 1, owners), core), device_id_type=MESH)

    def put_send(f, r, value):
        send_x[f, r, 0:chans, :] = value.astype(BF16)

    def clear_send():
        if pad > chans:
            for f in range(fronts):
                for r in range(rows):
                    send_x[f, r, chans:pad, :] = jnp.zeros((pad - chans, win), BF16)

    @pl.when(tm == last)
    def _():
        greet(dev(lat, tm - 1, core))
        clear_send()

        for f in range(fronts):
            inn_copy(f).wait()
            load_raw(f)
            for r in range(rows):
                value = forcing_row(r)
                put_out(f, r, value)
                put_send(f, r, value)
            if f == 0:
                pl.semaphore_wait(barrier, 1)
            x_copy(0, f).start()

        for f in range(fronts):
            x_copy(1, f).start()
        for f in range(fronts):
            for k in range(2):
                x_copy(k, f).wait_send()

    @pl.when(tm < last)
    def _():
        has_down = lat > 0
        has_up = lat < lats - 1
        greet(dev(lat, tm + 1, core))
        greet(dev(lat, tm, 1 - core))

        @pl.when(has_down)
        def _():
            greet(dev(lat - 1, tm, 0))
            greet(dev(lat - 1, tm, 1))

        @pl.when(has_up)
        def _():
            greet(dev(lat + 1, tm, 0))
            greet(dev(lat + 1, tm, 1))

        greeted = 2 + 2 * has_down.astype(jnp.int32) + 2 * has_up.astype(jnp.int32)
        if owners > 2:
            @pl.when(tm > 0)
            def _():
                greet(dev(lat, tm - 1, core))
            greeted = greeted + (tm > 0).astype(jnp.int32)
        clear_send()

        loads = [
            pltpu.make_async_copy(slopes_hbm, slopes_ref, load_rest.at[0]),
            pltpu.make_async_copy(w_out_hbm, w_out_ref, load_rest.at[1]),
            pltpu.make_async_copy(w_in_hbm, w_in_ref, load_rest.at[2]),
        ]
        for load in loads:
            load.start()
        w_wide[...] = jnp.zeros_like(w_wide)
        w_tall[...] = jnp.zeros_like(w_tall)

        loads[0].wait()
        slope_f32[...] = slopes_ref[...].astype(F32)
        for r in range(band):
            slope_rows[r] = slope_f32[pl.ds(r, half, stride=band), :].astype(BF16)

        first = (lat == 0) & (core == 0)
        final = (lat == lats - 1) & (core == 1)

        @pl.when(first)
        def _():
            slope_win[:, 0] = jnp.zeros((2, half, win), BF16)
            for f in range(fronts):
                adj[f, 0:2] = jnp.zeros((2, pad, win), BF16)

        @pl.when(final)
        def _():
            slope_win[:, hid_rows - 1] = jnp.zeros((2, half, win), BF16)
            for f in range(fronts):
                adj[f, rims - 2:rims] = jnp.zeros((2, pad, win), BF16)

        layer = layer_ref[tm]
        loads[1].wait()
        for a in range(3):
            for b in range(3):
                w_wide[b, a * half:(a + 1) * half, 0:chans] = w_out_ref[layer, a, b].astype(F32)
        wide = w_wide[0] + pltpu.roll(w_wide[1], pad, 1) + pltpu.roll(w_wide[2], 2 * pad, 1)
        w1_ref[...] = wide.astype(BF16)
        loads[2].wait()
        for a in range(3):
            for b in range(3):
                w_tall[a, b * half:(b + 1) * half, 0:chans] = w_in_ref[layer, a, b].astype(F32)
        for a in range(3):
            w2_ref[a * pad:(a + 1) * pad, :] = w_tall[a].T[0:pad].astype(BF16)

        pl.semaphore_wait(barrier, greeted)

        partner = dev(lat, tm, 1 - core)
        w1_copy = pltpu.make_async_remote_copy(
            src_ref=w1_ref, dst_ref=w1_other, send_sem=w_send.at[0], recv_sem=w_recv.at[0],
            device_id=partner, device_id_type=MESH)
        w2_copy = pltpu.make_async_remote_copy(
            src_ref=w2_ref, dst_ref=w2_other, send_sem=w_send.at[1], recv_sem=w_recv.at[1],
            device_id=partner, device_id_type=MESH)
        own = hid_rows - 1
        mine_from = core * (rows - 1)
        partner_from = (1 - core) * (rows - 1)
        s_copy = pltpu.make_async_remote_copy(
            src_ref=slope_rows.at[pl.ds(partner_from, own)],
            dst_ref=slope_win.at[1, pl.ds(core, own)],
            send_sem=s_send.at[0], recv_sem=s_recv.at[0],
            device_id=partner, device_id_type=MESH)
        s_down = pltpu.make_async_remote_copy(
            src_ref=slope_rows.at[0], dst_ref=slope_win.at[1 - core, hid_rows - 1],
            send_sem=s_send.at[1], recv_sem=s_recv.at[1 + (1 - core)],
            device_id=dev(lat - 1, tm, 1), device_id_type=MESH)
        s_up = pltpu.make_async_remote_copy(
            src_ref=slope_rows.at[band - 1], dst_ref=slope_win.at[core, 0],
            send_sem=s_send.at[2], recv_sem=s_recv.at[1 + core],
            device_id=dev(lat + 1, tm, 0), device_id_type=MESH)

        w1_copy.start()
        s_copy.start()
        w2_copy.start()

        @pl.when(has_down)
        def _():
            s_down.start()

        @pl.when(has_up)
        def _():
            s_up.start()

        slope_win[0, pl.ds(1 - core, own)] = slope_rows[pl.ds(mine_from, own)]

        not_first = jnp.logical_not(first)
        not_final = jnp.logical_not(final)

        def halo_down(f):
            return pltpu.make_async_remote_copy(
                src_ref=adj.at[f, pl.ds(2, 2)], dst_ref=adj.at[f, pl.ds(rims - 2, 2)],
                send_sem=h_send.at[0, f], recv_sem=h_recv.at[0, f],
                device_id=dev(lat - (1 - core), tm, 1 - core), device_id_type=MESH)

        def halo_up(f):
            return pltpu.make_async_remote_copy(
                src_ref=adj.at[f, pl.ds(rows, 2)], dst_ref=adj.at[f, pl.ds(0, 2)],
                send_sem=h_send.at[1, f], recv_sem=h_recv.at[1, f],
                device_id=dev(lat + core, tm, 1 - core), device_id_type=MESH)

        def pass_on(k, f):
            x_copy(k, f).wait_recv()

            @pl.when(not_first & (core == k))
            def _():
                halo_down(f).start()

            @pl.when(not_final & (core == 1 - k))
            def _():
                halo_up(f).start()

        left_edge = lane == 0
        right_edge = lane == win - 1

        def shifts(x):
            ahead = jnp.where(right_edge, 0.0, pltpu.roll(x, win - 1, 1))
            behind = jnp.where(left_edge, 0.0, pltpu.roll(x, 1, 1))
            return ahead.astype(BF16), x.astype(BF16), behind.astype(BF16)

        def spread_rows(f, row_nos):
            for r in row_nos:
                for b, part in enumerate(shifts(adj[f, r].astype(F32))):
                    vs[f % 2, b * pad:(b + 1) * pad, r * win:(r + 1) * win] = part

        def first_conv(f, low, high):
            columns = slice(low * win, high * win)
            for side, w_ref in enumerate((w1_ref, w1_other)):
                hs[f % 2, side, :, columns] = jnp.dot(
                    w_ref[:, 0:3 * pad], vs[f % 2, :, columns], preferred_element_type=F32)

        def compute(f):
            spread_rows(f, (0, 1, rims - 2, rims - 1))
            first_conv(f, 0, 2)
            first_conv(f, rims - 2, rims)
            for side in range(2):
                for p in range(hid_rows):
                    grad = sum(hs[f % 2, side, a * half:(a + 1) * half, (p + 2 - a) * win:(p + 3 - a) * win]
                               for a in range(3))
                    scaled = (slope_win[side, p].astype(F32) * grad).astype(BF16).astype(F32)
                    for b, part in enumerate(shifts(scaled)):
                        ss[f % 2, side, b * half:(b + 1) * half, p * win:(p + 1) * win] = part
            g = (jnp.dot(w2_ref[...], ss[f % 2, 0], preferred_element_type=F32)
                 + jnp.dot(w2_other[...], ss[f % 2, 1], preferred_element_type=F32))
            for r in range(rows):
                total = sum(g[a * pad:(a + 1) * pad, (r + 2 - a) * win:(r + 3 - a) * win]
                            for a in range(3))
                value = adj[f, r + 2].astype(F32) + total + send_x[f, r].astype(F32)
                value = value[0:chans]
                put_out(f, r, value)
                if owners > 2:
                    put_send(f, r, value)

        def finish(pair):
            for f in pair:
                @pl.when(not_final)
                def _():
                    halo_down(f).wait_recv()

                @pl.when(not_first)
                def _():
                    halo_up(f).wait_recv()

            for f in pair:
                compute(f)
            if owners > 2:
                @pl.when(tm > 0)
                def _():
                    for f in pair:
                        for k in range(2):
                            x_copy(k, f).start()

        for f in range(fronts):
            inn_copy(f).wait()
            load_raw(f)
            for r in range(rows):
                put_send(f, r, forcing_row(r))

        def begin(f):
            spread_rows(f, range(2, rows + 2))
            first_conv(f, 2, rows + 2)

        w1_copy.wait_recv()
        w2_copy.wait_recv()
        s_copy.wait_recv()

        @pl.when(has_down & (core == 0))
        def _():
            s_up_recv(slope_win, slope_rows, s_send, s_recv, 0, dev(lat, tm, 1 - core))

        @pl.when(has_up & (core == 1))
        def _():
            s_up_recv(slope_win, slope_rows, s_send, s_recv, hid_rows - 1, dev(lat, tm, 1 - core))

        @pl.loop(0, fronts)
        def _(f):
            pass_on(0, f)

        waiting = []
        for f in range(fronts):
            pass_on(1, f)
            if len(waiting) == 1:
                finish(waiting)
                waiting = []
            begin(f)
            waiting.append(f)
        finish(waiting)

        w1_copy.wait_send()
        w2_copy.wait_send()
        s_copy.wait_send()

        @pl.when(has_down)
        def _():
            s_down.wait_send()

        @pl.when(has_up)
        def _():
            s_up.wait_send()

        @pl.loop(0, fronts)
        def _(f):
            @pl.when(not_first)
            def _():
                halo_down(f).wait_send()

            @pl.when(not_final)
            def _():
                halo_up(f).wait_send()

            if owners > 2:
                @pl.when(tm > 0)
                def _():
                    for k in range(2):
                        x_copy(k, f).wait_send()


def s_up_recv(slope_win, slope_rows, s_send, s_recv, row, device):
    for side in range(2):
        pltpu.make_async_remote_copy(
            src_ref=slope_rows.at[0], dst_ref=slope_win.at[side, row],
            send_sem=s_send.at[1], recv_sem=s_recv.at[1 + side],
            device_id=device, device_id_type=MESH).wait_recv()


def in_hbm(array):
    return pltpu.with_memory_space_constraint(array, pltpu.HBM)


def per_device(mesh, innovations, obs_mask, slopes, layer_of, weight_in, weight_out):
    fronts, secs, chans, rows, win = innovations.shape
    _, half, band, _ = slopes.shape
    owners = mesh.shape["tm"]
    lats = mesh.shape["lat"]
    assert secs == 1 and band == 2 * rows and rows == 4 and owners > 1
    pair = owners == 2 and fronts > 1
    pad = round_up(chans, 16)
    rims, hid_rows = rows + 4, rows + 2

    layers = weight_in.shape[0]
    wide = round_up(3 * pad, 128)

    smem = pl.BlockSpec(memory_space=pltpu.SMEM)
    hbm = pl.BlockSpec(memory_space=pltpu.HBM)
    vmem = pl.BlockSpec(memory_space=pltpu.VMEM)
    out = pl.pallas_call(
        functools.partial(pair_kernel if pair else chain_kernel, (fronts, chans, rows, win, half, band, lats, owners)),
        out_shape=pltpu.VMEM((fronts * chans * rows, win), F32),
        in_specs=[smem, smem, hbm, hbm, hbm, hbm],
        out_specs=vmem,
        scratch_shapes=[
            pltpu.VMEM((fronts, chans, rows, win), BF16),
            pltpu.VMEM((half * band, win), BF16),
            pltpu.VMEM((layers, 3, 3, half, chans), BF16),
            pltpu.VMEM((layers, 3, 3, half, chans), BF16),
            pltpu.VMEM((3, 3 * half, wide), F32),
            pltpu.VMEM((3, 3 * half, 128), F32),
            pltpu.VMEM((chans * rows, win), F32),
            pltpu.VMEM((fronts, rows, pad, win), BF16),
            pltpu.VMEM((fronts, rims, pad, win), BF16),
            *([pltpu.VMEM((rows, pad, win), BF16)] if pair else []),
            pltpu.VMEM((half * band, win), F32),
            pltpu.VMEM((band, half, win), BF16),
            pltpu.VMEM((2, hid_rows, half, win), BF16),
            pltpu.VMEM((3 * half, wide), BF16),
            pltpu.VMEM((3 * pad, 3 * half), BF16),
            pltpu.VMEM((3 * half, wide), BF16),
            pltpu.VMEM((3 * pad, 3 * half), BF16),
            pltpu.VMEM((2, 3 * pad, rims * win), BF16),
            pltpu.VMEM((2, 2, 3 * half, rims * win), F32),
            pltpu.VMEM((2, 2, 3 * half, hid_rows * win), BF16),
            pltpu.SemaphoreType.DMA((fronts,)),
            pltpu.SemaphoreType.DMA((3,)),
            pltpu.SemaphoreType.DMA((2, fronts)),
            pltpu.SemaphoreType.DMA((2, fronts)),
            *([pltpu.SemaphoreType.DMA((2,))] * 2 if pair else []),
            pltpu.SemaphoreType.DMA((2, fronts)),
            pltpu.SemaphoreType.DMA((2, fronts)),
            pltpu.SemaphoreType.DMA((2,)),
            pltpu.SemaphoreType.DMA((2,)),
            pltpu.SemaphoreType.DMA((5,)),
            pltpu.SemaphoreType.DMA((3,)),
            *([pltpu.SemaphoreType.DMA((2,))] * 2 + [pltpu.SemaphoreType.REGULAR] if pair else []),
        ],
        compiler_params=pltpu.CompilerParams(
            collective_id=0, has_side_effects=True, vmem_limit_bytes=32 * 1024 * 1024
        ),
    )(
        in_hbm(layer_of),
        in_hbm(obs_mask.reshape(obs_mask.shape[-1])),
        in_hbm(innovations.reshape(fronts, chans, rows, win)),
        in_hbm(slopes.reshape(half * band, win)),
        in_hbm(weight_in.swapaxes(3, 4)),
        in_hbm(weight_out),
    )
    return out.reshape(innovations.shape)


def solution(mesh):
    return jax.shard_map(
        functools.partial(per_device, mesh),
        mesh=mesh,
        in_specs=(
            P(None, ("grp", "tm"), None, ("lat", "chan"), None),
            P(("grp", "tm"), ("lat", "chan"), None),
            P(("grp", "tm"), "chan", "lat", None),
            P(),
            P(None, None, None, None, "chan"),
            P(None, None, None, "chan", None),
        ),
        out_specs=P(None, ("grp", "tm"), None, ("lat", "chan"), None),
        check_vma=False,
    )
```

```python
import functools

import jax
import jax.numpy as jnp
from jax import lax
from jax.experimental import pallas as pl
from jax.experimental.pallas import tpu as pltpu
from jax.sharding import PartitionSpec as P

MESH = pl.DeviceIdType.MESH
BF16 = jnp.bfloat16
F32 = jnp.float32


def round_up(n, m):
    return -(-n // m) * m


def pair_kernel(dims, layer_ref, mask_ref, inn_hbm, slopes_hbm, w_in_hbm, w_out_hbm, out_ref,
                inn_ref, slopes_ref, w_in_ref, w_out_ref, w_wide, w_tall,
                raw, frc, adj, res, slope_f32, slope_rows, slope_win, w1_ref, w2_ref, w1_other,
                w2_other, vs, hs, ss, load_inn, load_rest,
                x_send, x_recv, r_send, r_recv, h_send, h_recv, w_send, w_recv, s_send, s_recv,
                t_send, t_recv, above):
    fronts, chans, rows, win, half, band, lats, owners = dims
    pad = frc.shape[2]
    rims = rows + 4
    hid_rows = rows + 2
    far = fronts - 1
    grp = lax.axis_index("grp")
    lat = lax.axis_index("lat")
    tm = lax.axis_index("tm")
    core = lax.axis_index("chan")

    def dev(lat_no, tm_no, core_no):
        return (grp, lat_no, tm_no, core_no)

    partner = dev(lat, tm, 1 - core)
    opposite = dev(lat, 1 - tm, core)
    has_down = lat > 0
    has_up = lat < lats - 1
    first = (lat == 0) & (core == 0)
    final = (lat == lats - 1) & (core == 1)
    not_first = jnp.logical_not(first)
    not_final = jnp.logical_not(final)

    barrier = pltpu.get_barrier_semaphore()

    def greet(device):
        pl.semaphore_signal(barrier, inc=1, device_id=device, device_id_type=MESH)

    greet(opposite)

    @pl.when(has_up)
    def _():
        greet(dev(lat + 1, tm, 0))

        @pl.when(core == 1)
        def _():
            greet(dev(lat + 1, tm, 1))

        @pl.when(tm == 0)
        def _():
            greet(dev(lat + 1, 1, 0))

        @pl.when((tm == 1) & (core == 1))
        def _():
            greet(dev(lat + 1, 0, 0))
            greet(dev(lat + 1, 0, 1))

    greet(partner)
    below = has_down.astype(jnp.int32)

    def enter():
        pl.semaphore_wait(barrier, 2 + below * (2 - core + (1 - tm) + 2 * tm * (1 - core)))

        @pl.when(has_down & (core == 0))
        def _():
            for c in range(2):
                pl.semaphore_signal(above, inc=1, device_id=dev(lat - 1, tm, c), device_id_type=MESH)

        @pl.when(has_down & (core == 0) & (tm == 1))
        def _():
            for c in range(2):
                pl.semaphore_signal(above, inc=1, device_id=dev(lat - 1, 0, c), device_id_type=MESH)

    def wait_above():
        @pl.when(has_up)
        def _():
            pl.semaphore_wait(above, 2 - tm)

    def inn_copy(f):
        return pltpu.make_async_copy(inn_hbm.at[f], inn_ref.at[f], load_inn.at[f])

    loads = [
        pltpu.make_async_copy(slopes_hbm, slopes_ref, load_rest.at[0]),
        pltpu.make_async_copy(w_out_hbm, w_out_ref, load_rest.at[1]),
        pltpu.make_async_copy(w_in_hbm, w_in_ref, load_rest.at[2]),
    ]

    lane = lax.broadcasted_iota(jnp.int32, (1, win), 1)
    tiles = mask_ref.shape[0]
    width = win // tiles
    spread = jnp.zeros((1, win), F32)
    for k in range(tiles):
        spread = jnp.where(lane // width == k, mask_ref[k].astype(F32), spread)

    def load_raw(f):
        raw[...] = inn_ref[f].astype(F32).reshape(chans * rows, win)

    def forcing_row(r):
        return raw[pl.ds(r, chans, stride=rows), :] * spread

    def put_out(f, r, value):
        out_ref[pl.ds(f * (chans * rows) + r, chans, stride=rows), :] = value

    starts = (core * 2, (1 - core) * 2)

    def x_copy(k, f):
        part = adj.at[f, pl.ds(2 + starts[k], 2)]
        return pltpu.make_async_remote_copy(
            src_ref=part, dst_ref=part, send_sem=x_send.at[k, f], recv_sem=x_recv.at[k, f],
            device_id=opposite, device_id_type=MESH)

    def r_copy(k):
        part = res.at[pl.ds(2 * k, 2)]
        return pltpu.make_async_remote_copy(
            src_ref=part, dst_ref=part, send_sem=r_send.at[k], recv_sem=r_recv.at[k],
            device_id=opposite, device_id_type=MESH)

    spans = ((3 - 3 * core, 5), (5 * core, 3))

    def t_copy(k):
        part = slope_rows.at[pl.ds(*spans[k])]
        return pltpu.make_async_remote_copy(
            src_ref=part, dst_ref=part, send_sem=t_send.at[k], recv_sem=t_recv.at[k],
            device_id=opposite, device_id_type=MESH)

    def halo_down(f):
        return pltpu.make_async_remote_copy(
            src_ref=adj.at[f, pl.ds(2, 2)], dst_ref=adj.at[f, pl.ds(rims - 2, 2)],
            send_sem=h_send.at[0, f], recv_sem=h_recv.at[0, f],
            device_id=dev(lat - (1 - core), tm, 1 - core), device_id_type=MESH)

    def halo_up(f):
        return pltpu.make_async_remote_copy(
            src_ref=adj.at[f, pl.ds(rows, 2)], dst_ref=adj.at[f, pl.ds(0, 2)],
            send_sem=h_send.at[1, f], recv_sem=h_recv.at[1, f],
            device_id=dev(lat + core, tm, 1 - core), device_id_type=MESH)

    def pass_on(k, f):
        @pl.when(not_first & (core == k))
        def _():
            halo_down(f).start()

        @pl.when(not_final & (core == 1 - k))
        def _():
            halo_up(f).start()

    def halos_here(f):
        @pl.when(not_final)
        def _():
            halo_down(f).wait_recv()

        @pl.when(not_first)
        def _():
            halo_up(f).wait_recv()

    def halos_sent(f):
        @pl.when(not_first)
        def _():
            halo_down(f).wait_send()

        @pl.when(not_final)
        def _():
            halo_up(f).wait_send()

    w1_copy = pltpu.make_async_remote_copy(
        src_ref=w1_ref, dst_ref=w1_other, send_sem=w_send.at[0], recv_sem=w_recv.at[0],
        device_id=partner, device_id_type=MESH)
    w2_copy = pltpu.make_async_remote_copy(
        src_ref=w2_ref, dst_ref=w2_other, send_sem=w_send.at[1], recv_sem=w_recv.at[1],
        device_id=partner, device_id_type=MESH)
    own = hid_rows - 1
    mine_from = core * (rows - 1)
    partner_from = (1 - core) * (rows - 1)
    s_copy = pltpu.make_async_remote_copy(
        src_ref=slope_rows.at[pl.ds(partner_from, own)],
        dst_ref=slope_win.at[1, pl.ds(core, own)],
        send_sem=s_send.at[0], recv_sem=s_recv.at[0],
        device_id=partner, device_id_type=MESH)

    def s_down(to, k):
        return pltpu.make_async_remote_copy(
            src_ref=slope_rows.at[0], dst_ref=slope_win.at[1 - core, hid_rows - 1],
            send_sem=s_send.at[1 + k], recv_sem=s_recv.at[1 + (1 - core)],
            device_id=dev(lat - 1, to, 1), device_id_type=MESH)

    def s_up(to, k):
        return pltpu.make_async_remote_copy(
            src_ref=slope_rows.at[band - 1], dst_ref=slope_win.at[core, 0],
            send_sem=s_send.at[3 + k], recv_sem=s_recv.at[1 + core],
            device_id=dev(lat + 1, to, 0), device_id_type=MESH)

    def slope_down(act, to):
        @pl.when(has_down)
        def _():
            act(s_down(to, to))

    def slope_up(act, to):
        @pl.when(has_up)
        def _():
            act(s_up(to, to))

    def start(copy):
        copy.start()

    def slopes_here():
        s_copy.wait_recv()

        @pl.when(has_down & (core == 0))
        def _():
            s_up_recv(slope_win, slope_rows, s_send, s_recv, 0, partner)

        @pl.when(has_up & (core == 1))
        def _():
            s_up_recv(slope_win, slope_rows, s_send, s_recv, hid_rows - 1, partner)

    def own_slopes():
        slope_win[0, pl.ds(1 - core, own)] = slope_rows[pl.ds(mine_from, own)]

    def all_sent():
        w1_copy.wait_send()
        w2_copy.wait_send()
        s_copy.wait_send()

    def clear_rims():
        @pl.when(first)
        def _():
            slope_win[:, 0] = jnp.zeros((2, half, win), BF16)
            for f in range(fronts):
                adj[f, 0:2] = jnp.zeros((2, pad, win), BF16)

        @pl.when(final)
        def _():
            slope_win[:, hid_rows - 1] = jnp.zeros((2, half, win), BF16)
            for f in range(fronts):
                adj[f, rims - 2:rims] = jnp.zeros((2, pad, win), BF16)

    def prepare_weights():
        w_wide[...] = jnp.zeros_like(w_wide)
        w_tall[...] = jnp.zeros_like(w_tall)
        layer = layer_ref[0]
        loads[1].wait()
        for a in range(3):
            for b in range(3):
                w_wide[b, a * half:(a + 1) * half, 0:chans] = w_out_ref[layer, a, b].astype(F32)
        wide = w_wide[0] + pltpu.roll(w_wide[1], pad, 1) + pltpu.roll(w_wide[2], 2 * pad, 1)
        w1_ref[...] = wide.astype(BF16)
        loads[2].wait()
        for a in range(3):
            for b in range(3):
                w_tall[a, b * half:(b + 1) * half, 0:chans] = w_in_ref[layer, a, b].astype(F32)
        for a in range(3):
            w2_ref[a * pad:(a + 1) * pad, :] = w_tall[a].T[0:pad].astype(BF16)

    left_edge = lane == 0
    right_edge = lane == win - 1

    def shifts(x):
        ahead = jnp.where(right_edge, 0.0, pltpu.roll(x, win - 1, 1))
        behind = jnp.where(left_edge, 0.0, pltpu.roll(x, 1, 1))
        return ahead.astype(BF16), x.astype(BF16), behind.astype(BF16)

    def spread_rows(f, row_nos):
        for r in row_nos:
            for b, part in enumerate(shifts(adj[f, r].astype(F32))):
                vs[f % 2, b * pad:(b + 1) * pad, r * win:(r + 1) * win] = part

    def first_conv(f, low, high):
        columns = slice(low * win, high * win)
        for side, w_ref in enumerate((w1_ref, w1_other)):
            hs[f % 2, side, :, columns] = jnp.dot(
                w_ref[:, 0:3 * pad], vs[f % 2, :, columns], preferred_element_type=F32)

    def begin(f):
        spread_rows(f, range(2, rows + 2))
        first_conv(f, 2, rows + 2)

    def rim_conv(f):
        spread_rows(f, (0, 1, rims - 2, rims - 1))
        first_conv(f, 0, 2)
        first_conv(f, rims - 2, rims)

    def rest(f):
        for side in range(2):
            for p in range(hid_rows):
                grad = sum(hs[f % 2, side, a * half:(a + 1) * half, (p + 2 - a) * win:(p + 3 - a) * win]
                           for a in range(3))
                scaled = (slope_win[side, p].astype(F32) * grad).astype(BF16).astype(F32)
                for b, part in enumerate(shifts(scaled)):
                    ss[f % 2, side, b * half:(b + 1) * half, p * win:(p + 1) * win] = part
        g = (jnp.dot(w2_ref[...], ss[f % 2, 0], preferred_element_type=F32)
             + jnp.dot(w2_other[...], ss[f % 2, 1], preferred_element_type=F32))
        return [adj[f, r + 2].astype(F32)
                + sum(g[a * pad:(a + 1) * pad, (r + 2 - a) * win:(r + 3 - a) * win] for a in range(3))
                for r in range(rows)]

    @pl.when(tm == 1)
    def _():
        for f in range(fronts):
            inn_copy(f).start()
        for load in loads[1:]:
            load.start()
        clear_rims()
        if pad > chans:
            for f in range(fronts):
                for r in range(rows):
                    adj[f, r + 2, chans:pad, :] = jnp.zeros((pad - chans, win), BF16)

        def take(f):
            inn_copy(f).wait()
            load_raw(f)
            for r in range(rows):
                adj[f, r + 2, 0:chans, :] = forcing_row(r).astype(BF16)

        take(0)
        enter()
        x_copy(0, 0).start()

        @pl.when(core == 1)
        def _():
            x_copy(0, 0).wait_send()

        for f in range(1, far):
            take(f)
            x_copy(0, f).start()
        for f in range(far):
            x_copy(1, f).start()
        take(far)

        @pl.when(not_first)
        def _():
            halo_down(far).start()

        @pl.when(not_final & (core == 0))
        def _():
            halo_up(far).start()

        prepare_weights()
        w1_copy.start()
        w2_copy.start()
        wait_above()

        @pl.when(not_final & (core == 1))
        def _():
            halo_up(far).start()

        for f in range(fronts):
            for r in range(rows):
                put_out(f, r, adj[f, r + 2, 0:chans, :].astype(F32))

        w1_copy.wait_recv()
        begin(far)
        t_copy(0).wait_recv()
        s_copy.start()
        halos_here(far)
        rim_conv(far)
        w2_copy.wait_recv()
        t_copy(1).wait_recv()
        own_slopes()
        slopes_here()
        for r, value in enumerate(rest(far)):
            res[r] = value.astype(BF16)
            if r % 2 == 1:
                r_copy(r // 2).start()

        all_sent()
        halos_sent(far)
        @pl.when(core == 0)
        def _():
            x_copy(0, 0).wait_send()

        for k in range(2):
            for f in range(1 - k, far):
                x_copy(k, f).wait_send()
        for k in range(2):
            r_copy(k).wait_send()

    @pl.when(tm == 0)
    def _():
        for load in loads:
            load.start()
        for f in range(fronts):
            inn_copy(f).start()
        clear_rims()

        loads[0].wait()
        slope_f32[...] = slopes_ref[...].astype(F32)
        for r in range(band):
            slope_rows[r] = slope_f32[pl.ds(r, half, stride=band), :].astype(BF16)
        enter()
        slope_down(start, 1)
        for k in range(2):
            t_copy(k).start()
        slope_down(start, 0)
        s_copy.start()
        own_slopes()
        prepare_weights()
        wait_above()
        slope_up(start, 1)
        slope_up(start, 0)
        w1_copy.start()
        w2_copy.start()

        for f in range(fronts):
            inn_copy(f).wait()
            load_raw(f)
            for r in range(rows):
                frc[f, r, 0:chans, :] = forcing_row(r).astype(BF16)

        for f in range(far):
            x_copy(0, f).wait_recv()
            pass_on(0, f)

        w1_copy.wait_recv()
        w2_copy.wait_recv()
        slopes_here()

        def finish(f):
            halos_here(f)
            rim_conv(f)
            for r, value in enumerate(rest(f)):
                put_out(f, r, value[0:chans] + frc[f, r, 0:chans, :].astype(F32))

        for f in range(far):
            x_copy(1, f).wait_recv()
            pass_on(1, f)
            if f > 0:
                finish(f - 1)
            begin(f)
        finish(far - 1)

        for k in range(2):
            r_copy(k).wait_recv()
            for r in (2 * k, 2 * k + 1):
                put_out(far, r, res[r, 0:chans, :].astype(F32) + frc[far, r, 0:chans, :].astype(F32))

        all_sent()
        for f in range(far):
            halos_sent(f)
        for k in range(2):
            t_copy(k).wait_send()
            slope_down(lambda copy: copy.wait_send(), k)
            slope_up(lambda copy: copy.wait_send(), k)


def chain_kernel(dims, layer_ref, mask_ref, inn_hbm, slopes_hbm, w_in_hbm, w_out_hbm, out_ref,
           inn_ref, slopes_ref, w_in_ref, w_out_ref, w_wide, w_tall,
           raw, send_x, adj, slope_f32, slope_rows, slope_win, w1_ref, w2_ref, w1_other,
           w2_other, vs, hs, ss, load_inn, load_rest,
           x_send, x_recv, h_send, h_recv, w_send, w_recv, s_send, s_recv):
    fronts, chans, rows, win, half, band, lats, owners = dims
    pad = send_x.shape[2]
    rims = rows + 4
    hid_rows = rows + 2
    grp = lax.axis_index("grp")
    lat = lax.axis_index("lat")
    tm = lax.axis_index("tm")
    core = lax.axis_index("chan")
    last = owners - 1

    def dev(lat_no, tm_no, core_no):
        return (grp, lat_no, tm_no, core_no)

    barrier = pltpu.get_barrier_semaphore()

    def greet(device):
        pl.semaphore_signal(barrier, inc=1, device_id=device, device_id_type=MESH)

    def inn_copy(f):
        return pltpu.make_async_copy(inn_hbm.at[f], inn_ref.at[f], load_inn.at[f])

    for f in range(fronts):
        inn_copy(f).start()

    lane = lax.broadcasted_iota(jnp.int32, (1, win), 1)
    tiles = mask_ref.shape[0]
    width = win // tiles
    spread = jnp.zeros((1, win), F32)
    for k in range(tiles):
        spread = jnp.where(lane // width == k, mask_ref[k].astype(F32), spread)

    def load_raw(f):
        raw[...] = inn_ref[f].astype(F32).reshape(chans * rows, win)

    def forcing_row(r):
        return raw[pl.ds(r, chans, stride=rows), :] * spread

    def put_out(f, r, value):
        out_ref[pl.ds(f * (chans * rows) + r, chans, stride=rows), :] = value

    starts = (core * 2, (1 - core) * 2)

    def x_copy(k, f):
        return pltpu.make_async_remote_copy(
            src_ref=send_x.at[f, pl.ds(starts[k], 2)], dst_ref=adj.at[f, pl.ds(2 + starts[k], 2)],
            send_sem=x_send.at[k, f], recv_sem=x_recv.at[k, f],
            device_id=dev(lat, lax.rem(tm + owners - 1, owners), core), device_id_type=MESH)

    def put_send(f, r, value):
        send_x[f, r, 0:chans, :] = value.astype(BF16)

    def clear_send():
        if pad > chans:
            for f in range(fronts):
                for r in range(rows):
                    send_x[f, r, chans:pad, :] = jnp.zeros((pad - chans, win), BF16)

    @pl.when(tm == last)
    def _():
        greet(dev(lat, tm - 1, core))
        clear_send()

        for f in range(fronts):
            inn_copy(f).wait()
            load_raw(f)
            for r in range(rows):
                value = forcing_row(r)
                put_out(f, r, value)
                put_send(f, r, value)
            if f == 0:
                pl.semaphore_wait(barrier, 1)
            x_copy(0, f).start()

        for f in range(fronts):
            x_copy(1, f).start()
        for f in range(fronts):
            for k in range(2):
                x_copy(k, f).wait_send()

    @pl.when(tm < last)
    def _():
        has_down = lat > 0
        has_up = lat < lats - 1
        greet(dev(lat, tm + 1, core))
        greet(dev(lat, tm, 1 - core))

        @pl.when(has_down)
        def _():
            greet(dev(lat - 1, tm, 0))
            greet(dev(lat - 1, tm, 1))

        @pl.when(has_up)
        def _():
            greet(dev(lat + 1, tm, 0))
            greet(dev(lat + 1, tm, 1))

        greeted = 2 + 2 * has_down.astype(jnp.int32) + 2 * has_up.astype(jnp.int32)
        if owners > 2:
            @pl.when(tm > 0)
            def _():
                greet(dev(lat, tm - 1, core))
            greeted = greeted + (tm > 0).astype(jnp.int32)
        clear_send()

        loads = [
            pltpu.make_async_copy(slopes_hbm, slopes_ref, load_rest.at[0]),
            pltpu.make_async_copy(w_out_hbm, w_out_ref, load_rest.at[1]),
            pltpu.make_async_copy(w_in_hbm, w_in_ref, load_rest.at[2]),
        ]
        for load in loads:
            load.start()
        w_wide[...] = jnp.zeros_like(w_wide)
        w_tall[...] = jnp.zeros_like(w_tall)

        loads[0].wait()
        slope_f32[...] = slopes_ref[...].astype(F32)
        for r in range(band):
            slope_rows[r] = slope_f32[pl.ds(r, half, stride=band), :].astype(BF16)

        first = (lat == 0) & (core == 0)
        final = (lat == lats - 1) & (core == 1)

        @pl.when(first)
        def _():
            slope_win[:, 0] = jnp.zeros((2, half, win), BF16)
            for f in range(fronts):
                adj[f, 0:2] = jnp.zeros((2, pad, win), BF16)

        @pl.when(final)
        def _():
            slope_win[:, hid_rows - 1] = jnp.zeros((2, half, win), BF16)
            for f in range(fronts):
                adj[f, rims - 2:rims] = jnp.zeros((2, pad, win), BF16)

        layer = layer_ref[tm]
        loads[1].wait()
        for a in range(3):
            for b in range(3):
                w_wide[b, a * half:(a + 1) * half, 0:chans] = w_out_ref[layer, a, b].astype(F32)
        wide = w_wide[0] + pltpu.roll(w_wide[1], pad, 1) + pltpu.roll(w_wide[2], 2 * pad, 1)
        w1_ref[...] = wide.astype(BF16)
        loads[2].wait()
        for a in range(3):
            for b in range(3):
                w_tall[a, b * half:(b + 1) * half, 0:chans] = w_in_ref[layer, a, b].astype(F32)
        for a in range(3):
            w2_ref[a * pad:(a + 1) * pad, :] = w_tall[a].T[0:pad].astype(BF16)

        pl.semaphore_wait(barrier, greeted)

        partner = dev(lat, tm, 1 - core)
        w1_copy = pltpu.make_async_remote_copy(
            src_ref=w1_ref, dst_ref=w1_other, send_sem=w_send.at[0], recv_sem=w_recv.at[0],
            device_id=partner, device_id_type=MESH)
        w2_copy = pltpu.make_async_remote_copy(
            src_ref=w2_ref, dst_ref=w2_other, send_sem=w_send.at[1], recv_sem=w_recv.at[1],
            device_id=partner, device_id_type=MESH)
        own = hid_rows - 1
        mine_from = core * (rows - 1)
        partner_from = (1 - core) * (rows - 1)
        s_copy = pltpu.make_async_remote_copy(
            src_ref=slope_rows.at[pl.ds(partner_from, own)],
            dst_ref=slope_win.at[1, pl.ds(core, own)],
            send_sem=s_send.at[0], recv_sem=s_recv.at[0],
            device_id=partner, device_id_type=MESH)
        s_down = pltpu.make_async_remote_copy(
            src_ref=slope_rows.at[0], dst_ref=slope_win.at[1 - core, hid_rows - 1],
            send_sem=s_send.at[1], recv_sem=s_recv.at[1 + (1 - core)],
            device_id=dev(lat - 1, tm, 1), device_id_type=MESH)
        s_up = pltpu.make_async_remote_copy(
            src_ref=slope_rows.at[band - 1], dst_ref=slope_win.at[core, 0],
            send_sem=s_send.at[2], recv_sem=s_recv.at[1 + core],
            device_id=dev(lat + 1, tm, 0), device_id_type=MESH)

        w1_copy.start()
        s_copy.start()
        w2_copy.start()

        @pl.when(has_down)
        def _():
            s_down.start()

        @pl.when(has_up)
        def _():
            s_up.start()

        slope_win[0, pl.ds(1 - core, own)] = slope_rows[pl.ds(mine_from, own)]

        not_first = jnp.logical_not(first)
        not_final = jnp.logical_not(final)

        def halo_down(f):
            return pltpu.make_async_remote_copy(
                src_ref=adj.at[f, pl.ds(2, 2)], dst_ref=adj.at[f, pl.ds(rims - 2, 2)],
                send_sem=h_send.at[0, f], recv_sem=h_recv.at[0, f],
                device_id=dev(lat - (1 - core), tm, 1 - core), device_id_type=MESH)

        def halo_up(f):
            return pltpu.make_async_remote_copy(
                src_ref=adj.at[f, pl.ds(rows, 2)], dst_ref=adj.at[f, pl.ds(0, 2)],
                send_sem=h_send.at[1, f], recv_sem=h_recv.at[1, f],
                device_id=dev(lat + core, tm, 1 - core), device_id_type=MESH)

        def pass_on(k, f):
            x_copy(k, f).wait_recv()

            @pl.when(not_first & (core == k))
            def _():
                halo_down(f).start()

            @pl.when(not_final & (core == 1 - k))
            def _():
                halo_up(f).start()

        left_edge = lane == 0
        right_edge = lane == win - 1

        def shifts(x):
            ahead = jnp.where(right_edge, 0.0, pltpu.roll(x, win - 1, 1))
            behind = jnp.where(left_edge, 0.0, pltpu.roll(x, 1, 1))
            return ahead.astype(BF16), x.astype(BF16), behind.astype(BF16)

        def spread_rows(f, row_nos):
            for r in row_nos:
                for b, part in enumerate(shifts(adj[f, r].astype(F32))):
                    vs[f % 2, b * pad:(b + 1) * pad, r * win:(r + 1) * win] = part

        def first_conv(f, low, high):
            columns = slice(low * win, high * win)
            for side, w_ref in enumerate((w1_ref, w1_other)):
                hs[f % 2, side, :, columns] = jnp.dot(
                    w_ref[:, 0:3 * pad], vs[f % 2, :, columns], preferred_element_type=F32)

        def compute(f):
            spread_rows(f, (0, 1, rims - 2, rims - 1))
            first_conv(f, 0, 2)
            first_conv(f, rims - 2, rims)
            for side in range(2):
                for p in range(hid_rows):
                    grad = sum(hs[f % 2, side, a * half:(a + 1) * half, (p + 2 - a) * win:(p + 3 - a) * win]
                               for a in range(3))
                    scaled = (slope_win[side, p].astype(F32) * grad).astype(BF16).astype(F32)
                    for b, part in enumerate(shifts(scaled)):
                        ss[f % 2, side, b * half:(b + 1) * half, p * win:(p + 1) * win] = part
            g = (jnp.dot(w2_ref[...], ss[f % 2, 0], preferred_element_type=F32)
                 + jnp.dot(w2_other[...], ss[f % 2, 1], preferred_element_type=F32))
            for r in range(rows):
                total = sum(g[a * pad:(a + 1) * pad, (r + 2 - a) * win:(r + 3 - a) * win]
                            for a in range(3))
                value = adj[f, r + 2].astype(F32) + total + send_x[f, r].astype(F32)
                value = value[0:chans]
                put_out(f, r, value)
                if owners > 2:
                    put_send(f, r, value)

        def finish(pair):
            for f in pair:
                @pl.when(not_final)
                def _():
                    halo_down(f).wait_recv()

                @pl.when(not_first)
                def _():
                    halo_up(f).wait_recv()

            for f in pair:
                compute(f)
            if owners > 2:
                @pl.when(tm > 0)
                def _():
                    for f in pair:
                        for k in range(2):
                            x_copy(k, f).start()

        for f in range(fronts):
            inn_copy(f).wait()
            load_raw(f)
            for r in range(rows):
                put_send(f, r, forcing_row(r))

        def begin(f):
            spread_rows(f, range(2, rows + 2))
            first_conv(f, 2, rows + 2)

        w1_copy.wait_recv()
        w2_copy.wait_recv()
        s_copy.wait_recv()

        @pl.when(has_down & (core == 0))
        def _():
            s_up_recv(slope_win, slope_rows, s_send, s_recv, 0, dev(lat, tm, 1 - core))

        @pl.when(has_up & (core == 1))
        def _():
            s_up_recv(slope_win, slope_rows, s_send, s_recv, hid_rows - 1, dev(lat, tm, 1 - core))

        @pl.loop(0, fronts)
        def _(f):
            pass_on(0, f)

        waiting = []
        for f in range(fronts):
            pass_on(1, f)
            if len(waiting) == 1:
                finish(waiting)
                waiting = []
            begin(f)
            waiting.append(f)
        finish(waiting)

        w1_copy.wait_send()
        w2_copy.wait_send()
        s_copy.wait_send()

        @pl.when(has_down)
        def _():
            s_down.wait_send()

        @pl.when(has_up)
        def _():
            s_up.wait_send()

        @pl.loop(0, fronts)
        def _(f):
            @pl.when(not_first)
            def _():
                halo_down(f).wait_send()

            @pl.when(not_final)
            def _():
                halo_up(f).wait_send()

            if owners > 2:
                @pl.when(tm > 0)
                def _():
                    for k in range(2):
                        x_copy(k, f).wait_send()


def s_up_recv(slope_win, slope_rows, s_send, s_recv, row, device):
    for side in range(2):
        pltpu.make_async_remote_copy(
            src_ref=slope_rows.at[0], dst_ref=slope_win.at[side, row],
            send_sem=s_send.at[1], recv_sem=s_recv.at[1 + side],
            device_id=device, device_id_type=MESH).wait_recv()


def in_hbm(array):
    return pltpu.with_memory_space_constraint(array, pltpu.HBM)


def per_device(mesh, innovations, obs_mask, slopes, layer_of, weight_in, weight_out):
    fronts, secs, chans, rows, win = innovations.shape
    _, half, band, _ = slopes.shape
    owners = mesh.shape["tm"]
    lats = mesh.shape["lat"]
    assert secs == 1 and band == 2 * rows and rows == 4 and owners > 1
    pair = owners == 2 and fronts > 1
    pad = round_up(chans, 16)
    rims, hid_rows = rows + 4, rows + 2

    layers = weight_in.shape[0]
    wide = round_up(3 * pad, 128)

    smem = pl.BlockSpec(memory_space=pltpu.SMEM)
    hbm = pl.BlockSpec(memory_space=pltpu.HBM)
    vmem = pl.BlockSpec(memory_space=pltpu.VMEM)
    out = pl.pallas_call(
        functools.partial(pair_kernel if pair else chain_kernel, (fronts, chans, rows, win, half, band, lats, owners)),
        out_shape=pltpu.VMEM((fronts * chans * rows, win), F32),
        in_specs=[smem, smem, hbm, hbm, hbm, hbm],
        out_specs=vmem,
        scratch_shapes=[
            pltpu.VMEM((fronts, chans, rows, win), BF16),
            pltpu.VMEM((half * band, win), BF16),
            pltpu.VMEM((layers, 3, 3, half, chans), BF16),
            pltpu.VMEM((layers, 3, 3, half, chans), BF16),
            pltpu.VMEM((3, 3 * half, wide), F32),
            pltpu.VMEM((3, 3 * half, 128), F32),
            pltpu.VMEM((chans * rows, win), F32),
            pltpu.VMEM((fronts, rows, pad, win), BF16),
            pltpu.VMEM((fronts, rims, pad, win), BF16),
            *([pltpu.VMEM((rows, pad, win), BF16)] if pair else []),
            pltpu.VMEM((half * band, win), F32),
            pltpu.VMEM((band, half, win), BF16),
            pltpu.VMEM((2, hid_rows, half, win), BF16),
            pltpu.VMEM((3 * half, wide), BF16),
            pltpu.VMEM((3 * pad, 3 * half), BF16),
            pltpu.VMEM((3 * half, wide), BF16),
            pltpu.VMEM((3 * pad, 3 * half), BF16),
            pltpu.VMEM((2, 3 * pad, rims * win), BF16),
            pltpu.VMEM((2, 2, 3 * half, rims * win), F32),
            pltpu.VMEM((2, 2, 3 * half, hid_rows * win), BF16),
            pltpu.SemaphoreType.DMA((fronts,)),
            pltpu.SemaphoreType.DMA((3,)),
            pltpu.SemaphoreType.DMA((2, fronts)),
            pltpu.SemaphoreType.DMA((2, fronts)),
            *([pltpu.SemaphoreType.DMA((2,))] * 2 if pair else []),
            pltpu.SemaphoreType.DMA((2, fronts)),
            pltpu.SemaphoreType.DMA((2, fronts)),
            pltpu.SemaphoreType.DMA((2,)),
            pltpu.SemaphoreType.DMA((2,)),
            pltpu.SemaphoreType.DMA((5,)),
            pltpu.SemaphoreType.DMA((3,)),
            *([pltpu.SemaphoreType.DMA((2,))] * 2 + [pltpu.SemaphoreType.REGULAR] if pair else []),
        ],
        compiler_params=pltpu.CompilerParams(
            collective_id=0, has_side_effects=True, vmem_limit_bytes=32 * 1024 * 1024
        ),
    )(
        in_hbm(layer_of),
        in_hbm(obs_mask.reshape(obs_mask.shape[-1])),
        in_hbm(innovations.reshape(fronts, chans, rows, win)),
        in_hbm(slopes.reshape(half * band, win)),
        in_hbm(weight_in.swapaxes(3, 4)),
        in_hbm(weight_out),
    )
    return out.reshape(innovations.shape)


def solution(mesh):
    return jax.shard_map(
        functools.partial(per_device, mesh),
        mesh=mesh,
        in_specs=(
            P(None, ("grp", "tm"), None, ("lat", "chan"), None),
            P(("grp", "tm"), ("lat", "chan"), None),
            P(("grp", "tm"), "chan", "lat", None),
            P(),
            P(None, None, None, None, "chan"),
            P(None, None, None, "chan", None),
        ),
        out_specs=P(None, ("grp", "tm"), None, ("lat", "chan"), None),
        check_vma=False,
    )
```

```python
import functools

import jax
import jax.numpy as jnp
from jax import lax
from jax.experimental import pallas as pl
from jax.experimental.pallas import tpu as pltpu
from jax.sharding import PartitionSpec as P

MESH = pl.DeviceIdType.MESH
BF16 = jnp.bfloat16
F32 = jnp.float32


def round_up(n, m):
    return -(-n // m) * m


def pair_kernel(dims, layer_ref, mask_ref, inn_hbm, slopes_hbm, w_in_hbm, w_out_hbm, out_ref,
                inn_ref, slopes_ref, w_in_ref, w_out_ref, w_wide, w_tall,
                raw, frc, adj, res, slope_f32, slope_rows, slope_win, w1_ref, w2_ref, vs, hs, ss, load_inn, load_rest,
                x_send, x_recv, r_send, r_recv, h_send, h_recv, w_send, w_recv, s_send, s_recv,
                t_send, t_recv, above):
    fronts, chans, rows, win, half, band, lats, owners = dims
    pad = frc.shape[2]
    rims = rows + 4
    hid_rows = rows + 2
    far = fronts - 1
    deep = w2_ref.shape[1] // 2
    grp = lax.axis_index("grp")
    lat = lax.axis_index("lat")
    tm = lax.axis_index("tm")
    core = lax.axis_index("chan")

    def dev(lat_no, tm_no, core_no):
        return (grp, lat_no, tm_no, core_no)

    partner = dev(lat, tm, 1 - core)
    opposite = dev(lat, 1 - tm, core)
    has_down = lat > 0
    has_up = lat < lats - 1
    first = (lat == 0) & (core == 0)
    final = (lat == lats - 1) & (core == 1)
    not_first = jnp.logical_not(first)
    not_final = jnp.logical_not(final)

    barrier = pltpu.get_barrier_semaphore()

    def greet(device):
        pl.semaphore_signal(barrier, inc=1, device_id=device, device_id_type=MESH)

    greet(opposite)

    @pl.when(has_up)
    def _():
        greet(dev(lat + 1, tm, 0))

        @pl.when(core == 1)
        def _():
            greet(dev(lat + 1, tm, 1))

        @pl.when(tm == 0)
        def _():
            greet(dev(lat + 1, 1, 0))

        @pl.when((tm == 1) & (core == 1))
        def _():
            greet(dev(lat + 1, 0, 0))
            greet(dev(lat + 1, 0, 1))

    greet(partner)
    below = has_down.astype(jnp.int32)

    def enter():
        pl.semaphore_wait(barrier, 2 + below * (2 - core + (1 - tm) + 2 * tm * (1 - core)))

        @pl.when(has_down & (core == 0))
        def _():
            for c in range(2):
                pl.semaphore_signal(above, inc=1, device_id=dev(lat - 1, tm, c), device_id_type=MESH)

        @pl.when(has_down & (core == 0) & (tm == 1))
        def _():
            for c in range(2):
                pl.semaphore_signal(above, inc=1, device_id=dev(lat - 1, 0, c), device_id_type=MESH)

    def wait_above():
        @pl.when(has_up)
        def _():
            pl.semaphore_wait(above, 2 - tm)

    def inn_copy(f):
        return pltpu.make_async_copy(inn_hbm.at[f], inn_ref.at[f], load_inn.at[f])

    loads = [
        pltpu.make_async_copy(slopes_hbm, slopes_ref, load_rest.at[0]),
        pltpu.make_async_copy(w_out_hbm, w_out_ref, load_rest.at[1]),
        pltpu.make_async_copy(w_in_hbm, w_in_ref, load_rest.at[2]),
    ]

    lane = lax.broadcasted_iota(jnp.int32, (1, win), 1)
    tiles = mask_ref.shape[0]
    width = win // tiles
    spread = jnp.zeros((1, win), F32)
    for k in range(tiles):
        spread = jnp.where(lane // width == k, mask_ref[k].astype(F32), spread)

    def load_raw(f):
        raw[...] = inn_ref[f].astype(F32).reshape(chans * rows, win)

    def forcing_row(r):
        return raw[pl.ds(r, chans, stride=rows), :] * spread

    def put_out(f, r, value):
        out_ref[pl.ds(f * (chans * rows) + r, chans, stride=rows), :] = value

    starts = (core * 2, (1 - core) * 2)

    def x_copy(k, f):
        part = adj.at[f, pl.ds(2 + starts[k], 2)]
        return pltpu.make_async_remote_copy(
            src_ref=part, dst_ref=part, send_sem=x_send.at[k, f], recv_sem=x_recv.at[k, f],
            device_id=opposite, device_id_type=MESH)

    def r_copy(k):
        part = res.at[pl.ds(2 * k, 2)]
        return pltpu.make_async_remote_copy(
            src_ref=part, dst_ref=part, send_sem=r_send.at[k], recv_sem=r_recv.at[k],
            device_id=opposite, device_id_type=MESH)

    spans = ((3 - 3 * core, 5), (5 * core, 3))

    def t_copy(k):
        part = slope_rows.at[pl.ds(*spans[k])]
        return pltpu.make_async_remote_copy(
            src_ref=part, dst_ref=part, send_sem=t_send.at[k], recv_sem=t_recv.at[k],
            device_id=opposite, device_id_type=MESH)

    def halo_down(f):
        return pltpu.make_async_remote_copy(
            src_ref=adj.at[f, pl.ds(2, 2)], dst_ref=adj.at[f, pl.ds(rims - 2, 2)],
            send_sem=h_send.at[0, f], recv_sem=h_recv.at[0, f],
            device_id=dev(lat - (1 - core), tm, 1 - core), device_id_type=MESH)

    def halo_up(f):
        return pltpu.make_async_remote_copy(
            src_ref=adj.at[f, pl.ds(rows, 2)], dst_ref=adj.at[f, pl.ds(0, 2)],
            send_sem=h_send.at[1, f], recv_sem=h_recv.at[1, f],
            device_id=dev(lat + core, tm, 1 - core), device_id_type=MESH)

    def pass_on(k, f):
        @pl.when(not_first & (core == k))
        def _():
            halo_down(f).start()

        @pl.when(not_final & (core == 1 - k))
        def _():
            halo_up(f).start()

    def halos_here(f):
        @pl.when(not_final)
        def _():
            halo_down(f).wait_recv()

        @pl.when(not_first)
        def _():
            halo_up(f).wait_recv()

    def halos_sent(f):
        @pl.when(not_first)
        def _():
            halo_down(f).wait_send()

        @pl.when(not_final)
        def _():
            halo_up(f).wait_send()

    w1_copy = pltpu.make_async_remote_copy(
        src_ref=w1_ref.at[0], dst_ref=w1_ref.at[1], send_sem=w_send.at[0], recv_sem=w_recv.at[0],
        device_id=partner, device_id_type=MESH)
    w2_copy = pltpu.make_async_remote_copy(
        src_ref=w2_ref.at[:, pl.ds(0, deep)], dst_ref=w2_ref.at[:, pl.ds(deep, deep)],
        send_sem=w_send.at[1], recv_sem=w_recv.at[1],
        device_id=partner, device_id_type=MESH)
    own = hid_rows - 1
    mine_from = core * (rows - 1)
    partner_from = (1 - core) * (rows - 1)
    s_copy = pltpu.make_async_remote_copy(
        src_ref=slope_rows.at[pl.ds(partner_from, own)],
        dst_ref=slope_win.at[1, pl.ds(core, own)],
        send_sem=s_send.at[0], recv_sem=s_recv.at[0],
        device_id=partner, device_id_type=MESH)

    def s_down(to, k):
        return pltpu.make_async_remote_copy(
            src_ref=slope_rows.at[0], dst_ref=slope_win.at[1 - core, hid_rows - 1],
            send_sem=s_send.at[1 + k], recv_sem=s_recv.at[1 + (1 - core)],
            device_id=dev(lat - 1, to, 1), device_id_type=MESH)

    def s_up(to, k):
        return pltpu.make_async_remote_copy(
            src_ref=slope_rows.at[band - 1], dst_ref=slope_win.at[core, 0],
            send_sem=s_send.at[3 + k], recv_sem=s_recv.at[1 + core],
            device_id=dev(lat + 1, to, 0), device_id_type=MESH)

    def slope_down(act, to):
        @pl.when(has_down)
        def _():
            act(s_down(to, to))

    def slope_up(act, to):
        @pl.when(has_up)
        def _():
            act(s_up(to, to))

    def start(copy):
        copy.start()

    def slopes_here():
        s_copy.wait_recv()

        @pl.when(has_down & (core == 0))
        def _():
            s_up_recv(slope_win, slope_rows, s_send, s_recv, 0, partner)

        @pl.when(has_up & (core == 1))
        def _():
            s_up_recv(slope_win, slope_rows, s_send, s_recv, hid_rows - 1, partner)

    def own_slopes():
        slope_win[0, pl.ds(1 - core, own)] = slope_rows[pl.ds(mine_from, own)]

    def all_sent():
        w1_copy.wait_send()
        w2_copy.wait_send()
        s_copy.wait_send()

    def clear_rims():
        @pl.when(first)
        def _():
            slope_win[:, 0] = jnp.zeros((2, half, win), BF16)
            for f in range(fronts):
                adj[f, 0:2] = jnp.zeros((2, pad, win), BF16)

        @pl.when(final)
        def _():
            slope_win[:, hid_rows - 1] = jnp.zeros((2, half, win), BF16)
            for f in range(fronts):
                adj[f, rims - 2:rims] = jnp.zeros((2, pad, win), BF16)

    def prepare_weights():
        w_wide[...] = jnp.zeros_like(w_wide)
        w_tall[...] = jnp.zeros_like(w_tall)
        if deep > 3 * half:
            w2_ref[:, 3 * half:deep] = jnp.zeros((3 * pad, deep - 3 * half), BF16)
            for side in range(2):
                ss[:, side * deep + 3 * half:(side + 1) * deep] = jnp.zeros(
                    (2, deep - 3 * half, hid_rows * win), BF16)
        layer = layer_ref[0]
        loads[1].wait()
        for a in range(3):
            for b in range(3):
                w_wide[b, a * half:(a + 1) * half, 0:chans] = w_out_ref[layer, a, b].astype(F32)
        wide = w_wide[0] + pltpu.roll(w_wide[1], pad, 1) + pltpu.roll(w_wide[2], 2 * pad, 1)
        w1_ref[0] = wide.astype(BF16)
        loads[2].wait()
        for a in range(3):
            for b in range(3):
                w_tall[a, b * half:(b + 1) * half, 0:chans] = w_in_ref[layer, a, b].astype(F32)
        for a in range(3):
            w2_ref[a * pad:(a + 1) * pad, 0:3 * half] = w_tall[a].T[0:pad].astype(BF16)

    left_edge = lane == 0
    right_edge = lane == win - 1

    def shifts(x):
        ahead = jnp.where(right_edge, 0.0, pltpu.roll(x, win - 1, 1))
        behind = jnp.where(left_edge, 0.0, pltpu.roll(x, 1, 1))
        return ahead.astype(BF16), x.astype(BF16), behind.astype(BF16)

    place = [*range(rows, rows + 2), *range(rows), *range(rows + 2, rims)]

    def columns(row):
        return slice(place[row] * win, (place[row] + 1) * win)

    def spread_rows(f, row_nos):
        for r in row_nos:
            for b, part in enumerate(shifts(adj[f, r].astype(F32))):
                vs[f % 2, b * pad:(b + 1) * pad, columns(r)] = part

    def first_conv(f, low, high):
        part = slice(low * win, high * win)
        both = w1_ref[...].reshape(6 * half, w1_ref.shape[2])
        hs[f % 2, :, part] = jnp.dot(both[:, 0:3 * pad], vs[f % 2, :, part], preferred_element_type=F32)

    def begin(f):
        spread_rows(f, range(2, rows + 2))
        first_conv(f, 0, rows)

    def rim_conv(f):
        spread_rows(f, (0, 1, rims - 2, rims - 1))
        first_conv(f, rows, rims)

    def rest(f):
        for side in range(2):
            for p in range(hid_rows):
                grad = sum(hs[f % 2, (3 * side + a) * half:(3 * side + a + 1) * half, columns(p + 2 - a)]
                           for a in range(3))
                scaled = (slope_win[side, p].astype(F32) * grad).astype(BF16).astype(F32)
                for b, part in enumerate(shifts(scaled)):
                    low = side * deep + b * half
                    ss[f % 2, low:low + half, p * win:(p + 1) * win] = part
        totals = [adj[f, r + 2].astype(F32) for r in range(rows)]
        for p in range(0, hid_rows, 2):
            offsets = [a for a in range(3) if p - 1 + a >= 0 and p - 2 + a < rows]
            first, count = offsets[0], len(offsets)
            g = jnp.dot(w2_ref[first * pad:(first + count) * pad, :], ss[f % 2, :, p * win:(p + 2) * win],
                        preferred_element_type=F32)
            for a in offsets:
                for step in range(2):
                    r = p + step - 2 + a
                    if 0 <= r < rows:
                        totals[r] = totals[r] + g[(a - first) * pad:(a - first + 1) * pad, step * win:(step + 1) * win]
        return totals

    @pl.when(tm == 1)
    def _():
        for f in range(fronts):
            inn_copy(f).start()
        for load in loads[1:]:
            load.start()
        clear_rims()
        if pad > chans:
            for f in range(fronts):
                for r in range(rows):
                    adj[f, r + 2, chans:pad, :] = jnp.zeros((pad - chans, win), BF16)

        def take(f):
            inn_copy(f).wait()
            load_raw(f)
            for r in range(rows):
                adj[f, r + 2, 0:chans, :] = forcing_row(r).astype(BF16)

        take(0)
        enter()
        x_copy(0, 0).start()

        @pl.when(core == 1)
        def _():
            x_copy(0, 0).wait_send()

        for f in range(1, far):
            take(f)
            x_copy(0, f).start()
        for f in range(far):
            x_copy(1, f).start()
        take(far)

        @pl.when(not_first)
        def _():
            halo_down(far).start()

        @pl.when(not_final & (core == 0))
        def _():
            halo_up(far).start()

        prepare_weights()
        w1_copy.start()
        w2_copy.start()
        wait_above()

        @pl.when(not_final & (core == 1))
        def _():
            halo_up(far).start()

        for f in range(fronts):
            for r in range(rows):
                put_out(f, r, adj[f, r + 2, 0:chans, :].astype(F32))

        w1_copy.wait_recv()
        begin(far)
        t_copy(0).wait_recv()
        s_copy.start()
        halos_here(far)
        rim_conv(far)
        w2_copy.wait_recv()
        t_copy(1).wait_recv()
        own_slopes()
        slopes_here()
        for r, value in enumerate(rest(far)):
            res[r] = value.astype(BF16)
            if r % 2 == 1:
                r_copy(r // 2).start()

        all_sent()
        halos_sent(far)
        @pl.when(core == 0)
        def _():
            x_copy(0, 0).wait_send()

        for k in range(2):
            for f in range(1 - k, far):
                x_copy(k, f).wait_send()
        for k in range(2):
            r_copy(k).wait_send()

    @pl.when(tm == 0)
    def _():
        for load in loads:
            load.start()
        for f in range(fronts):
            inn_copy(f).start()
        clear_rims()

        loads[0].wait()
        slope_f32[...] = slopes_ref[...].astype(F32)
        for r in range(band):
            slope_rows[r] = slope_f32[pl.ds(r, half, stride=band), :].astype(BF16)
        enter()
        slope_down(start, 1)
        for k in range(2):
            t_copy(k).start()
        slope_down(start, 0)
        s_copy.start()
        own_slopes()
        prepare_weights()
        wait_above()
        slope_up(start, 1)
        slope_up(start, 0)
        w1_copy.start()
        w2_copy.start()

        for f in range(fronts):
            inn_copy(f).wait()
            load_raw(f)
            for r in range(rows):
                frc[f, r, 0:chans, :] = forcing_row(r).astype(BF16)

        for f in range(far):
            x_copy(0, f).wait_recv()
            pass_on(0, f)

        w1_copy.wait_recv()
        w2_copy.wait_recv()
        slopes_here()

        def finish(f):
            halos_here(f)
            rim_conv(f)
            for r, value in enumerate(rest(f)):
                put_out(f, r, value[0:chans] + frc[f, r, 0:chans, :].astype(F32))

        for f in range(far):
            x_copy(1, f).wait_recv()
            pass_on(1, f)
            if f > 0:
                finish(f - 1)
            begin(f)
        finish(far - 1)

        for k in range(2):
            r_copy(k).wait_recv()
            for r in (2 * k, 2 * k + 1):
                put_out(far, r, res[r, 0:chans, :].astype(F32) + frc[far, r, 0:chans, :].astype(F32))

        all_sent()
        for f in range(far):
            halos_sent(f)
        for k in range(2):
            t_copy(k).wait_send()
            slope_down(lambda copy: copy.wait_send(), k)
            slope_up(lambda copy: copy.wait_send(), k)


def chain_kernel(dims, layer_ref, mask_ref, inn_hbm, slopes_hbm, w_in_hbm, w_out_hbm, out_ref,
           inn_ref, slopes_ref, w_in_ref, w_out_ref, w_wide, w_tall,
           raw, send_x, adj, slope_f32, slope_rows, slope_win, w1_ref, w2_ref, w1_other,
           w2_other, vs, hs, ss, load_inn, load_rest,
           x_send, x_recv, h_send, h_recv, w_send, w_recv, s_send, s_recv):
    fronts, chans, rows, win, half, band, lats, owners = dims
    pad = send_x.shape[2]
    rims = rows + 4
    hid_rows = rows + 2
    grp = lax.axis_index("grp")
    lat = lax.axis_index("lat")
    tm = lax.axis_index("tm")
    core = lax.axis_index("chan")
    last = owners - 1

    def dev(lat_no, tm_no, core_no):
        return (grp, lat_no, tm_no, core_no)

    barrier = pltpu.get_barrier_semaphore()

    def greet(device):
        pl.semaphore_signal(barrier, inc=1, device_id=device, device_id_type=MESH)

    def inn_copy(f):
        return pltpu.make_async_copy(inn_hbm.at[f], inn_ref.at[f], load_inn.at[f])

    for f in range(fronts):
        inn_copy(f).start()

    lane = lax.broadcasted_iota(jnp.int32, (1, win), 1)
    tiles = mask_ref.shape[0]
    width = win // tiles
    spread = jnp.zeros((1, win), F32)
    for k in range(tiles):
        spread = jnp.where(lane // width == k, mask_ref[k].astype(F32), spread)

    def load_raw(f):
        raw[...] = inn_ref[f].astype(F32).reshape(chans * rows, win)

    def forcing_row(r):
        return raw[pl.ds(r, chans, stride=rows), :] * spread

    def put_out(f, r, value):
        out_ref[pl.ds(f * (chans * rows) + r, chans, stride=rows), :] = value

    starts = (core * 2, (1 - core) * 2)

    def x_copy(k, f):
        return pltpu.make_async_remote_copy(
            src_ref=send_x.at[f, pl.ds(starts[k], 2)], dst_ref=adj.at[f, pl.ds(2 + starts[k], 2)],
            send_sem=x_send.at[k, f], recv_sem=x_recv.at[k, f],
            device_id=dev(lat, lax.rem(tm + owners - 1, owners), core), device_id_type=MESH)

    def put_send(f, r, value):
        send_x[f, r, 0:chans, :] = value.astype(BF16)

    def clear_send():
        if pad > chans:
            for f in range(fronts):
                for r in range(rows):
                    send_x[f, r, chans:pad, :] = jnp.zeros((pad - chans, win), BF16)

    @pl.when(tm == last)
    def _():
        greet(dev(lat, tm - 1, core))
        clear_send()

        for f in range(fronts):
            inn_copy(f).wait()
            load_raw(f)
            for r in range(rows):
                value = forcing_row(r)
                put_out(f, r, value)
                put_send(f, r, value)
            if f == 0:
                pl.semaphore_wait(barrier, 1)
            x_copy(0, f).start()

        for f in range(fronts):
            x_copy(1, f).start()
        for f in range(fronts):
            for k in range(2):
                x_copy(k, f).wait_send()

    @pl.when(tm < last)
    def _():
        has_down = lat > 0
        has_up = lat < lats - 1
        greet(dev(lat, tm + 1, core))
        greet(dev(lat, tm, 1 - core))

        @pl.when(has_down)
        def _():
            greet(dev(lat - 1, tm, 0))
            greet(dev(lat - 1, tm, 1))

        @pl.when(has_up)
        def _():
            greet(dev(lat + 1, tm, 0))
            greet(dev(lat + 1, tm, 1))

        greeted = 2 + 2 * has_down.astype(jnp.int32) + 2 * has_up.astype(jnp.int32)
        if owners > 2:
            @pl.when(tm > 0)
            def _():
                greet(dev(lat, tm - 1, core))
            greeted = greeted + (tm > 0).astype(jnp.int32)
        clear_send()

        loads = [
            pltpu.make_async_copy(slopes_hbm, slopes_ref, load_rest.at[0]),
            pltpu.make_async_copy(w_out_hbm, w_out_ref, load_rest.at[1]),
            pltpu.make_async_copy(w_in_hbm, w_in_ref, load_rest.at[2]),
        ]
        for load in loads:
            load.start()
        w_wide[...] = jnp.zeros_like(w_wide)
        w_tall[...] = jnp.zeros_like(w_tall)

        loads[0].wait()
        slope_f32[...] = slopes_ref[...].astype(F32)
        for r in range(band):
            slope_rows[r] = slope_f32[pl.ds(r, half, stride=band), :].astype(BF16)

        first = (lat == 0) & (core == 0)
        final = (lat == lats - 1) & (core == 1)

        @pl.when(first)
        def _():
            slope_win[:, 0] = jnp.zeros((2, half, win), BF16)
            for f in range(fronts):
                adj[f, 0:2] = jnp.zeros((2, pad, win), BF16)

        @pl.when(final)
        def _():
            slope_win[:, hid_rows - 1] = jnp.zeros((2, half, win), BF16)
            for f in range(fronts):
                adj[f, rims - 2:rims] = jnp.zeros((2, pad, win), BF16)

        layer = layer_ref[tm]
        loads[1].wait()
        for a in range(3):
            for b in range(3):
                w_wide[b, a * half:(a + 1) * half, 0:chans] = w_out_ref[layer, a, b].astype(F32)
        wide = w_wide[0] + pltpu.roll(w_wide[1], pad, 1) + pltpu.roll(w_wide[2], 2 * pad, 1)
        w1_ref[...] = wide.astype(BF16)
        loads[2].wait()
        for a in range(3):
            for b in range(3):
                w_tall[a, b * half:(b + 1) * half, 0:chans] = w_in_ref[layer, a, b].astype(F32)
        for a in range(3):
            w2_ref[a * pad:(a + 1) * pad, :] = w_tall[a].T[0:pad].astype(BF16)

        pl.semaphore_wait(barrier, greeted)

        partner = dev(lat, tm, 1 - core)
        w1_copy = pltpu.make_async_remote_copy(
            src_ref=w1_ref, dst_ref=w1_other, send_sem=w_send.at[0], recv_sem=w_recv.at[0],
            device_id=partner, device_id_type=MESH)
        w2_copy = pltpu.make_async_remote_copy(
            src_ref=w2_ref, dst_ref=w2_other, send_sem=w_send.at[1], recv_sem=w_recv.at[1],
            device_id=partner, device_id_type=MESH)
        own = hid_rows - 1
        mine_from = core * (rows - 1)
        partner_from = (1 - core) * (rows - 1)
        s_copy = pltpu.make_async_remote_copy(
            src_ref=slope_rows.at[pl.ds(partner_from, own)],
            dst_ref=slope_win.at[1, pl.ds(core, own)],
            send_sem=s_send.at[0], recv_sem=s_recv.at[0],
            device_id=partner, device_id_type=MESH)
        s_down = pltpu.make_async_remote_copy(
            src_ref=slope_rows.at[0], dst_ref=slope_win.at[1 - core, hid_rows - 1],
            send_sem=s_send.at[1], recv_sem=s_recv.at[1 + (1 - core)],
            device_id=dev(lat - 1, tm, 1), device_id_type=MESH)
        s_up = pltpu.make_async_remote_copy(
            src_ref=slope_rows.at[band - 1], dst_ref=slope_win.at[core, 0],
            send_sem=s_send.at[2], recv_sem=s_recv.at[1 + core],
            device_id=dev(lat + 1, tm, 0), device_id_type=MESH)

        w1_copy.start()
        s_copy.start()
        w2_copy.start()

        @pl.when(has_down)
        def _():
            s_down.start()

        @pl.when(has_up)
        def _():
            s_up.start()

        slope_win[0, pl.ds(1 - core, own)] = slope_rows[pl.ds(mine_from, own)]

        not_first = jnp.logical_not(first)
        not_final = jnp.logical_not(final)

        def halo_down(f):
            return pltpu.make_async_remote_copy(
                src_ref=adj.at[f, pl.ds(2, 2)], dst_ref=adj.at[f, pl.ds(rims - 2, 2)],
                send_sem=h_send.at[0, f], recv_sem=h_recv.at[0, f],
                device_id=dev(lat - (1 - core), tm, 1 - core), device_id_type=MESH)

        def halo_up(f):
            return pltpu.make_async_remote_copy(
                src_ref=adj.at[f, pl.ds(rows, 2)], dst_ref=adj.at[f, pl.ds(0, 2)],
                send_sem=h_send.at[1, f], recv_sem=h_recv.at[1, f],
                device_id=dev(lat + core, tm, 1 - core), device_id_type=MESH)

        def pass_on(k, f):
            x_copy(k, f).wait_recv()

            @pl.when(not_first & (core == k))
            def _():
                halo_down(f).start()

            @pl.when(not_final & (core == 1 - k))
            def _():
                halo_up(f).start()

        left_edge = lane == 0
        right_edge = lane == win - 1

        def shifts(x):
            ahead = jnp.where(right_edge, 0.0, pltpu.roll(x, win - 1, 1))
            behind = jnp.where(left_edge, 0.0, pltpu.roll(x, 1, 1))
            return ahead.astype(BF16), x.astype(BF16), behind.astype(BF16)

        def spread_rows(f, row_nos):
            for r in row_nos:
                for b, part in enumerate(shifts(adj[f, r].astype(F32))):
                    vs[f % 2, b * pad:(b + 1) * pad, r * win:(r + 1) * win] = part

        def first_conv(f, low, high):
            columns = slice(low * win, high * win)
            for side, w_ref in enumerate((w1_ref, w1_other)):
                hs[f % 2, side, :, columns] = jnp.dot(
                    w_ref[:, 0:3 * pad], vs[f % 2, :, columns], preferred_element_type=F32)

        def compute(f):
            spread_rows(f, (0, 1, rims - 2, rims - 1))
            first_conv(f, 0, 2)
            first_conv(f, rims - 2, rims)
            for side in range(2):
                for p in range(hid_rows):
                    grad = sum(hs[f % 2, side, a * half:(a + 1) * half, (p + 2 - a) * win:(p + 3 - a) * win]
                               for a in range(3))
                    scaled = (slope_win[side, p].astype(F32) * grad).astype(BF16).astype(F32)
                    for b, part in enumerate(shifts(scaled)):
                        ss[f % 2, side, b * half:(b + 1) * half, p * win:(p + 1) * win] = part
            g = (jnp.dot(w2_ref[...], ss[f % 2, 0], preferred_element_type=F32)
                 + jnp.dot(w2_other[...], ss[f % 2, 1], preferred_element_type=F32))
            for r in range(rows):
                total = sum(g[a * pad:(a + 1) * pad, (r + 2 - a) * win:(r + 3 - a) * win]
                            for a in range(3))
                value = adj[f, r + 2].astype(F32) + total + send_x[f, r].astype(F32)
                value = value[0:chans]
                put_out(f, r, value)
                if owners > 2:
                    put_send(f, r, value)

        def finish(pair):
            for f in pair:
                @pl.when(not_final)
                def _():
                    halo_down(f).wait_recv()

                @pl.when(not_first)
                def _():
                    halo_up(f).wait_recv()

            for f in pair:
                compute(f)
            if owners > 2:
                @pl.when(tm > 0)
                def _():
                    for f in pair:
                        for k in range(2):
                            x_copy(k, f).start()

        for f in range(fronts):
            inn_copy(f).wait()
            load_raw(f)
            for r in range(rows):
                put_send(f, r, forcing_row(r))

        def begin(f):
            spread_rows(f, range(2, rows + 2))
            first_conv(f, 2, rows + 2)

        w1_copy.wait_recv()
        w2_copy.wait_recv()
        s_copy.wait_recv()

        @pl.when(has_down & (core == 0))
        def _():
            s_up_recv(slope_win, slope_rows, s_send, s_recv, 0, dev(lat, tm, 1 - core))

        @pl.when(has_up & (core == 1))
        def _():
            s_up_recv(slope_win, slope_rows, s_send, s_recv, hid_rows - 1, dev(lat, tm, 1 - core))

        @pl.loop(0, fronts)
        def _(f):
            pass_on(0, f)

        waiting = []
        for f in range(fronts):
            pass_on(1, f)
            if len(waiting) == 1:
                finish(waiting)
                waiting = []
            begin(f)
            waiting.append(f)
        finish(waiting)

        w1_copy.wait_send()
        w2_copy.wait_send()
        s_copy.wait_send()

        @pl.when(has_down)
        def _():
            s_down.wait_send()

        @pl.when(has_up)
        def _():
            s_up.wait_send()

        @pl.loop(0, fronts)
        def _(f):
            @pl.when(not_first)
            def _():
                halo_down(f).wait_send()

            @pl.when(not_final)
            def _():
                halo_up(f).wait_send()

            if owners > 2:
                @pl.when(tm > 0)
                def _():
                    for k in range(2):
                        x_copy(k, f).wait_send()


def s_up_recv(slope_win, slope_rows, s_send, s_recv, row, device):
    for side in range(2):
        pltpu.make_async_remote_copy(
            src_ref=slope_rows.at[0], dst_ref=slope_win.at[side, row],
            send_sem=s_send.at[1], recv_sem=s_recv.at[1 + side],
            device_id=device, device_id_type=MESH).wait_recv()


def in_hbm(array):
    return pltpu.with_memory_space_constraint(array, pltpu.HBM)


def per_device(mesh, innovations, obs_mask, slopes, layer_of, weight_in, weight_out):
    fronts, secs, chans, rows, win = innovations.shape
    _, half, band, _ = slopes.shape
    owners = mesh.shape["tm"]
    lats = mesh.shape["lat"]
    assert secs == 1 and band == 2 * rows and rows == 4 and owners > 1
    pair = owners == 2 and fronts > 1
    pad = round_up(chans, 16)
    rims, hid_rows = rows + 4, rows + 2

    layers = weight_in.shape[0]
    wide = round_up(3 * pad, 128)
    deep = round_up(3 * half, 128)

    smem = pl.BlockSpec(memory_space=pltpu.SMEM)
    hbm = pl.BlockSpec(memory_space=pltpu.HBM)
    vmem = pl.BlockSpec(memory_space=pltpu.VMEM)
    out = pl.pallas_call(
        functools.partial(pair_kernel if pair else chain_kernel, (fronts, chans, rows, win, half, band, lats, owners)),
        out_shape=pltpu.VMEM((fronts * chans * rows, win), F32),
        in_specs=[smem, smem, hbm, hbm, hbm, hbm],
        out_specs=vmem,
        scratch_shapes=[
            pltpu.VMEM((fronts, chans, rows, win), BF16),
            pltpu.VMEM((half * band, win), BF16),
            pltpu.VMEM((layers, 3, 3, half, chans), BF16),
            pltpu.VMEM((layers, 3, 3, half, chans), BF16),
            pltpu.VMEM((3, 3 * half, wide), F32),
            pltpu.VMEM((3, 3 * half, 128), F32),
            pltpu.VMEM((chans * rows, win), F32),
            pltpu.VMEM((fronts, rows, pad, win), BF16),
            pltpu.VMEM((fronts, rims, pad, win), BF16),
            *([pltpu.VMEM((rows, pad, win), BF16)] if pair else []),
            pltpu.VMEM((half * band, win), F32),
            pltpu.VMEM((band, half, win), BF16),
            pltpu.VMEM((2, hid_rows, half, win), BF16),
            *([
                pltpu.VMEM((2, 3 * half, wide), BF16),
                pltpu.VMEM((3 * pad, 2 * deep), BF16),
                pltpu.VMEM((2, 3 * pad, rims * win), BF16),
                pltpu.VMEM((2, 6 * half, rims * win), F32),
                pltpu.VMEM((2, 2 * deep, hid_rows * win), BF16),
            ] if pair else [
                pltpu.VMEM((3 * half, wide), BF16),
                pltpu.VMEM((3 * pad, 3 * half), BF16),
                pltpu.VMEM((3 * half, wide), BF16),
                pltpu.VMEM((3 * pad, 3 * half), BF16),
                pltpu.VMEM((2, 3 * pad, rims * win), BF16),
                pltpu.VMEM((2, 2, 3 * half, rims * win), F32),
                pltpu.VMEM((2, 2, 3 * half, hid_rows * win), BF16),
            ]),
            pltpu.SemaphoreType.DMA((fronts,)),
            pltpu.SemaphoreType.DMA((3,)),
            pltpu.SemaphoreType.DMA((2, fronts)),
            pltpu.SemaphoreType.DMA((2, fronts)),
            *([pltpu.SemaphoreType.DMA((2,))] * 2 if pair else []),
            pltpu.SemaphoreType.DMA((2, fronts)),
            pltpu.SemaphoreType.DMA((2, fronts)),
            pltpu.SemaphoreType.DMA((2,)),
            pltpu.SemaphoreType.DMA((2,)),
            pltpu.SemaphoreType.DMA((5,)),
            pltpu.SemaphoreType.DMA((3,)),
            *([pltpu.SemaphoreType.DMA((2,))] * 2 + [pltpu.SemaphoreType.REGULAR] if pair else []),
        ],
        compiler_params=pltpu.CompilerParams(
            collective_id=0, has_side_effects=True, vmem_limit_bytes=32 * 1024 * 1024
        ),
    )(
        in_hbm(layer_of),
        in_hbm(obs_mask.reshape(obs_mask.shape[-1])),
        in_hbm(innovations.reshape(fronts, chans, rows, win)),
        in_hbm(slopes.reshape(half * band, win)),
        in_hbm(weight_in.swapaxes(3, 4)),
        in_hbm(weight_out),
    )
    return out.reshape(innovations.shape)


def solution(mesh):
    return jax.shard_map(
        functools.partial(per_device, mesh),
        mesh=mesh,
        in_specs=(
            P(None, ("grp", "tm"), None, ("lat", "chan"), None),
            P(("grp", "tm"), ("lat", "chan"), None),
            P(("grp", "tm"), "chan", "lat", None),
            P(),
            P(None, None, None, None, "chan"),
            P(None, None, None, "chan", None),
        ),
        out_specs=P(None, ("grp", "tm"), None, ("lat", "chan"), None),
        check_vma=False,
    )
```

```python
import functools

import jax
import jax.numpy as jnp
from jax import lax
from jax.experimental import pallas as pl
from jax.experimental.pallas import tpu as pltpu
from jax.sharding import PartitionSpec as P

MESH = pl.DeviceIdType.MESH
BF16 = jnp.bfloat16
F32 = jnp.float32


def round_up(n, m):
    return -(-n // m) * m


def pair_kernel(dims, layer_ref, mask_ref, inn_hbm, slopes_hbm, w_in_hbm, w_out_hbm, out_ref,
                inn_ref, slopes_ref, w_in_ref, w_out_ref, w_wide, w_tall,
                raw, frc, adj, packing, packed, folding, folded, slope_f32, slope_rows, slope_win, w1_ref, w2_ref, vs, hs, ss, load_inn, load_rest,
                x_send, x_recv, r_send, r_recv, h_send, h_recv, w_send, w_recv, s_send, s_recv,
                t_send, t_recv, above):
    fronts, chans, rows, win, half, band, lats, owners = dims
    pad = frc.shape[2]
    rims = rows + 4
    hid_rows = rows + 2
    far = fronts - 1
    deep = w2_ref.shape[1] // 2
    grp = lax.axis_index("grp")
    lat = lax.axis_index("lat")
    tm = lax.axis_index("tm")
    core = lax.axis_index("chan")

    def dev(lat_no, tm_no, core_no):
        return (grp, lat_no, tm_no, core_no)

    partner = dev(lat, tm, 1 - core)
    opposite = dev(lat, 1 - tm, core)
    has_down = lat > 0
    has_up = lat < lats - 1
    first = (lat == 0) & (core == 0)
    final = (lat == lats - 1) & (core == 1)
    not_first = jnp.logical_not(first)
    not_final = jnp.logical_not(final)

    barrier = pltpu.get_barrier_semaphore()

    def greet(device):
        pl.semaphore_signal(barrier, inc=1, device_id=device, device_id_type=MESH)

    greet(opposite)

    @pl.when(has_up)
    def _():
        greet(dev(lat + 1, tm, 0))

        @pl.when(core == 1)
        def _():
            greet(dev(lat + 1, tm, 1))

        @pl.when(tm == 0)
        def _():
            greet(dev(lat + 1, 1, 0))

        @pl.when((tm == 1) & (core == 1))
        def _():
            greet(dev(lat + 1, 0, 0))
            greet(dev(lat + 1, 0, 1))

    greet(partner)
    below = has_down.astype(jnp.int32)

    def enter():
        pl.semaphore_wait(barrier, 2 + below * (2 - core + (1 - tm) + 2 * tm * (1 - core)))

        @pl.when(has_down & (core == 0))
        def _():
            for c in range(2):
                pl.semaphore_signal(above, inc=1, device_id=dev(lat - 1, tm, c), device_id_type=MESH)

        @pl.when(has_down & (core == 0) & (tm == 1))
        def _():
            for c in range(2):
                pl.semaphore_signal(above, inc=1, device_id=dev(lat - 1, 0, c), device_id_type=MESH)

    def wait_above():
        @pl.when(has_up)
        def _():
            pl.semaphore_wait(above, 2 - tm)

    def inn_copy(f):
        return pltpu.make_async_copy(inn_hbm.at[f], inn_ref.at[f], load_inn.at[f])

    loads = [
        pltpu.make_async_copy(slopes_hbm, slopes_ref, load_rest.at[0]),
        pltpu.make_async_copy(w_out_hbm, w_out_ref, load_rest.at[1]),
        pltpu.make_async_copy(w_in_hbm, w_in_ref, load_rest.at[2]),
    ]

    lane = lax.broadcasted_iota(jnp.int32, (1, win), 1)
    tiles = mask_ref.shape[0]
    width = win // tiles
    spread = jnp.zeros((1, win), F32)
    for k in range(tiles):
        spread = jnp.where(lane // width == k, mask_ref[k].astype(F32), spread)

    def load_raw(f):
        raw[...] = inn_ref[f].astype(F32).reshape(chans * rows, win)

    def forcing_row(r):
        return raw[pl.ds(r, chans, stride=rows), :] * spread

    def put_out(f, r, value):
        out_ref[pl.ds(f * (chans * rows) + r, chans, stride=rows), :] = value

    starts = (core * 2, (1 - core) * 2)

    def tail(n):
        return round_up(chans * n + pad, 16)

    def span(f):
        low = tail(2 * f - 1) if f else 0
        return pl.ds(low, tail(2 * f + 1) - low)

    def x_copy(k, f):
        part = packed.at[k, span(f)]
        return pltpu.make_async_remote_copy(
            src_ref=part, dst_ref=part, send_sem=x_send.at[k, f], recv_sem=x_recv.at[k, f],
            device_id=opposite, device_id_type=MESH)

    def r_copy(k):
        part = folded.at[span(k)]
        return pltpu.make_async_remote_copy(
            src_ref=part, dst_ref=part, send_sem=r_send.at[k], recv_sem=r_recv.at[k],
            device_id=opposite, device_id_type=MESH)

    def unpacked(rows_of, n):
        low = chans * n // 16 * 16
        return rows_of[low:tail(n)].astype(F32)[chans * n - low:chans * n - low + pad]

    def unpack(k, f):
        x_copy(k, f).wait_recv()
        for r in range(2):
            adj[f, 2 + starts[k] + r] = unpacked(packed.at[k], 2 * f + r).astype(BF16)

    spans = ((3 - 3 * core, 5), (5 * core, 3))

    def t_copy(k):
        part = slope_rows.at[pl.ds(*spans[k])]
        return pltpu.make_async_remote_copy(
            src_ref=part, dst_ref=part, send_sem=t_send.at[k], recv_sem=t_recv.at[k],
            device_id=opposite, device_id_type=MESH)

    def halo_down(f):
        return pltpu.make_async_remote_copy(
            src_ref=adj.at[f, pl.ds(2, 2)], dst_ref=adj.at[f, pl.ds(rims - 2, 2)],
            send_sem=h_send.at[0, f], recv_sem=h_recv.at[0, f],
            device_id=dev(lat - (1 - core), tm, 1 - core), device_id_type=MESH)

    def halo_up(f):
        return pltpu.make_async_remote_copy(
            src_ref=adj.at[f, pl.ds(rows, 2)], dst_ref=adj.at[f, pl.ds(0, 2)],
            send_sem=h_send.at[1, f], recv_sem=h_recv.at[1, f],
            device_id=dev(lat + core, tm, 1 - core), device_id_type=MESH)

    def pass_on(k, f):
        @pl.when(not_first & (core == k))
        def _():
            halo_down(f).start()

        @pl.when(not_final & (core == 1 - k))
        def _():
            halo_up(f).start()

    def halos_here(f):
        @pl.when(not_final)
        def _():
            halo_down(f).wait_recv()

        @pl.when(not_first)
        def _():
            halo_up(f).wait_recv()

    def halos_sent(f):
        @pl.when(not_first)
        def _():
            halo_down(f).wait_send()

        @pl.when(not_final)
        def _():
            halo_up(f).wait_send()

    w1_copy = pltpu.make_async_remote_copy(
        src_ref=w1_ref.at[0], dst_ref=w1_ref.at[1], send_sem=w_send.at[0], recv_sem=w_recv.at[0],
        device_id=partner, device_id_type=MESH)
    w2_copy = pltpu.make_async_remote_copy(
        src_ref=w2_ref.at[:, pl.ds(0, deep)], dst_ref=w2_ref.at[:, pl.ds(deep, deep)],
        send_sem=w_send.at[1], recv_sem=w_recv.at[1],
        device_id=partner, device_id_type=MESH)
    own = hid_rows - 1
    mine_from = core * (rows - 1)
    partner_from = (1 - core) * (rows - 1)
    s_copy = pltpu.make_async_remote_copy(
        src_ref=slope_rows.at[pl.ds(partner_from, own)],
        dst_ref=slope_win.at[1, pl.ds(core, own)],
        send_sem=s_send.at[0], recv_sem=s_recv.at[0],
        device_id=partner, device_id_type=MESH)

    def s_down(to, k):
        return pltpu.make_async_remote_copy(
            src_ref=slope_rows.at[0], dst_ref=slope_win.at[1 - core, hid_rows - 1],
            send_sem=s_send.at[1 + k], recv_sem=s_recv.at[1 + (1 - core)],
            device_id=dev(lat - 1, to, 1), device_id_type=MESH)

    def s_up(to, k):
        return pltpu.make_async_remote_copy(
            src_ref=slope_rows.at[band - 1], dst_ref=slope_win.at[core, 0],
            send_sem=s_send.at[3 + k], recv_sem=s_recv.at[1 + core],
            device_id=dev(lat + 1, to, 0), device_id_type=MESH)

    def slope_down(act, to):
        @pl.when(has_down)
        def _():
            act(s_down(to, to))

    def slope_up(act, to):
        @pl.when(has_up)
        def _():
            act(s_up(to, to))

    def start(copy):
        copy.start()

    def slopes_here():
        s_copy.wait_recv()

        @pl.when(has_down & (core == 0))
        def _():
            s_up_recv(slope_win, slope_rows, s_send, s_recv, 0, partner)

        @pl.when(has_up & (core == 1))
        def _():
            s_up_recv(slope_win, slope_rows, s_send, s_recv, hid_rows - 1, partner)

    def own_slopes():
        slope_win[0, pl.ds(1 - core, own)] = slope_rows[pl.ds(mine_from, own)]

    def all_sent():
        w1_copy.wait_send()
        w2_copy.wait_send()
        s_copy.wait_send()

    def clear_rims():
        @pl.when(first)
        def _():
            slope_win[:, 0] = jnp.zeros((2, half, win), BF16)
            for f in range(fronts):
                adj[f, 0:2] = jnp.zeros((2, pad, win), BF16)

        @pl.when(final)
        def _():
            slope_win[:, hid_rows - 1] = jnp.zeros((2, half, win), BF16)
            for f in range(fronts):
                adj[f, rims - 2:rims] = jnp.zeros((2, pad, win), BF16)

    def prepare_weights():
        w_wide[...] = jnp.zeros_like(w_wide)
        w_tall[...] = jnp.zeros_like(w_tall)
        if deep > 3 * half:
            w2_ref[:, 3 * half:deep] = jnp.zeros((3 * pad, deep - 3 * half), BF16)
            for side in range(2):
                ss[:, side * deep + 3 * half:(side + 1) * deep] = jnp.zeros(
                    (2, deep - 3 * half, hid_rows * win), BF16)
        layer = layer_ref[0]
        loads[1].wait()
        for a in range(3):
            for b in range(3):
                w_wide[b, a * half:(a + 1) * half, 0:chans] = w_out_ref[layer, a, b].astype(F32)
        wide = w_wide[0] + pltpu.roll(w_wide[1], pad, 1) + pltpu.roll(w_wide[2], 2 * pad, 1)
        w1_ref[0] = wide.astype(BF16)
        loads[2].wait()
        for a in range(3):
            for b in range(3):
                w_tall[a, b * half:(b + 1) * half, 0:chans] = w_in_ref[layer, a, b].astype(F32)
        for a in range(3):
            w2_ref[a * pad:(a + 1) * pad, 0:3 * half] = w_tall[a].T[0:pad].astype(BF16)

    left_edge = lane == 0
    right_edge = lane == win - 1

    def shifts(x):
        ahead = jnp.where(right_edge, 0.0, pltpu.roll(x, win - 1, 1))
        behind = jnp.where(left_edge, 0.0, pltpu.roll(x, 1, 1))
        return ahead.astype(BF16), x.astype(BF16), behind.astype(BF16)

    place = [*range(rows, rows + 2), *range(rows), *range(rows + 2, rims)]

    def columns(row):
        return slice(place[row] * win, (place[row] + 1) * win)

    def convolve(own, rim):
        slot = own % 2 if own is not None else (rim + 1) % 2
        for f, row_nos in ((own, range(2, rows + 2)), (rim, (0, 1, rims - 2, rims - 1))):
            for r in row_nos if f is not None else ():
                for b, part in enumerate(shifts(adj[f, r].astype(F32))):
                    vs[slot, b * pad:(b + 1) * pad, columns(r)] = part
        low = 0 if own is not None else rows * win
        high = (rims if rim is not None else rows) * win
        both = w1_ref[...].reshape(6 * half, w1_ref.shape[2])
        product = jnp.dot(both[:, 0:3 * pad], vs[slot, :, low:high], preferred_element_type=F32)
        if own is not None:
            hs[own, :, 0:rows * win] = product[:, 0:rows * win]
        if rim is not None:
            hs[rim, :, rows * win:] = product[:, rows * win - low:]

    def rest(f):
        for side in range(2):
            for p in range(hid_rows):
                grad = sum(hs[f, (3 * side + a) * half:(3 * side + a + 1) * half, columns(p + 2 - a)]
                           for a in range(3))
                scaled = (slope_win[side, p].astype(F32) * grad).astype(BF16).astype(F32)
                for b, part in enumerate(shifts(scaled)):
                    low = side * deep + b * half
                    ss[f % 2, low:low + half, p * win:(p + 1) * win] = part
        totals = [adj[f, r + 2].astype(F32) for r in range(rows)]
        for p in range(0, hid_rows, 2):
            offsets = [a for a in range(3) if p - 1 + a >= 0 and p - 2 + a < rows]
            first, count = offsets[0], len(offsets)
            g = jnp.dot(w2_ref[first * pad:(first + count) * pad, :], ss[f % 2, :, p * win:(p + 2) * win],
                        preferred_element_type=F32)
            for a in offsets:
                for step in range(2):
                    r = p + step - 2 + a
                    if 0 <= r < rows:
                        totals[r] = totals[r] + g[(a - first) * pad:(a - first + 1) * pad, step * win:(step + 1) * win]
        return totals

    @pl.when(tm == 1)
    def _():
        for f in range(fronts):
            inn_copy(f).start()
        for load in loads[1:]:
            load.start()
        clear_rims()
        if pad > chans:
            for r in range(rows):
                adj[far, r + 2, chans:pad, :] = jnp.zeros((pad - chans, win), BF16)

        filled = 2 * far * chans
        packing[:, filled:, :] = jnp.zeros((2, tail(2 * far - 1) - filled, win), F32)
        folding[4 * chans:, :] = jnp.zeros((tail(3) - 4 * chans, win), F32)
        for f in range(far):
            inn_copy(f).wait()
            load_raw(f)
            for r in range(rows):
                kind = core if r < 2 else 1 - core
                packing[kind, chans * (2 * f + r % 2):chans * (2 * f + r % 2 + 1), :] = forcing_row(r)
        packed[...] = packing[...].astype(BF16)
        enter()
        x_copy(0, 0).start()

        @pl.when(core == 1)
        def _():
            x_copy(0, 0).wait_send()

        for f in range(1, far):
            x_copy(0, f).start()
        for f in range(far):
            x_copy(1, f).start()
        inn_copy(far).wait()
        load_raw(far)
        for r in range(rows):
            adj[far, r + 2, 0:chans, :] = forcing_row(r).astype(BF16)

        @pl.when(not_first)
        def _():
            halo_down(far).start()

        @pl.when(not_final & (core == 0))
        def _():
            halo_up(far).start()

        prepare_weights()
        w1_copy.start()
        w2_copy.start()
        wait_above()

        @pl.when(not_final & (core == 1))
        def _():
            halo_up(far).start()

        for f in reversed(range(fronts)):
            if f < far:
                load_raw(f)
            for r in range(rows):
                put_out(f, r, forcing_row(r))

        w1_copy.wait_recv()
        convolve(far, None)
        t_copy(0).wait_recv()
        s_copy.start()
        halos_here(far)
        convolve(None, far)
        w2_copy.wait_recv()
        t_copy(1).wait_recv()
        own_slopes()
        slopes_here()
        for r, value in enumerate(rest(far)):
            folding[chans * r:chans * (r + 1), :] = value[0:chans]
        folded[...] = folding[...].astype(BF16)
        r_copy(0).start()

        @pl.when(core == 1)
        def _():
            r_copy(0).wait_send()

        r_copy(1).start()

        all_sent()
        halos_sent(far)
        @pl.when(core == 0)
        def _():
            x_copy(0, 0).wait_send()

        for k in range(2):
            for f in range(1 - k, far):
                x_copy(k, f).wait_send()

        @pl.when(core == 0)
        def _():
            r_copy(0).wait_send()

        r_copy(1).wait_send()

    @pl.when(tm == 0)
    def _():
        for load in loads:
            load.start()
        for f in range(fronts):
            inn_copy(f).start()
        clear_rims()

        loads[0].wait()
        slope_f32[...] = slopes_ref[...].astype(F32)
        for r in range(band):
            slope_rows[r] = slope_f32[pl.ds(r, half, stride=band), :].astype(BF16)
        enter()
        slope_down(start, 1)
        t_copy(0).start()

        @pl.when(core == 0)
        def _():
            t_copy(1).start()

        slope_down(start, 0)
        s_copy.start()
        own_slopes()
        prepare_weights()

        @pl.when(core == 1)
        def _():
            t_copy(1).start()

        wait_above()
        slope_up(start, 1)
        slope_up(start, 0)
        w1_copy.start()
        w2_copy.start()

        for f in range(fronts):
            inn_copy(f).wait()
            load_raw(f)
            for r in range(rows):
                frc[f, r, 0:chans, :] = forcing_row(r).astype(BF16)

        for f in range(far):
            unpack(0, f)
            pass_on(0, f)

        w1_copy.wait_recv()
        w2_copy.wait_recv()
        slopes_here()

        def finish(f, following):
            halos_here(f)
            convolve(following, f)
            for r, value in enumerate(rest(f)):
                put_out(f, r, value[0:chans] + frc[f, r, 0:chans, :].astype(F32))

        def inner_rows(f):
            unpack(1, f)
            pass_on(1, f)

        @pl.when(core == 0)
        def _():
            for f in range(far):
                inner_rows(f)
                if f < far - 1 or far < 3:
                    convolve(f, None)
                if f < far - 2:
                    finish(f, None)
            for f in range(max(far - 2, 0), far):
                finish(f, far - 1 if far > 2 and f == far - 2 else None)

        @pl.when(core == 1)
        def _():
            for f in range(far):
                inner_rows(f)
                if f < far - 1:
                    convolve(f, None)
            for f in range(far):
                if far == 1:
                    convolve(f, None)
                finish(f, far - 1 if far > 1 and f == 0 else None)

        for k in range(2):
            r_copy(k).wait_recv()
            for r in (2 * k, 2 * k + 1):
                put_out(far, r, unpacked(folded, r)[0:chans] + frc[far, r, 0:chans, :].astype(F32))

        all_sent()
        for f in range(far):
            halos_sent(f)
        for k in range(2):
            t_copy(k).wait_send()
            slope_down(lambda copy: copy.wait_send(), k)
            slope_up(lambda copy: copy.wait_send(), k)


def chain_kernel(dims, layer_ref, mask_ref, inn_hbm, slopes_hbm, w_in_hbm, w_out_hbm, out_ref,
           inn_ref, slopes_ref, w_in_ref, w_out_ref, w_wide, w_tall,
           raw, send_x, adj, slope_f32, slope_rows, slope_win, w1_ref, w2_ref, w1_other,
           w2_other, vs, hs, ss, load_inn, load_rest,
           x_send, x_recv, h_send, h_recv, w_send, w_recv, s_send, s_recv):
    fronts, chans, rows, win, half, band, lats, owners = dims
    pad = send_x.shape[2]
    rims = rows + 4
    hid_rows = rows + 2
    grp = lax.axis_index("grp")
    lat = lax.axis_index("lat")
    tm = lax.axis_index("tm")
    core = lax.axis_index("chan")
    last = owners - 1

    def dev(lat_no, tm_no, core_no):
        return (grp, lat_no, tm_no, core_no)

    barrier = pltpu.get_barrier_semaphore()

    def greet(device):
        pl.semaphore_signal(barrier, inc=1, device_id=device, device_id_type=MESH)

    def inn_copy(f):
        return pltpu.make_async_copy(inn_hbm.at[f], inn_ref.at[f], load_inn.at[f])

    for f in range(fronts):
        inn_copy(f).start()

    lane = lax.broadcasted_iota(jnp.int32, (1, win), 1)
    tiles = mask_ref.shape[0]
    width = win // tiles
    spread = jnp.zeros((1, win), F32)
    for k in range(tiles):
        spread = jnp.where(lane // width == k, mask_ref[k].astype(F32), spread)

    def load_raw(f):
        raw[...] = inn_ref[f].astype(F32).reshape(chans * rows, win)

    def forcing_row(r):
        return raw[pl.ds(r, chans, stride=rows), :] * spread

    def put_out(f, r, value):
        out_ref[pl.ds(f * (chans * rows) + r, chans, stride=rows), :] = value

    starts = (core * 2, (1 - core) * 2)

    def x_copy(k, f):
        return pltpu.make_async_remote_copy(
            src_ref=send_x.at[f, pl.ds(starts[k], 2)], dst_ref=adj.at[f, pl.ds(2 + starts[k], 2)],
            send_sem=x_send.at[k, f], recv_sem=x_recv.at[k, f],
            device_id=dev(lat, lax.rem(tm + owners - 1, owners), core), device_id_type=MESH)

    def put_send(f, r, value):
        send_x[f, r, 0:chans, :] = value.astype(BF16)

    def clear_send():
        if pad > chans:
            for f in range(fronts):
                for r in range(rows):
                    send_x[f, r, chans:pad, :] = jnp.zeros((pad - chans, win), BF16)

    @pl.when(tm == last)
    def _():
        greet(dev(lat, tm - 1, core))
        clear_send()

        for f in range(fronts):
            inn_copy(f).wait()
            load_raw(f)
            for r in range(rows):
                value = forcing_row(r)
                put_out(f, r, value)
                put_send(f, r, value)
            if f == 0:
                pl.semaphore_wait(barrier, 1)
            x_copy(0, f).start()

        for f in range(fronts):
            x_copy(1, f).start()
        for f in range(fronts):
            for k in range(2):
                x_copy(k, f).wait_send()

    @pl.when(tm < last)
    def _():
        has_down = lat > 0
        has_up = lat < lats - 1
        greet(dev(lat, tm + 1, core))
        greet(dev(lat, tm, 1 - core))

        @pl.when(has_down)
        def _():
            greet(dev(lat - 1, tm, 0))
            greet(dev(lat - 1, tm, 1))

        @pl.when(has_up)
        def _():
            greet(dev(lat + 1, tm, 0))
            greet(dev(lat + 1, tm, 1))

        greeted = 2 + 2 * has_down.astype(jnp.int32) + 2 * has_up.astype(jnp.int32)
        if owners > 2:
            @pl.when(tm > 0)
            def _():
                greet(dev(lat, tm - 1, core))
            greeted = greeted + (tm > 0).astype(jnp.int32)
        clear_send()

        loads = [
            pltpu.make_async_copy(slopes_hbm, slopes_ref, load_rest.at[0]),
            pltpu.make_async_copy(w_out_hbm, w_out_ref, load_rest.at[1]),
            pltpu.make_async_copy(w_in_hbm, w_in_ref, load_rest.at[2]),
        ]
        for load in loads:
            load.start()
        w_wide[...] = jnp.zeros_like(w_wide)
        w_tall[...] = jnp.zeros_like(w_tall)

        loads[0].wait()
        slope_f32[...] = slopes_ref[...].astype(F32)
        for r in range(band):
            slope_rows[r] = slope_f32[pl.ds(r, half, stride=band), :].astype(BF16)

        first = (lat == 0) & (core == 0)
        final = (lat == lats - 1) & (core == 1)

        @pl.when(first)
        def _():
            slope_win[:, 0] = jnp.zeros((2, half, win), BF16)
            for f in range(fronts):
                adj[f, 0:2] = jnp.zeros((2, pad, win), BF16)

        @pl.when(final)
        def _():
            slope_win[:, hid_rows - 1] = jnp.zeros((2, half, win), BF16)
            for f in range(fronts):
                adj[f, rims - 2:rims] = jnp.zeros((2, pad, win), BF16)

        layer = layer_ref[tm]
        loads[1].wait()
        for a in range(3):
            for b in range(3):
                w_wide[b, a * half:(a + 1) * half, 0:chans] = w_out_ref[layer, a, b].astype(F32)
        wide = w_wide[0] + pltpu.roll(w_wide[1], pad, 1) + pltpu.roll(w_wide[2], 2 * pad, 1)
        w1_ref[...] = wide.astype(BF16)
        loads[2].wait()
        for a in range(3):
            for b in range(3):
                w_tall[a, b * half:(b + 1) * half, 0:chans] = w_in_ref[layer, a, b].astype(F32)
        for a in range(3):
            w2_ref[a * pad:(a + 1) * pad, :] = w_tall[a].T[0:pad].astype(BF16)

        pl.semaphore_wait(barrier, greeted)

        partner = dev(lat, tm, 1 - core)
        w1_copy = pltpu.make_async_remote_copy(
            src_ref=w1_ref, dst_ref=w1_other, send_sem=w_send.at[0], recv_sem=w_recv.at[0],
            device_id=partner, device_id_type=MESH)
        w2_copy = pltpu.make_async_remote_copy(
            src_ref=w2_ref, dst_ref=w2_other, send_sem=w_send.at[1], recv_sem=w_recv.at[1],
            device_id=partner, device_id_type=MESH)
        own = hid_rows - 1
        mine_from = core * (rows - 1)
        partner_from = (1 - core) * (rows - 1)
        s_copy = pltpu.make_async_remote_copy(
            src_ref=slope_rows.at[pl.ds(partner_from, own)],
            dst_ref=slope_win.at[1, pl.ds(core, own)],
            send_sem=s_send.at[0], recv_sem=s_recv.at[0],
            device_id=partner, device_id_type=MESH)
        s_down = pltpu.make_async_remote_copy(
            src_ref=slope_rows.at[0], dst_ref=slope_win.at[1 - core, hid_rows - 1],
            send_sem=s_send.at[1], recv_sem=s_recv.at[1 + (1 - core)],
            device_id=dev(lat - 1, tm, 1), device_id_type=MESH)
        s_up = pltpu.make_async_remote_copy(
            src_ref=slope_rows.at[band - 1], dst_ref=slope_win.at[core, 0],
            send_sem=s_send.at[2], recv_sem=s_recv.at[1 + core],
            device_id=dev(lat + 1, tm, 0), device_id_type=MESH)

        w1_copy.start()
        s_copy.start()
        w2_copy.start()

        @pl.when(has_down)
        def _():
            s_down.start()

        @pl.when(has_up)
        def _():
            s_up.start()

        slope_win[0, pl.ds(1 - core, own)] = slope_rows[pl.ds(mine_from, own)]

        not_first = jnp.logical_not(first)
        not_final = jnp.logical_not(final)

        def halo_down(f):
            return pltpu.make_async_remote_copy(
                src_ref=adj.at[f, pl.ds(2, 2)], dst_ref=adj.at[f, pl.ds(rims - 2, 2)],
                send_sem=h_send.at[0, f], recv_sem=h_recv.at[0, f],
                device_id=dev(lat - (1 - core), tm, 1 - core), device_id_type=MESH)

        def halo_up(f):
            return pltpu.make_async_remote_copy(
                src_ref=adj.at[f, pl.ds(rows, 2)], dst_ref=adj.at[f, pl.ds(0, 2)],
                send_sem=h_send.at[1, f], recv_sem=h_recv.at[1, f],
                device_id=dev(lat + core, tm, 1 - core), device_id_type=MESH)

        def pass_on(k, f):
            x_copy(k, f).wait_recv()

            @pl.when(not_first & (core == k))
            def _():
                halo_down(f).start()

            @pl.when(not_final & (core == 1 - k))
            def _():
                halo_up(f).start()

        left_edge = lane == 0
        right_edge = lane == win - 1

        def shifts(x):
            ahead = jnp.where(right_edge, 0.0, pltpu.roll(x, win - 1, 1))
            behind = jnp.where(left_edge, 0.0, pltpu.roll(x, 1, 1))
            return ahead.astype(BF16), x.astype(BF16), behind.astype(BF16)

        def spread_rows(f, row_nos):
            for r in row_nos:
                for b, part in enumerate(shifts(adj[f, r].astype(F32))):
                    vs[f % 2, b * pad:(b + 1) * pad, r * win:(r + 1) * win] = part

        def first_conv(f, low, high):
            columns = slice(low * win, high * win)
            for side, w_ref in enumerate((w1_ref, w1_other)):
                hs[f % 2, side, :, columns] = jnp.dot(
                    w_ref[:, 0:3 * pad], vs[f % 2, :, columns], preferred_element_type=F32)

        def compute(f):
            spread_rows(f, (0, 1, rims - 2, rims - 1))
            first_conv(f, 0, 2)
            first_conv(f, rims - 2, rims)
            for side in range(2):
                for p in range(hid_rows):
                    grad = sum(hs[f % 2, side, a * half:(a + 1) * half, (p + 2 - a) * win:(p + 3 - a) * win]
                               for a in range(3))
                    scaled = (slope_win[side, p].astype(F32) * grad).astype(BF16).astype(F32)
                    for b, part in enumerate(shifts(scaled)):
                        ss[f % 2, side, b * half:(b + 1) * half, p * win:(p + 1) * win] = part
            g = (jnp.dot(w2_ref[...], ss[f % 2, 0], preferred_element_type=F32)
                 + jnp.dot(w2_other[...], ss[f % 2, 1], preferred_element_type=F32))
            for r in range(rows):
                total = sum(g[a * pad:(a + 1) * pad, (r + 2 - a) * win:(r + 3 - a) * win]
                            for a in range(3))
                value = adj[f, r + 2].astype(F32) + total + send_x[f, r].astype(F32)
                value = value[0:chans]
                put_out(f, r, value)
                if owners > 2:
                    put_send(f, r, value)

        def finish(pair):
            for f in pair:
                @pl.when(not_final)
                def _():
                    halo_down(f).wait_recv()

                @pl.when(not_first)
                def _():
                    halo_up(f).wait_recv()

            for f in pair:
                compute(f)
            if owners > 2:
                @pl.when(tm > 0)
                def _():
                    for f in pair:
                        for k in range(2):
                            x_copy(k, f).start()

        for f in range(fronts):
            inn_copy(f).wait()
            load_raw(f)
            for r in range(rows):
                put_send(f, r, forcing_row(r))

        def begin(f):
            spread_rows(f, range(2, rows + 2))
            first_conv(f, 2, rows + 2)

        w1_copy.wait_recv()
        w2_copy.wait_recv()
        s_copy.wait_recv()

        @pl.when(has_down & (core == 0))
        def _():
            s_up_recv(slope_win, slope_rows, s_send, s_recv, 0, dev(lat, tm, 1 - core))

        @pl.when(has_up & (core == 1))
        def _():
            s_up_recv(slope_win, slope_rows, s_send, s_recv, hid_rows - 1, dev(lat, tm, 1 - core))

        @pl.loop(0, fronts)
        def _(f):
            pass_on(0, f)

        waiting = []
        for f in range(fronts):
            pass_on(1, f)
            if len(waiting) == 1:
                finish(waiting)
                waiting = []
            begin(f)
            waiting.append(f)
        finish(waiting)

        w1_copy.wait_send()
        w2_copy.wait_send()
        s_copy.wait_send()

        @pl.when(has_down)
        def _():
            s_down.wait_send()

        @pl.when(has_up)
        def _():
            s_up.wait_send()

        @pl.loop(0, fronts)
        def _(f):
            @pl.when(not_first)
            def _():
                halo_down(f).wait_send()

            @pl.when(not_final)
            def _():
                halo_up(f).wait_send()

            if owners > 2:
                @pl.when(tm > 0)
                def _():
                    for k in range(2):
                        x_copy(k, f).wait_send()


def s_up_recv(slope_win, slope_rows, s_send, s_recv, row, device):
    for side in range(2):
        pltpu.make_async_remote_copy(
            src_ref=slope_rows.at[0], dst_ref=slope_win.at[side, row],
            send_sem=s_send.at[1], recv_sem=s_recv.at[1 + side],
            device_id=device, device_id_type=MESH).wait_recv()


def in_hbm(array):
    return pltpu.with_memory_space_constraint(array, pltpu.HBM)


def per_device(mesh, innovations, obs_mask, slopes, layer_of, weight_in, weight_out):
    fronts, secs, chans, rows, win = innovations.shape
    _, half, band, _ = slopes.shape
    owners = mesh.shape["tm"]
    lats = mesh.shape["lat"]
    assert secs == 1 and band == 2 * rows and rows == 4 and owners > 1
    pair = owners == 2 and fronts > 1
    pad = round_up(chans, 16)
    rims, hid_rows = rows + 4, rows + 2

    layers = weight_in.shape[0]
    packed_rows = round_up(chans * (2 * fronts - 3) + pad, 16)
    folded_rows = round_up(3 * chans + pad, 16)
    wide = round_up(3 * pad, 128)
    deep = round_up(3 * half, 128)

    smem = pl.BlockSpec(memory_space=pltpu.SMEM)
    hbm = pl.BlockSpec(memory_space=pltpu.HBM)
    vmem = pl.BlockSpec(memory_space=pltpu.VMEM)
    out = pl.pallas_call(
        functools.partial(pair_kernel if pair else chain_kernel, (fronts, chans, rows, win, half, band, lats, owners)),
        out_shape=pltpu.VMEM((fronts * chans * rows, win), F32),
        in_specs=[smem, smem, hbm, hbm, hbm, hbm],
        out_specs=vmem,
        scratch_shapes=[
            pltpu.VMEM((fronts, chans, rows, win), BF16),
            pltpu.VMEM((half * band, win), BF16),
            pltpu.VMEM((layers, 3, 3, half, chans), BF16),
            pltpu.VMEM((layers, 3, 3, half, chans), BF16),
            pltpu.VMEM((3, 3 * half, wide), F32),
            pltpu.VMEM((3, 3 * half, 128), F32),
            pltpu.VMEM((chans * rows, win), F32),
            pltpu.VMEM((fronts, rows, pad, win), BF16),
            pltpu.VMEM((fronts, rims, pad, win), BF16),
            *([
                pltpu.VMEM((2, packed_rows, win), F32),
                pltpu.VMEM((2, packed_rows, win), BF16),
                pltpu.VMEM((folded_rows, win), F32),
                pltpu.VMEM((folded_rows, win), BF16),
            ] if pair else []),
            pltpu.VMEM((half * band, win), F32),
            pltpu.VMEM((band, half, win), BF16),
            pltpu.VMEM((2, hid_rows, half, win), BF16),
            *([
                pltpu.VMEM((2, 3 * half, wide), BF16),
                pltpu.VMEM((3 * pad, 2 * deep), BF16),
                pltpu.VMEM((2, 3 * pad, rims * win), BF16),
                pltpu.VMEM((fronts, 6 * half, rims * win), F32),
                pltpu.VMEM((2, 2 * deep, hid_rows * win), BF16),
            ] if pair else [
                pltpu.VMEM((3 * half, wide), BF16),
                pltpu.VMEM((3 * pad, 3 * half), BF16),
                pltpu.VMEM((3 * half, wide), BF16),
                pltpu.VMEM((3 * pad, 3 * half), BF16),
                pltpu.VMEM((2, 3 * pad, rims * win), BF16),
                pltpu.VMEM((2, 2, 3 * half, rims * win), F32),
                pltpu.VMEM((2, 2, 3 * half, hid_rows * win), BF16),
            ]),
            pltpu.SemaphoreType.DMA((fronts,)),
            pltpu.SemaphoreType.DMA((3,)),
            pltpu.SemaphoreType.DMA((2, fronts)),
            pltpu.SemaphoreType.DMA((2, fronts)),
            *([pltpu.SemaphoreType.DMA((2,))] * 2 if pair else []),
            pltpu.SemaphoreType.DMA((2, fronts)),
            pltpu.SemaphoreType.DMA((2, fronts)),
            pltpu.SemaphoreType.DMA((2,)),
            pltpu.SemaphoreType.DMA((2,)),
            pltpu.SemaphoreType.DMA((5,)),
            pltpu.SemaphoreType.DMA((3,)),
            *([pltpu.SemaphoreType.DMA((2,))] * 2 + [pltpu.SemaphoreType.REGULAR] if pair else []),
        ],
        compiler_params=pltpu.CompilerParams(
            collective_id=0, has_side_effects=True, vmem_limit_bytes=32 * 1024 * 1024
        ),
    )(
        in_hbm(layer_of),
        in_hbm(obs_mask.reshape(obs_mask.shape[-1])),
        in_hbm(innovations.reshape(fronts, chans, rows, win)),
        in_hbm(slopes.reshape(half * band, win)),
        in_hbm(weight_in.swapaxes(3, 4)),
        in_hbm(weight_out),
    )
    return out.reshape(innovations.shape)


def solution(mesh):
    return jax.shard_map(
        functools.partial(per_device, mesh),
        mesh=mesh,
        in_specs=(
            P(None, ("grp", "tm"), None, ("lat", "chan"), None),
            P(("grp", "tm"), ("lat", "chan"), None),
            P(("grp", "tm"), "chan", "lat", None),
            P(),
            P(None, None, None, None, "chan"),
            P(None, None, None, "chan", None),
        ),
        out_specs=P(None, ("grp", "tm"), None, ("lat", "chan"), None),
        check_vma=False,
    )
```

```python
import functools

import jax
import jax.numpy as jnp
from jax import lax
from jax.experimental import pallas as pl
from jax.experimental.pallas import tpu as pltpu
from jax.sharding import PartitionSpec as P

MESH = pl.DeviceIdType.MESH
BF16 = jnp.bfloat16
F32 = jnp.float32


def round_up(n, m):
    return -(-n // m) * m


def pair_kernel(dims, layer_ref, mask_ref, inn_hbm, slopes_hbm, w_in_hbm, w_out_hbm, out_ref,
                inn_ref, slopes_ref, w_in_ref, w_out_ref, w_wide, w_tall,
                raw, frc, adj, res, slope_f32, slope_rows, slope_win, w1_ref, w2_ref, vs, hs, ss, load_inn, load_rest,
                x_send, x_recv, r_send, r_recv, h_send, h_recv, w_send, w_recv, s_send, s_recv,
                t_send, t_recv, above):
    fronts, chans, rows, win, half, band, lats, owners = dims
    pad = frc.shape[2]
    rims = rows + 4
    hid_rows = rows + 2
    far = fronts - 1
    deep = w2_ref.shape[1] // 2
    grp = lax.axis_index("grp")
    lat = lax.axis_index("lat")
    tm = lax.axis_index("tm")
    core = lax.axis_index("chan")

    def dev(lat_no, tm_no, core_no):
        return (grp, lat_no, tm_no, core_no)

    partner = dev(lat, tm, 1 - core)
    opposite = dev(lat, 1 - tm, core)
    has_down = lat > 0
    has_up = lat < lats - 1
    first = (lat == 0) & (core == 0)
    final = (lat == lats - 1) & (core == 1)
    not_first = jnp.logical_not(first)
    not_final = jnp.logical_not(final)

    barrier = pltpu.get_barrier_semaphore()

    def greet(device):
        pl.semaphore_signal(barrier, inc=1, device_id=device, device_id_type=MESH)

    greet(opposite)

    @pl.when(has_up)
    def _():
        greet(dev(lat + 1, tm, 0))

        @pl.when(core == 1)
        def _():
            greet(dev(lat + 1, tm, 1))

        @pl.when(tm == 0)
        def _():
            greet(dev(lat + 1, 1, 0))

        @pl.when((tm == 1) & (core == 1))
        def _():
            greet(dev(lat + 1, 0, 0))
            greet(dev(lat + 1, 0, 1))

    greet(partner)
    below = has_down.astype(jnp.int32)

    def enter():
        pl.semaphore_wait(barrier, 2 + below * (2 - core + (1 - tm) + 2 * tm * (1 - core)))

        @pl.when(has_down & (core == 0))
        def _():
            for c in range(2):
                pl.semaphore_signal(above, inc=1, device_id=dev(lat - 1, tm, c), device_id_type=MESH)

        @pl.when(has_down & (core == 0) & (tm == 1))
        def _():
            for c in range(2):
                pl.semaphore_signal(above, inc=1, device_id=dev(lat - 1, 0, c), device_id_type=MESH)

    def wait_above():
        @pl.when(has_up)
        def _():
            pl.semaphore_wait(above, 2 - tm)

    def inn_copy(f):
        return pltpu.make_async_copy(inn_hbm.at[f], inn_ref.at[f], load_inn.at[f])

    loads = [
        pltpu.make_async_copy(slopes_hbm, slopes_ref, load_rest.at[0]),
        pltpu.make_async_copy(w_out_hbm, w_out_ref, load_rest.at[1]),
        pltpu.make_async_copy(w_in_hbm, w_in_ref, load_rest.at[2]),
    ]

    lane = lax.broadcasted_iota(jnp.int32, (1, win), 1)
    tiles = mask_ref.shape[0]
    width = win // tiles
    spread = jnp.zeros((1, win), F32)
    for k in range(tiles):
        spread = jnp.where(lane // width == k, mask_ref[k].astype(F32), spread)

    def load_raw(f):
        raw[...] = inn_ref[f].astype(F32).reshape(chans * rows, win)

    def forcing_row(r):
        return raw[pl.ds(r, chans, stride=rows), :] * spread

    def put_out(f, r, value):
        out_ref[pl.ds(f * (chans * rows) + r, chans, stride=rows), :] = value

    starts = (core * 2, (1 - core) * 2)

    def x_copy(k, f):
        part = adj.at[f, pl.ds(2 + starts[k], 2)]
        return pltpu.make_async_remote_copy(
            src_ref=part, dst_ref=part, send_sem=x_send.at[k, f], recv_sem=x_recv.at[k, f],
            device_id=opposite, device_id_type=MESH)

    def r_copy(k):
        part = res.at[pl.ds(2 * k, 2)]
        return pltpu.make_async_remote_copy(
            src_ref=part, dst_ref=part, send_sem=r_send.at[k], recv_sem=r_recv.at[k],
            device_id=opposite, device_id_type=MESH)

    spans = ((3 - 3 * core, 5), (5 * core, 3))

    def t_copy(k):
        part = slope_rows.at[pl.ds(*spans[k])]
        return pltpu.make_async_remote_copy(
            src_ref=part, dst_ref=part, send_sem=t_send.at[k], recv_sem=t_recv.at[k],
            device_id=opposite, device_id_type=MESH)

    def halo_down(f):
        return pltpu.make_async_remote_copy(
            src_ref=adj.at[f, pl.ds(2, 2)], dst_ref=adj.at[f, pl.ds(rims - 2, 2)],
            send_sem=h_send.at[0, f], recv_sem=h_recv.at[0, f],
            device_id=dev(lat - (1 - core), tm, 1 - core), device_id_type=MESH)

    def halo_up(f):
        return pltpu.make_async_remote_copy(
            src_ref=adj.at[f, pl.ds(rows, 2)], dst_ref=adj.at[f, pl.ds(0, 2)],
            send_sem=h_send.at[1, f], recv_sem=h_recv.at[1, f],
            device_id=dev(lat + core, tm, 1 - core), device_id_type=MESH)

    def pass_on(k, f):
        @pl.when(not_first & (core == k))
        def _():
            halo_down(f).start()

        @pl.when(not_final & (core == 1 - k))
        def _():
            halo_up(f).start()

    def halos_here(f):
        @pl.when(not_final)
        def _():
            halo_down(f).wait_recv()

        @pl.when(not_first)
        def _():
            halo_up(f).wait_recv()

    def halos_sent(f):
        @pl.when(not_first)
        def _():
            halo_down(f).wait_send()

        @pl.when(not_final)
        def _():
            halo_up(f).wait_send()

    w1_copy = pltpu.make_async_remote_copy(
        src_ref=w1_ref.at[0], dst_ref=w1_ref.at[1], send_sem=w_send.at[0], recv_sem=w_recv.at[0],
        device_id=partner, device_id_type=MESH)
    w2_copy = pltpu.make_async_remote_copy(
        src_ref=w2_ref.at[:, pl.ds(0, deep)], dst_ref=w2_ref.at[:, pl.ds(deep, deep)],
        send_sem=w_send.at[1], recv_sem=w_recv.at[1],
        device_id=partner, device_id_type=MESH)
    own = hid_rows - 1
    mine_from = core * (rows - 1)
    partner_from = (1 - core) * (rows - 1)
    s_copy = pltpu.make_async_remote_copy(
        src_ref=slope_rows.at[pl.ds(partner_from, own)],
        dst_ref=slope_win.at[1, pl.ds(core, own)],
        send_sem=s_send.at[0], recv_sem=s_recv.at[0],
        device_id=partner, device_id_type=MESH)

    def s_down(to, k):
        return pltpu.make_async_remote_copy(
            src_ref=slope_rows.at[0], dst_ref=slope_win.at[1 - core, hid_rows - 1],
            send_sem=s_send.at[1 + k], recv_sem=s_recv.at[1 + (1 - core)],
            device_id=dev(lat - 1, to, 1), device_id_type=MESH)

    def s_up(to, k):
        return pltpu.make_async_remote_copy(
            src_ref=slope_rows.at[band - 1], dst_ref=slope_win.at[core, 0],
            send_sem=s_send.at[3 + k], recv_sem=s_recv.at[1 + core],
            device_id=dev(lat + 1, to, 0), device_id_type=MESH)

    def slope_down(act, to):
        @pl.when(has_down)
        def _():
            act(s_down(to, to))

    def slope_up(act, to):
        @pl.when(has_up)
        def _():
            act(s_up(to, to))

    def start(copy):
        copy.start()

    def slopes_here():
        s_copy.wait_recv()

        @pl.when(has_down & (core == 0))
        def _():
            s_up_recv(slope_win, slope_rows, s_send, s_recv, 0, partner)

        @pl.when(has_up & (core == 1))
        def _():
            s_up_recv(slope_win, slope_rows, s_send, s_recv, hid_rows - 1, partner)

    def own_slopes():
        slope_win[0, pl.ds(1 - core, own)] = slope_rows[pl.ds(mine_from, own)]

    def all_sent():
        w1_copy.wait_send()
        w2_copy.wait_send()
        s_copy.wait_send()

    def clear_rims():
        @pl.when(first)
        def _():
            slope_win[:, 0] = jnp.zeros((2, half, win), BF16)
            for f in range(fronts):
                adj[f, 0:2] = jnp.zeros((2, pad, win), BF16)

        @pl.when(final)
        def _():
            slope_win[:, hid_rows - 1] = jnp.zeros((2, half, win), BF16)
            for f in range(fronts):
                adj[f, rims - 2:rims] = jnp.zeros((2, pad, win), BF16)

    def prepare_weights():
        w_wide[...] = jnp.zeros_like(w_wide)
        w_tall[...] = jnp.zeros_like(w_tall)
        if deep > 3 * half:
            w2_ref[:, 3 * half:deep] = jnp.zeros((3 * pad, deep - 3 * half), BF16)
            for side in range(2):
                ss[:, side * deep + 3 * half:(side + 1) * deep] = jnp.zeros(
                    (2, deep - 3 * half, hid_rows * win), BF16)
        layer = layer_ref[0]
        loads[1].wait()
        for a in range(3):
            for b in range(3):
                w_wide[b, a * half:(a + 1) * half, 0:chans] = w_out_ref[layer, a, b].astype(F32)
        wide = w_wide[0] + pltpu.roll(w_wide[1], pad, 1) + pltpu.roll(w_wide[2], 2 * pad, 1)
        w1_ref[0] = wide.astype(BF16)
        loads[2].wait()
        for a in range(3):
            for b in range(3):
                w_tall[a, b * half:(b + 1) * half, 0:chans] = w_in_ref[layer, a, b].astype(F32)
        for a in range(3):
            w2_ref[a * pad:(a + 1) * pad, 0:3 * half] = w_tall[a].T[0:pad].astype(BF16)

    left_edge = lane == 0
    right_edge = lane == win - 1

    def shifts(x):
        ahead = jnp.where(right_edge, 0.0, pltpu.roll(x, win - 1, 1))
        behind = jnp.where(left_edge, 0.0, pltpu.roll(x, 1, 1))
        return ahead.astype(BF16), x.astype(BF16), behind.astype(BF16)

    place = [*range(rows, rows + 2), *range(rows), *range(rows + 2, rims)]

    def columns(row):
        return slice(place[row] * win, (place[row] + 1) * win)

    def spread_rows(f, row_nos):
        for r in row_nos:
            for b, part in enumerate(shifts(adj[f, r].astype(F32))):
                vs[f % 2, b * pad:(b + 1) * pad, columns(r)] = part

    def first_conv(f, low, high):
        part = slice(low * win, high * win)
        both = w1_ref[...].reshape(6 * half, w1_ref.shape[2])
        hs[f % 2, :, part] = jnp.dot(both[:, 0:3 * pad], vs[f % 2, :, part], preferred_element_type=F32)

    def begin(f):
        spread_rows(f, range(2, rows + 2))
        first_conv(f, 0, rows)

    def rim_conv(f):
        spread_rows(f, (0, 1, rims - 2, rims - 1))
        first_conv(f, rows, rims)

    def rest(f):
        for side in range(2):
            for p in range(hid_rows):
                grad = sum(hs[f % 2, (3 * side + a) * half:(3 * side + a + 1) * half, columns(p + 2 - a)]
                           for a in range(3))
                scaled = (slope_win[side, p].astype(F32) * grad).astype(BF16).astype(F32)
                for b, part in enumerate(shifts(scaled)):
                    low = side * deep + b * half
                    ss[f % 2, low:low + half, p * win:(p + 1) * win] = part
        totals = [adj[f, r + 2].astype(F32) for r in range(rows)]
        for p in range(0, hid_rows, 2):
            offsets = [a for a in range(3) if p - 1 + a >= 0 and p - 2 + a < rows]
            first, count = offsets[0], len(offsets)
            g = jnp.dot(w2_ref[first * pad:(first + count) * pad, :], ss[f % 2, :, p * win:(p + 2) * win],
                        preferred_element_type=F32)
            for a in offsets:
                for step in range(2):
                    r = p + step - 2 + a
                    if 0 <= r < rows:
                        totals[r] = totals[r] + g[(a - first) * pad:(a - first + 1) * pad, step * win:(step + 1) * win]
        return totals

    @pl.when(tm == 1)
    def _():
        for f in range(fronts):
            inn_copy(f).start()
        for load in loads[1:]:
            load.start()
        clear_rims()
        if pad > chans:
            for f in range(fronts):
                for r in range(rows):
                    adj[f, r + 2, chans:pad, :] = jnp.zeros((pad - chans, win), BF16)

        def take(f):
            inn_copy(f).wait()
            load_raw(f)
            for r in range(rows):
                adj[f, r + 2, 0:chans, :] = forcing_row(r).astype(BF16)

        take(0)
        enter()
        x_copy(0, 0).start()

        @pl.when(core == 1)
        def _():
            x_copy(0, 0).wait_send()

        for f in range(1, far):
            take(f)
            x_copy(0, f).start()
        for f in range(far):
            x_copy(1, f).start()
        take(far)

        @pl.when(not_first)
        def _():
            halo_down(far).start()

        @pl.when(not_final & (core == 0))
        def _():
            halo_up(far).start()

        prepare_weights()
        w1_copy.start()
        w2_copy.start()
        wait_above()

        @pl.when(not_final & (core == 1))
        def _():
            halo_up(far).start()

        for f in range(fronts):
            for r in range(rows):
                put_out(f, r, adj[f, r + 2, 0:chans, :].astype(F32))

        w1_copy.wait_recv()
        begin(far)
        t_copy(0).wait_recv()
        s_copy.start()
        halos_here(far)
        rim_conv(far)
        w2_copy.wait_recv()
        t_copy(1).wait_recv()
        own_slopes()
        slopes_here()
        for r, value in enumerate(rest(far)):
            res[r] = value.astype(BF16)
        r_copy(0).start()

        @pl.when(core == 1)
        def _():
            r_copy(0).wait_send()

        r_copy(1).start()

        all_sent()
        halos_sent(far)
        @pl.when(core == 0)
        def _():
            x_copy(0, 0).wait_send()

        for k in range(2):
            for f in range(1 - k, far):
                x_copy(k, f).wait_send()

        @pl.when(core == 0)
        def _():
            r_copy(0).wait_send()

        r_copy(1).wait_send()

    @pl.when(tm == 0)
    def _():
        for load in loads:
            load.start()
        for f in range(fronts):
            inn_copy(f).start()
        clear_rims()

        loads[0].wait()
        slope_f32[...] = slopes_ref[...].astype(F32)
        for r in range(band):
            slope_rows[r] = slope_f32[pl.ds(r, half, stride=band), :].astype(BF16)
        enter()
        slope_down(start, 1)
        t_copy(0).start()

        @pl.when(core == 0)
        def _():
            t_copy(1).start()

        slope_down(start, 0)
        s_copy.start()
        own_slopes()
        prepare_weights()

        @pl.when(core == 1)
        def _():
            t_copy(1).start()

        wait_above()
        slope_up(start, 1)
        slope_up(start, 0)
        w1_copy.start()
        w2_copy.start()

        for f in range(fronts):
            inn_copy(f).wait()
            load_raw(f)
            for r in range(rows):
                frc[f, r, 0:chans, :] = forcing_row(r).astype(BF16)

        for f in range(far):
            x_copy(0, f).wait_recv()
            pass_on(0, f)

        w1_copy.wait_recv()
        w2_copy.wait_recv()
        slopes_here()

        def finish(f):
            halos_here(f)
            rim_conv(f)
            for r, value in enumerate(rest(f)):
                put_out(f, r, value[0:chans] + frc[f, r, 0:chans, :].astype(F32))

        for f in range(far):
            x_copy(1, f).wait_recv()
            pass_on(1, f)
            if f > 0:
                finish(f - 1)
            begin(f)
        finish(far - 1)

        for k in range(2):
            r_copy(k).wait_recv()
            for r in (2 * k, 2 * k + 1):
                put_out(far, r, res[r, 0:chans, :].astype(F32) + frc[far, r, 0:chans, :].astype(F32))

        all_sent()
        for f in range(far):
            halos_sent(f)
        for k in range(2):
            t_copy(k).wait_send()
            slope_down(lambda copy: copy.wait_send(), k)
            slope_up(lambda copy: copy.wait_send(), k)


def chain_kernel(dims, layer_ref, mask_ref, inn_hbm, slopes_hbm, w_in_hbm, w_out_hbm, out_ref,
           inn_ref, slopes_ref, w_in_ref, w_out_ref, w_wide, w_tall,
           raw, send_x, adj, slope_f32, slope_rows, slope_win, w1_ref, w2_ref, w1_other,
           w2_other, vs, hs, ss, load_inn, load_rest,
           x_send, x_recv, h_send, h_recv, w_send, w_recv, s_send, s_recv):
    fronts, chans, rows, win, half, band, lats, owners = dims
    pad = send_x.shape[2]
    rims = rows + 4
    hid_rows = rows + 2
    grp = lax.axis_index("grp")
    lat = lax.axis_index("lat")
    tm = lax.axis_index("tm")
    core = lax.axis_index("chan")
    last = owners - 1

    def dev(lat_no, tm_no, core_no):
        return (grp, lat_no, tm_no, core_no)

    barrier = pltpu.get_barrier_semaphore()

    def greet(device):
        pl.semaphore_signal(barrier, inc=1, device_id=device, device_id_type=MESH)

    def inn_copy(f):
        return pltpu.make_async_copy(inn_hbm.at[f], inn_ref.at[f], load_inn.at[f])

    for f in range(fronts):
        inn_copy(f).start()

    lane = lax.broadcasted_iota(jnp.int32, (1, win), 1)
    tiles = mask_ref.shape[0]
    width = win // tiles
    spread = jnp.zeros((1, win), F32)
    for k in range(tiles):
        spread = jnp.where(lane // width == k, mask_ref[k].astype(F32), spread)

    def load_raw(f):
        raw[...] = inn_ref[f].astype(F32).reshape(chans * rows, win)

    def forcing_row(r):
        return raw[pl.ds(r, chans, stride=rows), :] * spread

    def put_out(f, r, value):
        out_ref[pl.ds(f * (chans * rows) + r, chans, stride=rows), :] = value

    starts = (core * 2, (1 - core) * 2)

    def x_copy(k, f):
        return pltpu.make_async_remote_copy(
            src_ref=send_x.at[f, pl.ds(starts[k], 2)], dst_ref=adj.at[f, pl.ds(2 + starts[k], 2)],
            send_sem=x_send.at[k, f], recv_sem=x_recv.at[k, f],
            device_id=dev(lat, lax.rem(tm + owners - 1, owners), core), device_id_type=MESH)

    def put_send(f, r, value):
        send_x[f, r, 0:chans, :] = value.astype(BF16)

    def clear_send():
        if pad > chans:
            for f in range(fronts):
                for r in range(rows):
                    send_x[f, r, chans:pad, :] = jnp.zeros((pad - chans, win), BF16)

    @pl.when(tm == last)
    def _():
        greet(dev(lat, tm - 1, core))
        clear_send()

        for f in range(fronts):
            inn_copy(f).wait()
            load_raw(f)
            for r in range(rows):
                value = forcing_row(r)
                put_out(f, r, value)
                put_send(f, r, value)
            if f == 0:
                pl.semaphore_wait(barrier, 1)
            x_copy(0, f).start()

        for f in range(fronts):
            x_copy(1, f).start()
        for f in range(fronts):
            for k in range(2):
                x_copy(k, f).wait_send()

    @pl.when(tm < last)
    def _():
        has_down = lat > 0
        has_up = lat < lats - 1
        greet(dev(lat, tm + 1, core))
        greet(dev(lat, tm, 1 - core))

        @pl.when(has_down)
        def _():
            greet(dev(lat - 1, tm, 0))
            greet(dev(lat - 1, tm, 1))

        @pl.when(has_up)
        def _():
            greet(dev(lat + 1, tm, 0))
            greet(dev(lat + 1, tm, 1))

        greeted = 2 + 2 * has_down.astype(jnp.int32) + 2 * has_up.astype(jnp.int32)
        if owners > 2:
            @pl.when(tm > 0)
            def _():
                greet(dev(lat, tm - 1, core))
            greeted = greeted + (tm > 0).astype(jnp.int32)
        clear_send()

        loads = [
            pltpu.make_async_copy(slopes_hbm, slopes_ref, load_rest.at[0]),
            pltpu.make_async_copy(w_out_hbm, w_out_ref, load_rest.at[1]),
            pltpu.make_async_copy(w_in_hbm, w_in_ref, load_rest.at[2]),
        ]
        for load in loads:
            load.start()
        w_wide[...] = jnp.zeros_like(w_wide)
        w_tall[...] = jnp.zeros_like(w_tall)

        loads[0].wait()
        slope_f32[...] = slopes_ref[...].astype(F32)
        for r in range(band):
            slope_rows[r] = slope_f32[pl.ds(r, half, stride=band), :].astype(BF16)

        first = (lat == 0) & (core == 0)
        final = (lat == lats - 1) & (core == 1)

        @pl.when(first)
        def _():
            slope_win[:, 0] = jnp.zeros((2, half, win), BF16)
            for f in range(fronts):
                adj[f, 0:2] = jnp.zeros((2, pad, win), BF16)

        @pl.when(final)
        def _():
            slope_win[:, hid_rows - 1] = jnp.zeros((2, half, win), BF16)
            for f in range(fronts):
                adj[f, rims - 2:rims] = jnp.zeros((2, pad, win), BF16)

        layer = layer_ref[tm]
        loads[1].wait()
        for a in range(3):
            for b in range(3):
                w_wide[b, a * half:(a + 1) * half, 0:chans] = w_out_ref[layer, a, b].astype(F32)
        wide = w_wide[0] + pltpu.roll(w_wide[1], pad, 1) + pltpu.roll(w_wide[2], 2 * pad, 1)
        w1_ref[...] = wide.astype(BF16)
        loads[2].wait()
        for a in range(3):
            for b in range(3):
                w_tall[a, b * half:(b + 1) * half, 0:chans] = w_in_ref[layer, a, b].astype(F32)
        for a in range(3):
            w2_ref[a * pad:(a + 1) * pad, :] = w_tall[a].T[0:pad].astype(BF16)

        pl.semaphore_wait(barrier, greeted)

        partner = dev(lat, tm, 1 - core)
        w1_copy = pltpu.make_async_remote_copy(
            src_ref=w1_ref, dst_ref=w1_other, send_sem=w_send.at[0], recv_sem=w_recv.at[0],
            device_id=partner, device_id_type=MESH)
        w2_copy = pltpu.make_async_remote_copy(
            src_ref=w2_ref, dst_ref=w2_other, send_sem=w_send.at[1], recv_sem=w_recv.at[1],
            device_id=partner, device_id_type=MESH)
        own = hid_rows - 1
        mine_from = core * (rows - 1)
        partner_from = (1 - core) * (rows - 1)
        s_copy = pltpu.make_async_remote_copy(
            src_ref=slope_rows.at[pl.ds(partner_from, own)],
            dst_ref=slope_win.at[1, pl.ds(core, own)],
            send_sem=s_send.at[0], recv_sem=s_recv.at[0],
            device_id=partner, device_id_type=MESH)
        s_down = pltpu.make_async_remote_copy(
            src_ref=slope_rows.at[0], dst_ref=slope_win.at[1 - core, hid_rows - 1],
            send_sem=s_send.at[1], recv_sem=s_recv.at[1 + (1 - core)],
            device_id=dev(lat - 1, tm, 1), device_id_type=MESH)
        s_up = pltpu.make_async_remote_copy(
            src_ref=slope_rows.at[band - 1], dst_ref=slope_win.at[core, 0],
            send_sem=s_send.at[2], recv_sem=s_recv.at[1 + core],
            device_id=dev(lat + 1, tm, 0), device_id_type=MESH)

        w1_copy.start()
        s_copy.start()
        w2_copy.start()

        @pl.when(has_down)
        def _():
            s_down.start()

        @pl.when(has_up)
        def _():
            s_up.start()

        slope_win[0, pl.ds(1 - core, own)] = slope_rows[pl.ds(mine_from, own)]

        not_first = jnp.logical_not(first)
        not_final = jnp.logical_not(final)

        def halo_down(f):
            return pltpu.make_async_remote_copy(
                src_ref=adj.at[f, pl.ds(2, 2)], dst_ref=adj.at[f, pl.ds(rims - 2, 2)],
                send_sem=h_send.at[0, f], recv_sem=h_recv.at[0, f],
                device_id=dev(lat - (1 - core), tm, 1 - core), device_id_type=MESH)

        def halo_up(f):
            return pltpu.make_async_remote_copy(
                src_ref=adj.at[f, pl.ds(rows, 2)], dst_ref=adj.at[f, pl.ds(0, 2)],
                send_sem=h_send.at[1, f], recv_sem=h_recv.at[1, f],
                device_id=dev(lat + core, tm, 1 - core), device_id_type=MESH)

        def pass_on(k, f):
            x_copy(k, f).wait_recv()

            @pl.when(not_first & (core == k))
            def _():
                halo_down(f).start()

            @pl.when(not_final & (core == 1 - k))
            def _():
                halo_up(f).start()

        left_edge = lane == 0
        right_edge = lane == win - 1

        def shifts(x):
            ahead = jnp.where(right_edge, 0.0, pltpu.roll(x, win - 1, 1))
            behind = jnp.where(left_edge, 0.0, pltpu.roll(x, 1, 1))
            return ahead.astype(BF16), x.astype(BF16), behind.astype(BF16)

        def spread_rows(f, row_nos):
            for r in row_nos:
                for b, part in enumerate(shifts(adj[f, r].astype(F32))):
                    vs[f % 2, b * pad:(b + 1) * pad, r * win:(r + 1) * win] = part

        def first_conv(f, low, high):
            columns = slice(low * win, high * win)
            for side, w_ref in enumerate((w1_ref, w1_other)):
                hs[f % 2, side, :, columns] = jnp.dot(
                    w_ref[:, 0:3 * pad], vs[f % 2, :, columns], preferred_element_type=F32)

        def compute(f):
            spread_rows(f, (0, 1, rims - 2, rims - 1))
            first_conv(f, 0, 2)
            first_conv(f, rims - 2, rims)
            for side in range(2):
                for p in range(hid_rows):
                    grad = sum(hs[f % 2, side, a * half:(a + 1) * half, (p + 2 - a) * win:(p + 3 - a) * win]
                               for a in range(3))
                    scaled = (slope_win[side, p].astype(F32) * grad).astype(BF16).astype(F32)
                    for b, part in enumerate(shifts(scaled)):
                        ss[f % 2, side, b * half:(b + 1) * half, p * win:(p + 1) * win] = part
            g = (jnp.dot(w2_ref[...], ss[f % 2, 0], preferred_element_type=F32)
                 + jnp.dot(w2_other[...], ss[f % 2, 1], preferred_element_type=F32))
            for r in range(rows):
                total = sum(g[a * pad:(a + 1) * pad, (r + 2 - a) * win:(r + 3 - a) * win]
                            for a in range(3))
                value = adj[f, r + 2].astype(F32) + total + send_x[f, r].astype(F32)
                value = value[0:chans]
                put_out(f, r, value)
                if owners > 2:
                    put_send(f, r, value)

        def finish(pair):
            for f in pair:
                @pl.when(not_final)
                def _():
                    halo_down(f).wait_recv()

                @pl.when(not_first)
                def _():
                    halo_up(f).wait_recv()

            for f in pair:
                compute(f)
            if owners > 2:
                @pl.when(tm > 0)
                def _():
                    for f in pair:
                        for k in range(2):
                            x_copy(k, f).start()

        for f in range(fronts):
            inn_copy(f).wait()
            load_raw(f)
            for r in range(rows):
                put_send(f, r, forcing_row(r))

        def begin(f):
            spread_rows(f, range(2, rows + 2))
            first_conv(f, 2, rows + 2)

        w1_copy.wait_recv()
        w2_copy.wait_recv()
        s_copy.wait_recv()

        @pl.when(has_down & (core == 0))
        def _():
            s_up_recv(slope_win, slope_rows, s_send, s_recv, 0, dev(lat, tm, 1 - core))

        @pl.when(has_up & (core == 1))
        def _():
            s_up_recv(slope_win, slope_rows, s_send, s_recv, hid_rows - 1, dev(lat, tm, 1 - core))

        @pl.loop(0, fronts)
        def _(f):
            pass_on(0, f)

        waiting = []
        for f in range(fronts):
            pass_on(1, f)
            if len(waiting) == 1:
                finish(waiting)
                waiting = []
            begin(f)
            waiting.append(f)
        finish(waiting)

        w1_copy.wait_send()
        w2_copy.wait_send()
        s_copy.wait_send()

        @pl.when(has_down)
        def _():
            s_down.wait_send()

        @pl.when(has_up)
        def _():
            s_up.wait_send()

        @pl.loop(0, fronts)
        def _(f):
            @pl.when(not_first)
            def _():
                halo_down(f).wait_send()

            @pl.when(not_final)
            def _():
                halo_up(f).wait_send()

            if owners > 2:
                @pl.when(tm > 0)
                def _():
                    for k in range(2):
                        x_copy(k, f).wait_send()


def s_up_recv(slope_win, slope_rows, s_send, s_recv, row, device):
    for side in range(2):
        pltpu.make_async_remote_copy(
            src_ref=slope_rows.at[0], dst_ref=slope_win.at[side, row],
            send_sem=s_send.at[1], recv_sem=s_recv.at[1 + side],
            device_id=device, device_id_type=MESH).wait_recv()


def in_hbm(array):
    return pltpu.with_memory_space_constraint(array, pltpu.HBM)


def per_device(mesh, innovations, obs_mask, slopes, layer_of, weight_in, weight_out):
    fronts, secs, chans, rows, win = innovations.shape
    _, half, band, _ = slopes.shape
    owners = mesh.shape["tm"]
    lats = mesh.shape["lat"]
    assert secs == 1 and band == 2 * rows and rows == 4 and owners > 1
    pair = owners == 2 and fronts > 1
    pad = round_up(chans, 16)
    rims, hid_rows = rows + 4, rows + 2

    layers = weight_in.shape[0]
    wide = round_up(3 * pad, 128)
    deep = round_up(3 * half, 128)

    smem = pl.BlockSpec(memory_space=pltpu.SMEM)
    hbm = pl.BlockSpec(memory_space=pltpu.HBM)
    vmem = pl.BlockSpec(memory_space=pltpu.VMEM)
    out = pl.pallas_call(
        functools.partial(pair_kernel if pair else chain_kernel, (fronts, chans, rows, win, half, band, lats, owners)),
        out_shape=pltpu.VMEM((fronts * chans * rows, win), F32),
        in_specs=[smem, smem, hbm, hbm, hbm, hbm],
        out_specs=vmem,
        scratch_shapes=[
            pltpu.VMEM((fronts, chans, rows, win), BF16),
            pltpu.VMEM((half * band, win), BF16),
            pltpu.VMEM((layers, 3, 3, half, chans), BF16),
            pltpu.VMEM((layers, 3, 3, half, chans), BF16),
            pltpu.VMEM((3, 3 * half, wide), F32),
            pltpu.VMEM((3, 3 * half, 128), F32),
            pltpu.VMEM((chans * rows, win), F32),
            pltpu.VMEM((fronts, rows, pad, win), BF16),
            pltpu.VMEM((fronts, rims, pad, win), BF16),
            *([pltpu.VMEM((rows, pad, win), BF16)] if pair else []),
            pltpu.VMEM((half * band, win), F32),
            pltpu.VMEM((band, half, win), BF16),
            pltpu.VMEM((2, hid_rows, half, win), BF16),
            *([
                pltpu.VMEM((2, 3 * half, wide), BF16),
                pltpu.VMEM((3 * pad, 2 * deep), BF16),
                pltpu.VMEM((2, 3 * pad, rims * win), BF16),
                pltpu.VMEM((2, 6 * half, rims * win), F32),
                pltpu.VMEM((2, 2 * deep, hid_rows * win), BF16),
            ] if pair else [
                pltpu.VMEM((3 * half, wide), BF16),
                pltpu.VMEM((3 * pad, 3 * half), BF16),
                pltpu.VMEM((3 * half, wide), BF16),
                pltpu.VMEM((3 * pad, 3 * half), BF16),
                pltpu.VMEM((2, 3 * pad, rims * win), BF16),
                pltpu.VMEM((2, 2, 3 * half, rims * win), F32),
                pltpu.VMEM((2, 2, 3 * half, hid_rows * win), BF16),
            ]),
            pltpu.SemaphoreType.DMA((fronts,)),
            pltpu.SemaphoreType.DMA((3,)),
            pltpu.SemaphoreType.DMA((2, fronts)),
            pltpu.SemaphoreType.DMA((2, fronts)),
            *([pltpu.SemaphoreType.DMA((2,))] * 2 if pair else []),
            pltpu.SemaphoreType.DMA((2, fronts)),
            pltpu.SemaphoreType.DMA((2, fronts)),
            pltpu.SemaphoreType.DMA((2,)),
            pltpu.SemaphoreType.DMA((2,)),
            pltpu.SemaphoreType.DMA((5,)),
            pltpu.SemaphoreType.DMA((3,)),
            *([pltpu.SemaphoreType.DMA((2,))] * 2 + [pltpu.SemaphoreType.REGULAR] if pair else []),
        ],
        compiler_params=pltpu.CompilerParams(
            collective_id=0, has_side_effects=True, vmem_limit_bytes=32 * 1024 * 1024
        ),
    )(
        in_hbm(layer_of),
        in_hbm(obs_mask.reshape(obs_mask.shape[-1])),
        in_hbm(innovations.reshape(fronts, chans, rows, win)),
        in_hbm(slopes.reshape(half * band, win)),
        in_hbm(weight_in.swapaxes(3, 4)),
        in_hbm(weight_out),
    )
    return out.reshape(innovations.shape)


def solution(mesh):
    return jax.shard_map(
        functools.partial(per_device, mesh),
        mesh=mesh,
        in_specs=(
            P(None, ("grp", "tm"), None, ("lat", "chan"), None),
            P(("grp", "tm"), ("lat", "chan"), None),
            P(("grp", "tm"), "chan", "lat", None),
            P(),
            P(None, None, None, None, "chan"),
            P(None, None, None, "chan", None),
        ),
        out_specs=P(None, ("grp", "tm"), None, ("lat", "chan"), None),
        check_vma=False,
    )
```

```python
import functools

import jax
import jax.numpy as jnp
from jax import lax
from jax.experimental import pallas as pl
from jax.experimental.pallas import tpu as pltpu
from jax.sharding import PartitionSpec as P

MESH = pl.DeviceIdType.MESH
BF16 = jnp.bfloat16
F32 = jnp.float32


def round_up(n, m):
    return -(-n // m) * m


def pair_kernel(dims, layer_ref, mask_ref, inn_hbm, slopes_hbm, w_in_hbm, w_out_hbm, out_ref,
                inn_ref, slopes_ref, w_in_ref, w_out_ref, w_wide, w_tall,
                raw, frc, adj, res, slope_f32, slope_rows, slope_win, w1_ref, w2_ref, vs, hs, ss, load_inn, load_rest,
                x_send, x_recv, r_send, r_recv, h_send, h_recv, w_send, w_recv, s_send, s_recv,
                t_send, t_recv, above):
    fronts, chans, rows, win, half, band, lats, owners = dims
    pad = frc.shape[2]
    rims = rows + 4
    hid_rows = rows + 2
    far = fronts - 1
    deep = w2_ref.shape[1] // 2
    grp = lax.axis_index("grp")
    lat = lax.axis_index("lat")
    tm = lax.axis_index("tm")
    core = lax.axis_index("chan")

    def dev(lat_no, tm_no, core_no):
        return (grp, lat_no, tm_no, core_no)

    partner = dev(lat, tm, 1 - core)
    opposite = dev(lat, 1 - tm, core)
    has_down = lat > 0
    has_up = lat < lats - 1
    first = (lat == 0) & (core == 0)
    final = (lat == lats - 1) & (core == 1)
    not_first = jnp.logical_not(first)
    not_final = jnp.logical_not(final)

    barrier = pltpu.get_barrier_semaphore()

    def greet(device):
        pl.semaphore_signal(barrier, inc=1, device_id=device, device_id_type=MESH)

    greet(opposite)

    @pl.when(has_up)
    def _():
        greet(dev(lat + 1, tm, 0))

        @pl.when(core == 1)
        def _():
            greet(dev(lat + 1, tm, 1))

        @pl.when(tm == 0)
        def _():
            greet(dev(lat + 1, 1, 0))

        @pl.when((tm == 1) & (core == 1))
        def _():
            greet(dev(lat + 1, 0, 0))
            greet(dev(lat + 1, 0, 1))

    greet(partner)
    below = has_down.astype(jnp.int32)

    def enter():
        pl.semaphore_wait(barrier, 2 + below * (2 - core + (1 - tm) + 2 * tm * (1 - core)))

        @pl.when(has_down & (core == 0))
        def _():
            for c in range(2):
                pl.semaphore_signal(above, inc=1, device_id=dev(lat - 1, tm, c), device_id_type=MESH)

        @pl.when(has_down & (core == 0) & (tm == 1))
        def _():
            for c in range(2):
                pl.semaphore_signal(above, inc=1, device_id=dev(lat - 1, 0, c), device_id_type=MESH)

    def wait_above():
        @pl.when(has_up)
        def _():
            pl.semaphore_wait(above, 2 - tm)

    def inn_copy(f):
        return pltpu.make_async_copy(inn_hbm.at[f], inn_ref.at[f], load_inn.at[f])

    loads = [
        pltpu.make_async_copy(slopes_hbm, slopes_ref, load_rest.at[0]),
        pltpu.make_async_copy(w_out_hbm, w_out_ref, load_rest.at[1]),
        pltpu.make_async_copy(w_in_hbm, w_in_ref, load_rest.at[2]),
    ]

    lane = lax.broadcasted_iota(jnp.int32, (1, win), 1)
    tiles = mask_ref.shape[0]
    width = win // tiles
    spread = jnp.zeros((1, win), F32)
    for k in range(tiles):
        spread = jnp.where(lane // width == k, mask_ref[k].astype(F32), spread)

    def load_raw(f):
        raw[...] = inn_ref[f].astype(F32).reshape(chans * rows, win)

    def forcing_row(r):
        return raw[pl.ds(r, chans, stride=rows), :] * spread

    def put_out(f, r, value):
        out_ref[pl.ds(f * (chans * rows) + r, chans, stride=rows), :] = value

    starts = (core * 2, (1 - core) * 2)

    def x_copy(k, f):
        part = adj.at[f, pl.ds(2 + starts[k], 2)]
        return pltpu.make_async_remote_copy(
            src_ref=part, dst_ref=part, send_sem=x_send.at[k, f], recv_sem=x_recv.at[k, f],
            device_id=opposite, device_id_type=MESH)

    def r_copy(k):
        part = res.at[pl.ds(2 * k, 2)]
        return pltpu.make_async_remote_copy(
            src_ref=part, dst_ref=part, send_sem=r_send.at[k], recv_sem=r_recv.at[k],
            device_id=opposite, device_id_type=MESH)

    spans = ((3 - 3 * core, 5), (5 * core, 3))

    def t_copy(k):
        part = slope_rows.at[pl.ds(*spans[k])]
        return pltpu.make_async_remote_copy(
            src_ref=part, dst_ref=part, send_sem=t_send.at[k], recv_sem=t_recv.at[k],
            device_id=opposite, device_id_type=MESH)

    def halo_down(f):
        return pltpu.make_async_remote_copy(
            src_ref=adj.at[f, pl.ds(2, 2)], dst_ref=adj.at[f, pl.ds(rims - 2, 2)],
            send_sem=h_send.at[0, f], recv_sem=h_recv.at[0, f],
            device_id=dev(lat - (1 - core), tm, 1 - core), device_id_type=MESH)

    def halo_up(f):
        return pltpu.make_async_remote_copy(
            src_ref=adj.at[f, pl.ds(rows, 2)], dst_ref=adj.at[f, pl.ds(0, 2)],
            send_sem=h_send.at[1, f], recv_sem=h_recv.at[1, f],
            device_id=dev(lat + core, tm, 1 - core), device_id_type=MESH)

    def pass_on(k, f):
        @pl.when(not_first & (core == k))
        def _():
            halo_down(f).start()

        @pl.when(not_final & (core == 1 - k))
        def _():
            halo_up(f).start()

    def halos_here(f):
        @pl.when(not_final)
        def _():
            halo_down(f).wait_recv()

        @pl.when(not_first)
        def _():
            halo_up(f).wait_recv()

    def halos_sent(f):
        @pl.when(not_first)
        def _():
            halo_down(f).wait_send()

        @pl.when(not_final)
        def _():
            halo_up(f).wait_send()

    w1_copy = pltpu.make_async_remote_copy(
        src_ref=w1_ref.at[0], dst_ref=w1_ref.at[1], send_sem=w_send.at[0], recv_sem=w_recv.at[0],
        device_id=partner, device_id_type=MESH)
    w2_copy = pltpu.make_async_remote_copy(
        src_ref=w2_ref.at[:, pl.ds(0, deep)], dst_ref=w2_ref.at[:, pl.ds(deep, deep)],
        send_sem=w_send.at[1], recv_sem=w_recv.at[1],
        device_id=partner, device_id_type=MESH)
    own = hid_rows - 1
    mine_from = core * (rows - 1)
    partner_from = (1 - core) * (rows - 1)
    s_copy = pltpu.make_async_remote_copy(
        src_ref=slope_rows.at[pl.ds(partner_from, own)],
        dst_ref=slope_win.at[1, pl.ds(core, own)],
        send_sem=s_send.at[0], recv_sem=s_recv.at[0],
        device_id=partner, device_id_type=MESH)

    def s_down(to, k):
        return pltpu.make_async_remote_copy(
            src_ref=slope_rows.at[0], dst_ref=slope_win.at[1 - core, hid_rows - 1],
            send_sem=s_send.at[1 + k], recv_sem=s_recv.at[1 + (1 - core)],
            device_id=dev(lat - 1, to, 1), device_id_type=MESH)

    def s_up(to, k):
        return pltpu.make_async_remote_copy(
            src_ref=slope_rows.at[band - 1], dst_ref=slope_win.at[core, 0],
            send_sem=s_send.at[3 + k], recv_sem=s_recv.at[1 + core],
            device_id=dev(lat + 1, to, 0), device_id_type=MESH)

    def slope_down(act, to):
        @pl.when(has_down)
        def _():
            act(s_down(to, to))

    def slope_up(act, to):
        @pl.when(has_up)
        def _():
            act(s_up(to, to))

    def start(copy):
        copy.start()

    def slopes_here():
        s_copy.wait_recv()

        @pl.when(has_down & (core == 0))
        def _():
            s_up_recv(slope_win, slope_rows, s_send, s_recv, 0, partner)

        @pl.when(has_up & (core == 1))
        def _():
            s_up_recv(slope_win, slope_rows, s_send, s_recv, hid_rows - 1, partner)

    def own_slopes():
        slope_win[0, pl.ds(1 - core, own)] = slope_rows[pl.ds(mine_from, own)]

    def all_sent():
        w1_copy.wait_send()
        w2_copy.wait_send()
        s_copy.wait_send()

    def clear_rims():
        @pl.when(first)
        def _():
            slope_win[:, 0] = jnp.zeros((2, half, win), BF16)
            for f in range(fronts):
                adj[f, 0:2] = jnp.zeros((2, pad, win), BF16)

        @pl.when(final)
        def _():
            slope_win[:, hid_rows - 1] = jnp.zeros((2, half, win), BF16)
            for f in range(fronts):
                adj[f, rims - 2:rims] = jnp.zeros((2, pad, win), BF16)

    def prepare_weights():
        w_wide[...] = jnp.zeros_like(w_wide)
        w_tall[...] = jnp.zeros_like(w_tall)
        if deep > 3 * half:
            w2_ref[:, 3 * half:deep] = jnp.zeros((3 * pad, deep - 3 * half), BF16)
            for side in range(2):
                ss[:, side * deep + 3 * half:(side + 1) * deep] = jnp.zeros(
                    (2, deep - 3 * half, hid_rows * win), BF16)
        layer = layer_ref[0]
        loads[1].wait()
        for a in range(3):
            for b in range(3):
                w_wide[b, a * half:(a + 1) * half, 0:chans] = w_out_ref[layer, a, b].astype(F32)
        wide = w_wide[0] + pltpu.roll(w_wide[1], pad, 1) + pltpu.roll(w_wide[2], 2 * pad, 1)
        w1_ref[0] = wide.astype(BF16)
        loads[2].wait()
        for a in range(3):
            for b in range(3):
                w_tall[a, b * half:(b + 1) * half, 0:chans] = w_in_ref[layer, a, b].astype(F32)
        for a in range(3):
            w2_ref[a * pad:(a + 1) * pad, 0:3 * half] = w_tall[a].T[0:pad].astype(BF16)

    left_edge = lane == 0
    right_edge = lane == win - 1

    def shifts(x):
        ahead = jnp.where(right_edge, 0.0, pltpu.roll(x, win - 1, 1))
        behind = jnp.where(left_edge, 0.0, pltpu.roll(x, 1, 1))
        return ahead.astype(BF16), x.astype(BF16), behind.astype(BF16)

    place = [*range(rows, rows + 2), *range(rows), *range(rows + 2, rims)]

    def columns(row):
        return slice(place[row] * win, (place[row] + 1) * win)

    def convolve(own, rim):
        slot = own % 2 if own is not None else (rim + 1) % 2
        for f, row_nos in ((own, range(2, rows + 2)), (rim, (0, 1, rims - 2, rims - 1))):
            for r in row_nos if f is not None else ():
                for b, part in enumerate(shifts(adj[f, r].astype(F32))):
                    vs[slot, b * pad:(b + 1) * pad, columns(r)] = part
        low = 0 if own is not None else rows * win
        high = (rims if rim is not None else rows) * win
        both = w1_ref[...].reshape(6 * half, w1_ref.shape[2])
        product = jnp.dot(both[:, 0:3 * pad], vs[slot, :, low:high], preferred_element_type=F32)
        if own is not None:
            hs[own % 2, :, 0:rows * win] = product[:, 0:rows * win]
        if rim is not None:
            hs[rim % 2, :, rows * win:] = product[:, rows * win - low:]

    def rest(f):
        for side in range(2):
            for p in range(hid_rows):
                grad = sum(hs[f % 2, (3 * side + a) * half:(3 * side + a + 1) * half, columns(p + 2 - a)]
                           for a in range(3))
                scaled = (slope_win[side, p].astype(F32) * grad).astype(BF16).astype(F32)
                for b, part in enumerate(shifts(scaled)):
                    low = side * deep + b * half
                    ss[f % 2, low:low + half, p * win:(p + 1) * win] = part
        totals = [adj[f, r + 2].astype(F32) for r in range(rows)]
        for p in range(0, hid_rows, 2):
            offsets = [a for a in range(3) if p - 1 + a >= 0 and p - 2 + a < rows]
            first, count = offsets[0], len(offsets)
            g = jnp.dot(w2_ref[first * pad:(first + count) * pad, :], ss[f % 2, :, p * win:(p + 2) * win],
                        preferred_element_type=F32)
            for a in offsets:
                for step in range(2):
                    r = p + step - 2 + a
                    if 0 <= r < rows:
                        totals[r] = totals[r] + g[(a - first) * pad:(a - first + 1) * pad, step * win:(step + 1) * win]
        return totals

    @pl.when(tm == 1)
    def _():
        for f in range(fronts):
            inn_copy(f).start()
        for load in loads[1:]:
            load.start()
        clear_rims()
        if pad > chans:
            for f in range(fronts):
                for r in range(rows):
                    adj[f, r + 2, chans:pad, :] = jnp.zeros((pad - chans, win), BF16)

        def take(f):
            inn_copy(f).wait()
            load_raw(f)
            for r in range(rows):
                adj[f, r + 2, 0:chans, :] = forcing_row(r).astype(BF16)

        take(0)
        enter()
        x_copy(0, 0).start()

        @pl.when(core == 1)
        def _():
            x_copy(0, 0).wait_send()

        for f in range(1, far):
            take(f)
            x_copy(0, f).start()
        for f in range(far):
            x_copy(1, f).start()
        take(far)

        @pl.when(not_first)
        def _():
            halo_down(far).start()

        @pl.when(not_final & (core == 0))
        def _():
            halo_up(far).start()

        prepare_weights()
        w1_copy.start()
        w2_copy.start()
        wait_above()

        @pl.when(not_final & (core == 1))
        def _():
            halo_up(far).start()

        for f in range(fronts):
            for r in range(rows):
                put_out(f, r, adj[f, r + 2, 0:chans, :].astype(F32))

        w1_copy.wait_recv()
        convolve(far, None)
        t_copy(0).wait_recv()
        s_copy.start()
        halos_here(far)
        convolve(None, far)
        w2_copy.wait_recv()
        t_copy(1).wait_recv()
        own_slopes()
        slopes_here()
        for r, value in enumerate(rest(far)):
            res[r] = value.astype(BF16)
        r_copy(0).start()

        @pl.when(core == 1)
        def _():
            r_copy(0).wait_send()

        r_copy(1).start()

        all_sent()
        halos_sent(far)
        @pl.when(core == 0)
        def _():
            x_copy(0, 0).wait_send()

        for k in range(2):
            for f in range(1 - k, far):
                x_copy(k, f).wait_send()

        @pl.when(core == 0)
        def _():
            r_copy(0).wait_send()

        r_copy(1).wait_send()

    @pl.when(tm == 0)
    def _():
        for load in loads:
            load.start()
        for f in range(fronts):
            inn_copy(f).start()
        clear_rims()

        loads[0].wait()
        slope_f32[...] = slopes_ref[...].astype(F32)
        for r in range(band):
            slope_rows[r] = slope_f32[pl.ds(r, half, stride=band), :].astype(BF16)
        enter()
        slope_down(start, 1)
        t_copy(0).start()

        @pl.when(core == 0)
        def _():
            t_copy(1).start()

        slope_down(start, 0)
        s_copy.start()
        own_slopes()
        prepare_weights()

        @pl.when(core == 1)
        def _():
            t_copy(1).start()

        wait_above()
        slope_up(start, 1)
        slope_up(start, 0)
        w1_copy.start()
        w2_copy.start()

        for f in range(fronts):
            inn_copy(f).wait()
            load_raw(f)
            for r in range(rows):
                frc[f, r, 0:chans, :] = forcing_row(r).astype(BF16)

        for f in range(far):
            x_copy(0, f).wait_recv()
            pass_on(0, f)

        w1_copy.wait_recv()
        w2_copy.wait_recv()
        slopes_here()

        def finish(f, following):
            halos_here(f)
            convolve(following, f)
            for r, value in enumerate(rest(f)):
                put_out(f, r, value[0:chans] + frc[f, r, 0:chans, :].astype(F32))

        for f in range(far):
            x_copy(1, f).wait_recv()
            pass_on(1, f)
            if f > 0:
                finish(f - 1, f)
            else:
                convolve(f, None)
        finish(far - 1, None)

        for k in range(2):
            r_copy(k).wait_recv()
            for r in (2 * k, 2 * k + 1):
                put_out(far, r, res[r, 0:chans, :].astype(F32) + frc[far, r, 0:chans, :].astype(F32))

        all_sent()
        for f in range(far):
            halos_sent(f)
        for k in range(2):
            t_copy(k).wait_send()
            slope_down(lambda copy: copy.wait_send(), k)
            slope_up(lambda copy: copy.wait_send(), k)


def chain_kernel(dims, layer_ref, mask_ref, inn_hbm, slopes_hbm, w_in_hbm, w_out_hbm, out_ref,
           inn_ref, slopes_ref, w_in_ref, w_out_ref, w_wide, w_tall,
           raw, send_x, adj, slope_f32, slope_rows, slope_win, w1_ref, w2_ref, w1_other,
           w2_other, vs, hs, ss, load_inn, load_rest,
           x_send, x_recv, h_send, h_recv, w_send, w_recv, s_send, s_recv):
    fronts, chans, rows, win, half, band, lats, owners = dims
    pad = send_x.shape[2]
    rims = rows + 4
    hid_rows = rows + 2
    grp = lax.axis_index("grp")
    lat = lax.axis_index("lat")
    tm = lax.axis_index("tm")
    core = lax.axis_index("chan")
    last = owners - 1

    def dev(lat_no, tm_no, core_no):
        return (grp, lat_no, tm_no, core_no)

    barrier = pltpu.get_barrier_semaphore()

    def greet(device):
        pl.semaphore_signal(barrier, inc=1, device_id=device, device_id_type=MESH)

    def inn_copy(f):
        return pltpu.make_async_copy(inn_hbm.at[f], inn_ref.at[f], load_inn.at[f])

    for f in range(fronts):
        inn_copy(f).start()

    lane = lax.broadcasted_iota(jnp.int32, (1, win), 1)
    tiles = mask_ref.shape[0]
    width = win // tiles
    spread = jnp.zeros((1, win), F32)
    for k in range(tiles):
        spread = jnp.where(lane // width == k, mask_ref[k].astype(F32), spread)

    def load_raw(f):
        raw[...] = inn_ref[f].astype(F32).reshape(chans * rows, win)

    def forcing_row(r):
        return raw[pl.ds(r, chans, stride=rows), :] * spread

    def put_out(f, r, value):
        out_ref[pl.ds(f * (chans * rows) + r, chans, stride=rows), :] = value

    starts = (core * 2, (1 - core) * 2)

    def x_copy(k, f):
        return pltpu.make_async_remote_copy(
            src_ref=send_x.at[f, pl.ds(starts[k], 2)], dst_ref=adj.at[f, pl.ds(2 + starts[k], 2)],
            send_sem=x_send.at[k, f], recv_sem=x_recv.at[k, f],
            device_id=dev(lat, lax.rem(tm + owners - 1, owners), core), device_id_type=MESH)

    def put_send(f, r, value):
        send_x[f, r, 0:chans, :] = value.astype(BF16)

    def clear_send():
        if pad > chans:
            for f in range(fronts):
                for r in range(rows):
                    send_x[f, r, chans:pad, :] = jnp.zeros((pad - chans, win), BF16)

    @pl.when(tm == last)
    def _():
        greet(dev(lat, tm - 1, core))
        clear_send()

        for f in range(fronts):
            inn_copy(f).wait()
            load_raw(f)
            for r in range(rows):
                value = forcing_row(r)
                put_out(f, r, value)
                put_send(f, r, value)
            if f == 0:
                pl.semaphore_wait(barrier, 1)
            x_copy(0, f).start()

        for f in range(fronts):
            x_copy(1, f).start()
        for f in range(fronts):
            for k in range(2):
                x_copy(k, f).wait_send()

    @pl.when(tm < last)
    def _():
        has_down = lat > 0
        has_up = lat < lats - 1
        greet(dev(lat, tm + 1, core))
        greet(dev(lat, tm, 1 - core))

        @pl.when(has_down)
        def _():
            greet(dev(lat - 1, tm, 0))
            greet(dev(lat - 1, tm, 1))

        @pl.when(has_up)
        def _():
            greet(dev(lat + 1, tm, 0))
            greet(dev(lat + 1, tm, 1))

        greeted = 2 + 2 * has_down.astype(jnp.int32) + 2 * has_up.astype(jnp.int32)
        if owners > 2:
            @pl.when(tm > 0)
            def _():
                greet(dev(lat, tm - 1, core))
            greeted = greeted + (tm > 0).astype(jnp.int32)
        clear_send()

        loads = [
            pltpu.make_async_copy(slopes_hbm, slopes_ref, load_rest.at[0]),
            pltpu.make_async_copy(w_out_hbm, w_out_ref, load_rest.at[1]),
            pltpu.make_async_copy(w_in_hbm, w_in_ref, load_rest.at[2]),
        ]
        for load in loads:
            load.start()
        w_wide[...] = jnp.zeros_like(w_wide)
        w_tall[...] = jnp.zeros_like(w_tall)

        loads[0].wait()
        slope_f32[...] = slopes_ref[...].astype(F32)
        for r in range(band):
            slope_rows[r] = slope_f32[pl.ds(r, half, stride=band), :].astype(BF16)

        first = (lat == 0) & (core == 0)
        final = (lat == lats - 1) & (core == 1)

        @pl.when(first)
        def _():
            slope_win[:, 0] = jnp.zeros((2, half, win), BF16)
            for f in range(fronts):
                adj[f, 0:2] = jnp.zeros((2, pad, win), BF16)

        @pl.when(final)
        def _():
            slope_win[:, hid_rows - 1] = jnp.zeros((2, half, win), BF16)
            for f in range(fronts):
                adj[f, rims - 2:rims] = jnp.zeros((2, pad, win), BF16)

        layer = layer_ref[tm]
        loads[1].wait()
        for a in range(3):
            for b in range(3):
                w_wide[b, a * half:(a + 1) * half, 0:chans] = w_out_ref[layer, a, b].astype(F32)
        wide = w_wide[0] + pltpu.roll(w_wide[1], pad, 1) + pltpu.roll(w_wide[2], 2 * pad, 1)
        w1_ref[...] = wide.astype(BF16)
        loads[2].wait()
        for a in range(3):
            for b in range(3):
                w_tall[a, b * half:(b + 1) * half, 0:chans] = w_in_ref[layer, a, b].astype(F32)
        for a in range(3):
            w2_ref[a * pad:(a + 1) * pad, :] = w_tall[a].T[0:pad].astype(BF16)

        pl.semaphore_wait(barrier, greeted)

        partner = dev(lat, tm, 1 - core)
        w1_copy = pltpu.make_async_remote_copy(
            src_ref=w1_ref, dst_ref=w1_other, send_sem=w_send.at[0], recv_sem=w_recv.at[0],
            device_id=partner, device_id_type=MESH)
        w2_copy = pltpu.make_async_remote_copy(
            src_ref=w2_ref, dst_ref=w2_other, send_sem=w_send.at[1], recv_sem=w_recv.at[1],
            device_id=partner, device_id_type=MESH)
        own = hid_rows - 1
        mine_from = core * (rows - 1)
        partner_from = (1 - core) * (rows - 1)
        s_copy = pltpu.make_async_remote_copy(
            src_ref=slope_rows.at[pl.ds(partner_from, own)],
            dst_ref=slope_win.at[1, pl.ds(core, own)],
            send_sem=s_send.at[0], recv_sem=s_recv.at[0],
            device_id=partner, device_id_type=MESH)
        s_down = pltpu.make_async_remote_copy(
            src_ref=slope_rows.at[0], dst_ref=slope_win.at[1 - core, hid_rows - 1],
            send_sem=s_send.at[1], recv_sem=s_recv.at[1 + (1 - core)],
            device_id=dev(lat - 1, tm, 1), device_id_type=MESH)
        s_up = pltpu.make_async_remote_copy(
            src_ref=slope_rows.at[band - 1], dst_ref=slope_win.at[core, 0],
            send_sem=s_send.at[2], recv_sem=s_recv.at[1 + core],
            device_id=dev(lat + 1, tm, 0), device_id_type=MESH)

        w1_copy.start()
        s_copy.start()
        w2_copy.start()

        @pl.when(has_down)
        def _():
            s_down.start()

        @pl.when(has_up)
        def _():
            s_up.start()

        slope_win[0, pl.ds(1 - core, own)] = slope_rows[pl.ds(mine_from, own)]

        not_first = jnp.logical_not(first)
        not_final = jnp.logical_not(final)

        def halo_down(f):
            return pltpu.make_async_remote_copy(
                src_ref=adj.at[f, pl.ds(2, 2)], dst_ref=adj.at[f, pl.ds(rims - 2, 2)],
                send_sem=h_send.at[0, f], recv_sem=h_recv.at[0, f],
                device_id=dev(lat - (1 - core), tm, 1 - core), device_id_type=MESH)

        def halo_up(f):
            return pltpu.make_async_remote_copy(
                src_ref=adj.at[f, pl.ds(rows, 2)], dst_ref=adj.at[f, pl.ds(0, 2)],
                send_sem=h_send.at[1, f], recv_sem=h_recv.at[1, f],
                device_id=dev(lat + core, tm, 1 - core), device_id_type=MESH)

        def pass_on(k, f):
            x_copy(k, f).wait_recv()

            @pl.when(not_first & (core == k))
            def _():
                halo_down(f).start()

            @pl.when(not_final & (core == 1 - k))
            def _():
                halo_up(f).start()

        left_edge = lane == 0
        right_edge = lane == win - 1

        def shifts(x):
            ahead = jnp.where(right_edge, 0.0, pltpu.roll(x, win - 1, 1))
            behind = jnp.where(left_edge, 0.0, pltpu.roll(x, 1, 1))
            return ahead.astype(BF16), x.astype(BF16), behind.astype(BF16)

        def spread_rows(f, row_nos):
            for r in row_nos:
                for b, part in enumerate(shifts(adj[f, r].astype(F32))):
                    vs[f % 2, b * pad:(b + 1) * pad, r * win:(r + 1) * win] = part

        def first_conv(f, low, high):
            columns = slice(low * win, high * win)
            for side, w_ref in enumerate((w1_ref, w1_other)):
                hs[f % 2, side, :, columns] = jnp.dot(
                    w_ref[:, 0:3 * pad], vs[f % 2, :, columns], preferred_element_type=F32)

        def compute(f):
            spread_rows(f, (0, 1, rims - 2, rims - 1))
            first_conv(f, 0, 2)
            first_conv(f, rims - 2, rims)
            for side in range(2):
                for p in range(hid_rows):
                    grad = sum(hs[f % 2, side, a * half:(a + 1) * half, (p + 2 - a) * win:(p + 3 - a) * win]
                               for a in range(3))
                    scaled = (slope_win[side, p].astype(F32) * grad).astype(BF16).astype(F32)
                    for b, part in enumerate(shifts(scaled)):
                        ss[f % 2, side, b * half:(b + 1) * half, p * win:(p + 1) * win] = part
            g = (jnp.dot(w2_ref[...], ss[f % 2, 0], preferred_element_type=F32)
                 + jnp.dot(w2_other[...], ss[f % 2, 1], preferred_element_type=F32))
            for r in range(rows):
                total = sum(g[a * pad:(a + 1) * pad, (r + 2 - a) * win:(r + 3 - a) * win]
                            for a in range(3))
                value = adj[f, r + 2].astype(F32) + total + send_x[f, r].astype(F32)
                value = value[0:chans]
                put_out(f, r, value)
                if owners > 2:
                    put_send(f, r, value)

        def finish(pair):
            for f in pair:
                @pl.when(not_final)
                def _():
                    halo_down(f).wait_recv()

                @pl.when(not_first)
                def _():
                    halo_up(f).wait_recv()

            for f in pair:
                compute(f)
            if owners > 2:
                @pl.when(tm > 0)
                def _():
                    for f in pair:
                        for k in range(2):
                            x_copy(k, f).start()

        for f in range(fronts):
            inn_copy(f).wait()
            load_raw(f)
            for r in range(rows):
                put_send(f, r, forcing_row(r))

        def begin(f):
            spread_rows(f, range(2, rows + 2))
            first_conv(f, 2, rows + 2)

        w1_copy.wait_recv()
        w2_copy.wait_recv()
        s_copy.wait_recv()

        @pl.when(has_down & (core == 0))
        def _():
            s_up_recv(slope_win, slope_rows, s_send, s_recv, 0, dev(lat, tm, 1 - core))

        @pl.when(has_up & (core == 1))
        def _():
            s_up_recv(slope_win, slope_rows, s_send, s_recv, hid_rows - 1, dev(lat, tm, 1 - core))

        @pl.loop(0, fronts)
        def _(f):
            pass_on(0, f)

        waiting = []
        for f in range(fronts):
            pass_on(1, f)
            if len(waiting) == 1:
                finish(waiting)
                waiting = []
            begin(f)
            waiting.append(f)
        finish(waiting)

        w1_copy.wait_send()
        w2_copy.wait_send()
        s_copy.wait_send()

        @pl.when(has_down)
        def _():
            s_down.wait_send()

        @pl.when(has_up)
        def _():
            s_up.wait_send()

        @pl.loop(0, fronts)
        def _(f):
            @pl.when(not_first)
            def _():
                halo_down(f).wait_send()

            @pl.when(not_final)
            def _():
                halo_up(f).wait_send()

            if owners > 2:
                @pl.when(tm > 0)
                def _():
                    for k in range(2):
                        x_copy(k, f).wait_send()


def s_up_recv(slope_win, slope_rows, s_send, s_recv, row, device):
    for side in range(2):
        pltpu.make_async_remote_copy(
            src_ref=slope_rows.at[0], dst_ref=slope_win.at[side, row],
            send_sem=s_send.at[1], recv_sem=s_recv.at[1 + side],
            device_id=device, device_id_type=MESH).wait_recv()


def in_hbm(array):
    return pltpu.with_memory_space_constraint(array, pltpu.HBM)


def per_device(mesh, innovations, obs_mask, slopes, layer_of, weight_in, weight_out):
    fronts, secs, chans, rows, win = innovations.shape
    _, half, band, _ = slopes.shape
    owners = mesh.shape["tm"]
    lats = mesh.shape["lat"]
    assert secs == 1 and band == 2 * rows and rows == 4 and owners > 1
    pair = owners == 2 and fronts > 1
    pad = round_up(chans, 16)
    rims, hid_rows = rows + 4, rows + 2

    layers = weight_in.shape[0]
    wide = round_up(3 * pad, 128)
    deep = round_up(3 * half, 128)

    smem = pl.BlockSpec(memory_space=pltpu.SMEM)
    hbm = pl.BlockSpec(memory_space=pltpu.HBM)
    vmem = pl.BlockSpec(memory_space=pltpu.VMEM)
    out = pl.pallas_call(
        functools.partial(pair_kernel if pair else chain_kernel, (fronts, chans, rows, win, half, band, lats, owners)),
        out_shape=pltpu.VMEM((fronts * chans * rows, win), F32),
        in_specs=[smem, smem, hbm, hbm, hbm, hbm],
        out_specs=vmem,
        scratch_shapes=[
            pltpu.VMEM((fronts, chans, rows, win), BF16),
            pltpu.VMEM((half * band, win), BF16),
            pltpu.VMEM((layers, 3, 3, half, chans), BF16),
            pltpu.VMEM((layers, 3, 3, half, chans), BF16),
            pltpu.VMEM((3, 3 * half, wide), F32),
            pltpu.VMEM((3, 3 * half, 128), F32),
            pltpu.VMEM((chans * rows, win), F32),
            pltpu.VMEM((fronts, rows, pad, win), BF16),
            pltpu.VMEM((fronts, rims, pad, win), BF16),
            *([pltpu.VMEM((rows, pad, win), BF16)] if pair else []),
            pltpu.VMEM((half * band, win), F32),
            pltpu.VMEM((band, half, win), BF16),
            pltpu.VMEM((2, hid_rows, half, win), BF16),
            *([
                pltpu.VMEM((2, 3 * half, wide), BF16),
                pltpu.VMEM((3 * pad, 2 * deep), BF16),
                pltpu.VMEM((2, 3 * pad, rims * win), BF16),
                pltpu.VMEM((2, 6 * half, rims * win), F32),
                pltpu.VMEM((2, 2 * deep, hid_rows * win), BF16),
            ] if pair else [
                pltpu.VMEM((3 * half, wide), BF16),
                pltpu.VMEM((3 * pad, 3 * half), BF16),
                pltpu.VMEM((3 * half, wide), BF16),
                pltpu.VMEM((3 * pad, 3 * half), BF16),
                pltpu.VMEM((2, 3 * pad, rims * win), BF16),
                pltpu.VMEM((2, 2, 3 * half, rims * win), F32),
                pltpu.VMEM((2, 2, 3 * half, hid_rows * win), BF16),
            ]),
            pltpu.SemaphoreType.DMA((fronts,)),
            pltpu.SemaphoreType.DMA((3,)),
            pltpu.SemaphoreType.DMA((2, fronts)),
            pltpu.SemaphoreType.DMA((2, fronts)),
            *([pltpu.SemaphoreType.DMA((2,))] * 2 if pair else []),
            pltpu.SemaphoreType.DMA((2, fronts)),
            pltpu.SemaphoreType.DMA((2, fronts)),
            pltpu.SemaphoreType.DMA((2,)),
            pltpu.SemaphoreType.DMA((2,)),
            pltpu.SemaphoreType.DMA((5,)),
            pltpu.SemaphoreType.DMA((3,)),
            *([pltpu.SemaphoreType.DMA((2,))] * 2 + [pltpu.SemaphoreType.REGULAR] if pair else []),
        ],
        compiler_params=pltpu.CompilerParams(
            collective_id=0, has_side_effects=True, vmem_limit_bytes=32 * 1024 * 1024
        ),
    )(
        in_hbm(layer_of),
        in_hbm(obs_mask.reshape(obs_mask.shape[-1])),
        in_hbm(innovations.reshape(fronts, chans, rows, win)),
        in_hbm(slopes.reshape(half * band, win)),
        in_hbm(weight_in.swapaxes(3, 4)),
        in_hbm(weight_out),
    )
    return out.reshape(innovations.shape)


def solution(mesh):
    return jax.shard_map(
        functools.partial(per_device, mesh),
        mesh=mesh,
        in_specs=(
            P(None, ("grp", "tm"), None, ("lat", "chan"), None),
            P(("grp", "tm"), ("lat", "chan"), None),
            P(("grp", "tm"), "chan", "lat", None),
            P(),
            P(None, None, None, None, "chan"),
            P(None, None, None, "chan", None),
        ),
        out_specs=P(None, ("grp", "tm"), None, ("lat", "chan"), None),
        check_vma=False,
    )
```
